128 devices in a mesh: wide: 16 (over z, y), head: 8 (over x, core).
Axes of the slice: x: 4, y: 4, z: 4, core: 2. Of those that a mesh axis runs over, the one named last changes fastest.
Arguments:
- queries: bfloat16 [64, 4, 128, 192], P('wide', None, 'head'), may hold values from -120 to 120, as said below
- w_uk: bfloat16 [128, 128, 512], P('head'), may hold values from -0.5 to 0.5
- w_uv: bfloat16 [128, 512, 128], P('head'), may hold values from -4 to 4
- prefix_cache: bfloat16 [32768, 576], P('wide'), may hold values from -5 to 5, as said below
- suffix_cache: bfloat16 [64, 512, 576], P('wide'), may hold values from -6 to 6
- new_latent: bfloat16 [64, 4, 576], P('wide'), may hold values from -6 to 6
- w_out: bfloat16 [16384, 7168], P('head', 'wide'), may hold values from -0.046875 to 0.046875
- request_prefix: int32 [64], P('wide'), may hold values from 0 to 7
- prefix_lengths: int32 [8], replicated, may hold values from 1 to 8192, 32768 in all
- suffix_len: int32 [64], P('wide'), may hold values from 1 to 512, 16384 in all
Outputs:
- layer_out: bfloat16 [64, 4, 7168], P('head', None, 'wide')
The draws below stay inside these ranges and needn't reach their ends.
Inputs may be any that keep to these rules, and one draw needn't show every extreme that they name: `queries`: bounds of the entries. `prefix_cache`: bounds of the entries.
All inputs are finite; a program needn't handle non-finite values. No bound on the sum of `suffix_len` on one device may be relied on, other than what follows from the above.
Results may differ from the reference program's by a relative error of at most 0.019.
Values may be sent and summed in bfloat16 or wider, within the bound.
No kernel may reach another device: no remote copies, remote signals or barrier semaphores. Data moves between devices by JAX's collectives and lax.ppermute only.
A program may use at most 192 MiB of HBM per device.

```python
import math
import jax
import jax.numpy as jnp
import numpy as np
from jax import lax

H = 128
NOPE = 128
ROPE = 64
LAT = 512
D = 7168
DRAFT = 4
P_SIZE = 8
SHARD_TOK = 2048
SUF = 512
REQS = 64
POOL = 32768
N_WIDE = 16


def draw_queries(key, part):
    key = jax.random.fold_in(key, 1)
    first = jax.random.fold_in(key, 0)
    values = jnp.clip(jax.random.normal(first, (REQS, DRAFT, H, NOPE + ROPE), jnp.float32), -5.0, 5.0)
    return values.astype(jnp.bfloat16)


def draw_prefix_cache(key, part):
    key = jax.random.fold_in(key, 2)
    first = jax.random.fold_in(key, 0)
    values = jnp.clip(jax.random.normal(first, (POOL, LAT + ROPE), jnp.float32), -5.0, 5.0)
    return values.astype(jnp.bfloat16)


def with_ends(drawn, stream_key, low, high):
    place = [jax.random.randint(jax.random.fold_in(stream_key, axis), (), 0, length) for axis, length in enumerate(drawn.shape)]
    main_axis = drawn.shape.index(max(drawn.shape))
    next_to = place[:main_axis] + [(place[main_axis] + 1) % drawn.shape[main_axis]] + place[main_axis + 1:]
    return drawn.at[tuple(place)].set(low).at[tuple(next_to)].set(high)


def block_scale(stream_key, shape, cuts, least, largest):
    level, own = 1.0, jax.random.fold_in(stream_key, 6)
    for axis_at, blocks in cuts:
        heights = jnp.exp(jax.random.uniform(jax.random.fold_in(own, axis_at), (blocks,), jnp.float32, least / len(cuts), largest / len(cuts)))
        level = level * jnp.repeat(heights, shape[axis_at] // blocks).reshape([-1 if axis == axis_at else 1 for axis in range(len(shape))])
    return level


def rank_bounds(count, lean):
    loads = [(1 << 20) // math.isqrt(grade ** lean) + 1 for grade in range(1, count + 1)]
    spread = 1 + sum(loads) // (1 << 30)
    return np.cumsum(np.array([max(1, weight // spread) for weight in loads]))


def skewed_ids(stream_key, extent, count, slope):
    table = rank_bounds(count, slope)
    pick = jax.random.randint(jax.random.fold_in(stream_key, 1), extent, 0, int(table[count - 1]))
    standing = jnp.searchsorted(jnp.asarray(table, jnp.int32), pick, side="right")
    return jax.random.permutation(jax.random.fold_in(stream_key, 2), count)[standing].astype(jnp.int32)


def length_profile(amount, total, reach, lean):
    portions = [(1 << 20) // math.isqrt(standing ** lean) + 1 for standing in range(2, amount + 1)]
    spare, counts = total - reach - (amount - 1), [1] * (amount - 1)
    while spare > 0:
        candidates = [i for i in range(amount - 1) if counts[i] < reach]
        pool, remaining = sum([portions[i] for i in candidates]), spare
        for i in candidates:
            more = min(reach - counts[i], max(1, remaining * portions[i] // pool), spare)
            counts[i] = counts[i] + more
            spare = spare - more
    return np.array([reach] + counts)


def uneven(key, count, total, reach, skew):
    if count == 2:
        one = jax.random.randint(key, (), max(1, total - reach), min(reach, total - 1) + 1)
        return jnp.stack([one, total - one])
    sizes = jnp.asarray(length_profile(count, total, reach, skew), jnp.int32)
    twos = (count - 1) // 2
    source_of, taker = sizes[1:1 + 2 * twos:2], sizes[2:2 + 2 * twos:2]
    slack = jnp.minimum(source_of - 1, reach - taker)
    moved = jax.random.randint(jax.random.fold_in(key, 1), (twos,), 0, 1 << 20) % (slack + 1)
    sizes = sizes.at[1:1 + 2 * twos:2].set(source_of - moved).at[2:2 + 2 * twos:2].set(taker + moved)
    return sizes[jax.random.permutation(jax.random.fold_in(key, 2), count)]


def bell_draw(key, extent, scale, most, cuts=(), kind=jnp.bfloat16):
    entries = scale * jax.random.normal(key, extent, jnp.float32)
    if cuts:
        entries = entries * block_scale(key, extent, cuts, -0.22, 0.18)
    return jnp.clip(entries, -most, most).astype(kind)


def setup_inputs(seed: int = 0) -> dict:
    splits = jax.random.split(jax.random.key(seed), 11)
    queries = draw_queries(jax.random.fold_in(splits[10], 71), 0)
    w_uk = bell_draw(splits[1], (H, NOPE, LAT), NOPE ** -0.5, 0.5, ((0, 8),))
    w_uv = bell_draw(splits[2], (H, LAT, NOPE), (max(1, LAT // 256)) ** -0.5, 4.0, ((0, 8),))
    prefix_cache = draw_prefix_cache(jax.random.fold_in(splits[10], 71), 0)
    suffix_cache = bell_draw(splits[4], (REQS, SUF, LAT + ROPE), 1.0, 6.0, ((0, 16),))
    new_latent = bell_draw(splits[5], (REQS, DRAFT, LAT + ROPE), 1.0, 6.0, ((0, 16),))
    w_out = bell_draw(splits[6], (H * NOPE, D), (H * NOPE) ** -0.5, 0.046875, ((0, 8), (1, 16)))
    request_prefix = with_ends(skewed_ids(splits[7], (REQS,), P_SIZE, 2), jax.random.fold_in(splits[7], 3), 0, P_SIZE - 1).astype(jnp.int32)
    prefix_lengths = uneven(splits[8], P_SIZE, POOL, 4 * SHARD_TOK, 2).astype(jnp.int32)
    suffix_len = uneven(splits[9], REQS, REQS * SUF // 2, SUF, 1).astype(jnp.int32)
    return {"queries": queries, "w_uk": w_uk, "w_uv": w_uv, "prefix_cache": prefix_cache, "suffix_cache": suffix_cache, "new_latent": new_latent, "w_out": w_out, "request_prefix": request_prefix, "prefix_lengths": prefix_lengths, "suffix_len": suffix_len}


NEG = -1e30


def block_terms(scores, valid, values, form):
    masked = jnp.where(valid, scores, NEG)
    top = jnp.max(masked, axis=-1)
    weights = jnp.where(valid, jnp.exp(masked - top[..., None]), 0.0)
    total = jnp.sum(weights, axis=-1)
    rounded = weights.astype(jnp.bfloat16).astype(jnp.float32)
    summed = jnp.einsum(form, rounded, values.astype(jnp.float32))
    return top, total, summed


def reference(queries, w_uk, w_uv, prefix_cache, suffix_cache, new_latent, w_out, request_prefix, prefix_lengths, suffix_len):
    scale = 1.0 / ((NOPE + ROPE) ** 0.5)
    q_lat = jnp.einsum('rihn,hnl->rihl', queries[..., :NOPE].astype(jnp.float32), w_uk.astype(jnp.float32)).astype(jnp.bfloat16)
    full_query = jnp.concatenate([q_lat, queries[..., NOPE:]], axis=-1).astype(jnp.float32)
    starts = jnp.cumsum(prefix_lengths) - prefix_lengths
    onehot = request_prefix[:, None] == jnp.arange(P_SIZE, dtype=jnp.int32)[None, :]
    low = jnp.sum(jnp.where(onehot, starts[None, :], 0), axis=1)
    high = low + jnp.sum(jnp.where(onehot, prefix_lengths[None, :], 0), axis=1)
    blocks = prefix_cache.reshape(N_WIDE, SHARD_TOK, LAT + ROPE)

    def one_block(carry, item):
        run_max, run_sum, run_out = carry
        cache, index = item
        position = index * SHARD_TOK + jnp.arange(SHARD_TOK, dtype=jnp.int32)
        valid = (position[None, :] >= low[:, None]) & (position[None, :] < high[:, None])
        scores = jnp.einsum('rihc,tc->riht', full_query, cache.astype(jnp.float32)) * scale
        top, total, summed = block_terms(scores, valid[:, None, None, :], cache[:, :LAT], 'riht,tl->rihl')
        new_max = jnp.maximum(run_max, top)
        old_w = jnp.exp(run_max - new_max)
        new_w = jnp.exp(top - new_max)
        return (new_max, run_sum * old_w + total * new_w, run_out * old_w[..., None] + summed * new_w[..., None]), None

    shape = (REQS, DRAFT, H)
    init = (jnp.full(shape, NEG, jnp.float32), jnp.zeros(shape, jnp.float32), jnp.zeros(shape + (LAT,), jnp.float32))
    (run_max, run_sum, run_out), _ = lax.scan(one_block, init, (blocks, jnp.arange(N_WIDE, dtype=jnp.int32)))

    keys = jnp.concatenate([suffix_cache, new_latent], axis=1)
    slot = jnp.arange(SUF + DRAFT, dtype=jnp.int32)
    draft = jnp.arange(DRAFT, dtype=jnp.int32)
    valid = (slot[None, None, :] < suffix_len[:, None, None]) | ((slot[None, None, :] >= SUF) & (slot[None, None, :] - SUF <= draft[None, :, None]))
    scores = jnp.einsum('rihc,rkc->rihk', full_query, keys.astype(jnp.float32)) * scale
    top, total, summed = block_terms(scores, valid[:, :, None, :], keys[:, :, :LAT], 'rihk,rkl->rihl')
    new_max = jnp.maximum(run_max, top)
    old_w = jnp.exp(run_max - new_max)
    new_w = jnp.exp(top - new_max)
    numer = run_out * old_w[..., None] + summed * new_w[..., None]
    denom = run_sum * old_w + total * new_w
    attn_lat = numer / denom[..., None]
    head_out = jnp.einsum('rihl,hlv->rihv', attn_lat, w_uv.astype(jnp.float32), precision=lax.Precision.HIGHEST).astype(jnp.bfloat16)
    flat = head_out.reshape(REQS * DRAFT, H * NOPE)
    layer_out = jnp.dot(flat, w_out, preferred_element_type=jnp.float32).astype(jnp.bfloat16)
    return layer_out.reshape(REQS, DRAFT, D)
```

```python
import functools
import math
import jax
import jax.numpy as jnp
from jax import lax
from jax.experimental import pallas as pl
from jax.experimental.pallas import tpu as pltpu
from jax.sharding import PartitionSpec as P

NEG = -1e30
BF = jnp.bfloat16
F32 = jnp.float32
NT = (((1,), (1,)), ((), ()))
VLIM = 56 * 1024 * 1024
VM = pl.BlockSpec(memory_space=pltpu.VMEM)
SM = pl.BlockSpec(memory_space=pltpu.SMEM)


def mm(a, b):
    return jnp.dot(a, b, preferred_element_type=F32)


def mm_nt(a, b):
    return lax.dot_general(a, b, NT, preferred_element_type=F32)


def iota(shape, dim):
    return lax.broadcasted_iota(jnp.int32, shape, dim)


def params(limit=VLIM):
    return pltpu.CompilerParams(vmem_limit_bytes=limit)


def pack_kernel(copies, ids_ref, q_ref, out_ref):
    rows = q_ref.shape[0]
    a, b = iota((rows, rows), 0), iota((rows, rows), 1)
    turn = jnp.where((a // 16 == b % 16) & (a % 16 == b // 16), 1.0, 0.0).astype(BF)
    y = mm(turn, q_ref[...]).astype(BF)
    half = rows // 2
    c, d = iota((192, 128), 0), iota((192, 128), 1)
    left = jnp.where((c - 128 == d), 1.0, 0.0).astype(BF)
    right = jnp.where((c - 128 == d - 64) & (c >= 128), 1.0, 0.0).astype(BF)
    rope = (mm(y[:half], left) + mm(y[half:], right)).astype(BF)
    which = iota((16, 128), 0) // 4
    ids = jnp.zeros((16, 128), jnp.int32)
    for r in range(4):
        ids = jnp.where(which == r, ids_ref[r], ids)
    ids = ids.astype(F32).astype(BF)
    nope = y[:, :128]
    for k in range(copies):
        out_ref[k, 0:rows, :] = nope
        out_ref[k, rows : rows + half, :] = rope
        out_ref[k, rows + half : rows + half + 16, :] = ids


def pack(ids, queries, copies):
    return pl.pallas_call(
        functools.partial(pack_kernel, copies),
        out_shape=jax.ShapeDtypeStruct((copies, 400, 128), BF),
        in_specs=[SM, VM],
        out_specs=VM,
        compiler_params=params(),
        name="pack",
    )(ids, queries)


def expand_kernel(scale, cache_ref, uk_ref, uv_ref, k_ref, v_ref, rope_ref):
    lat = cache_ref[:, :512]
    wk = uk_ref[...].reshape(256, 512)
    k_ref[...] = (mm_nt(lat, wk) * scale).astype(BF)
    wv = jnp.concatenate([uv_ref[0], uv_ref[1]], axis=1)
    v_ref[...] = mm(lat, wv).astype(BF)

    @pl.when(pl.program_id(0) == 0)
    def _():
        c, d = iota((64, 256), 0), iota((64, 256), 1)
        place = jnp.where((c == d) | (c == d - 192), 1.0, 0.0).astype(BF)
        rope_ref[...] = (mm(cache_ref[:, 512:576], place) * scale).astype(BF)


def expand(cache, w_uk, w_uv, scale):
    tok = cache.shape[0]
    return pl.pallas_call(
        functools.partial(expand_kernel, scale),
        grid=(8,),
        out_shape=[
            jax.ShapeDtypeStruct((tok, 2048), BF),
            jax.ShapeDtypeStruct((tok, 2048), BF),
            jax.ShapeDtypeStruct((tok, 256), BF),
        ],
        in_specs=[
            pl.BlockSpec((tok, 576), lambda g: (0, 0)),
            pl.BlockSpec((2, 128, 512), lambda g: (g, 0, 0)),
            pl.BlockSpec((2, 512, 128), lambda g: (g, 0, 0)),
        ],
        out_specs=[
            pl.BlockSpec((tok, 256), lambda g: (0, g)),
            pl.BlockSpec((tok, 256), lambda g: (0, g)),
            pl.BlockSpec((tok, 256), lambda g: (0, 0)),
        ],
        compiler_params=params(),
        cost_estimate=pl.CostEstimate(
            flops=2 * 2 * tok * 512 * 2048, bytes_accessed=24 << 20, transcendentals=0
        ),
        name="expand",
    )(cache, w_uk, w_uv)


def own_kernel(scale, len_ref, q_ref, uk_ref, uv_ref, suf_ref, new_ref, o_ref, lse_ref, ql, sc):
    for h in range(16):
        ql[h * 16 : h * 16 + 16, 0:512] = mm(q_ref[0, h * 16 : h * 16 + 16, :], uk_ref[h]).astype(BF)
    c, d = iota((128, 64), 0), iota((128, 64), 1)
    first = jnp.where(c == d, 1.0, 0.0).astype(BF)
    second = jnp.where(c == d + 64, 1.0, 0.0).astype(BF)
    rope = q_ref[0, 256:384, :]
    ql[0:128, 512:576] = mm(rope, first).astype(BF)
    ql[128:256, 512:576] = mm(rope, second).astype(BF)
    q = ql[...]
    req = (iota((256, 1), 0) % 16) // 4
    top = jnp.full((256, 1), NEG, F32)
    for r in range(4):
        s = mm_nt(q, suf_ref[r * 512 : (r + 1) * 512, :]) * scale
        ok = (req == r) & (iota((256, 512), 1) < len_ref[r])
        s = jnp.where(ok, s, NEG)
        sc[:, r * 512 : (r + 1) * 512] = s
        top = jnp.maximum(top, jnp.max(s, axis=1, keepdims=True))
    s = mm_nt(q, new_ref[...]) * scale
    row, col = iota((256, 16), 0) % 16, iota((256, 16), 1)
    ok = (row // 4 == col // 4) & (col % 4 <= row % 4)
    s = jnp.where(ok, s, NEG)
    top = jnp.maximum(top, jnp.max(s, axis=1, keepdims=True))
    p = jnp.exp2(s - top)
    total = jnp.sum(p, axis=1, keepdims=True)
    o = mm(p.astype(BF), new_ref[:, 0:512])
    for r in range(4):
        p = jnp.exp2(sc[:, r * 512 : (r + 1) * 512] - top)
        total = total + jnp.sum(p, axis=1, keepdims=True)
        o = o + mm(p.astype(BF), suf_ref[r * 512 : (r + 1) * 512, 0:512])
    o = (o / total).astype(BF)
    lse = top + jnp.log2(total)
    lane = iota((16, 128), 1)
    packed = jnp.zeros((16, 128), F32)
    for h in range(16):
        o_ref[h * 16 : h * 16 + 16, :] = mm(o[h * 16 : h * 16 + 16], uv_ref[h])
        packed = jnp.where(lane == h, lse[h * 16 : h * 16 + 16], packed)
    lse_ref[...] = packed


def own(suffix_len, packed, w_uk, w_uv, suffix, new, scale):
    return pl.pallas_call(
        functools.partial(own_kernel, scale),
        grid=(1,),
        out_shape=[jax.ShapeDtypeStruct((256, 128), F32), jax.ShapeDtypeStruct((16, 128), F32)],
        in_specs=[SM, pl.BlockSpec((1, 400, 128), lambda g: (0, 0, 0)), VM, VM, VM, VM],
        out_specs=[VM, VM],
        scratch_shapes=[pltpu.VMEM((256, 576), BF), pltpu.VMEM((256, 2048), F32)],
        compiler_params=params(),
        cost_estimate=pl.CostEstimate(flops=3 << 30, bytes_accessed=8 << 20, transcendentals=1 << 19),
        name="own",
    )(suffix_len, packed, w_uk, w_uv, suffix, new)


STEP = 4
CHUNK = 64


def prefix_kernel(
    len_ref, base_ref, q_ref, k_ref, v_ref, rope_ref, out_ref,
    pick, back, okay, qs, bias, osc, lsc, count,
):
    step = pl.program_id(0)
    tok = k_ref.shape[0]

    @pl.when(step == 0)
    def _():
        ids = q_ref[:, 384:400, :].reshape(256, 128).astype(F32)
        base = base_ref[0]

        def bounds(which):
            low = jnp.zeros(which.shape, jnp.int32)
            high = jnp.zeros(which.shape, jnp.int32)
            start = jnp.int32(0) - base
            for p in range(8):
                end = start + len_ref[p]
                hit = which == float(p)
                low = jnp.where(hit, start, low)
                high = jnp.where(hit, end, high)
                start = end
            return jnp.maximum(low, 0), jnp.minimum(high, tok)

        low, high = bounds(ids)
        valid = high > low
        index = iota((256, 128), 0).astype(F32)
        key = jnp.where(valid, ids * 256.0 + index, 8192.0 + index)
        across = jnp.transpose(key)[0:1, :]
        down = key[:, 0:1]
        rank = jnp.sum(jnp.where(across < down, 1.0, 0.0), axis=1, keepdims=True)
        good = valid[:, 0:1]
        okay[...] = jnp.where(valid, 1.0, 0.0)
        lane = iota((256, 256), 1).astype(F32)
        to_row = jnp.where((lane == rank) & (down < 8192.0), 1.0, 0.0)
        back[...] = to_row.astype(BF)
        pickv = jnp.transpose(to_row).astype(BF)
        pick[...] = pickv
        sid = mm(pickv, (ids + 1.0).astype(BF))[:, 0:1] - 1.0
        slow, shigh = bounds(sid)
        pos = iota((256, tok), 1)
        bias[...] = jnp.where((pos >= slow) & (pos < shigh), 0.0, NEG)
        count[0] = jnp.sum(jnp.where(valid, 1.0, 0.0)[:, 0:1]).astype(jnp.int32)
        for h in range(16):
            qs[h, :, 0:128] = mm(pickv, q_ref[:, h * 16 : h * 16 + 16, :].reshape(256, 128)).astype(BF)
        for h in range(8):
            r = mm(pickv, q_ref[:, 256 + h * 16 : 272 + h * 16, :].reshape(256, 128)).astype(BF)
            qs[h, :, 128:256] = r
            qs[h + 8, :, 128:256] = r
        osc[...] = jnp.zeros(osc.shape, BF)
        lsc[...] = jnp.zeros(lsc.shape, F32)

    chunks = (count[0] + (CHUNK - 1)) // CHUNK
    rope = rope_ref[...]

    def work(c, _):
        rows = pl.ds(pl.multiple_of(c * CHUNK, CHUNK), CHUNK)
        lane = iota((CHUNK, 128), 1)
        lse_all = lsc[rows, :]
        for j in range(STEP):
            h = step * STEP + j
            key = jnp.concatenate([k_ref[:, j * 128 : (j + 1) * 128], rope], axis=1)
            s = mm_nt(qs[h, rows, :], key) + bias[rows, :]
            top = jnp.max(s, axis=1, keepdims=True)
            p = jnp.exp2(s - top)
            total = jnp.sum(p, axis=1, keepdims=True)
            o = mm(p.astype(BF), v_ref[:, j * 128 : (j + 1) * 128])
            osc[h, rows, :] = (o / total).astype(BF)
            lse_all = jnp.where(lane == h, top + jnp.log2(total), lse_all)
        lsc[rows, :] = lse_all
        return 0

    lax.fori_loop(0, chunks, work, 0)

    for j in range(STEP):
        h = step * STEP + j
        o = mm(back[...], osc[h]).astype(BF)
        out_ref[:, pl.ds(pl.multiple_of(h * 16, 16), 16), :] = o.reshape(16, 16, 128)

    @pl.when(step == pl.num_programs(0) - 1)
    def _():
        lse = lsc[...]
        hi = lse.astype(BF)
        rest = lse - hi.astype(F32)
        mid = rest.astype(BF)
        lo = (rest - mid.astype(F32)).astype(BF)
        ok = okay[...] > 0.5
        hi = jnp.where(ok, mm(back[...], hi), NEG)
        mid = jnp.where(ok, mm(back[...], mid), 0.0)
        lo = jnp.where(ok, mm(back[...], lo), 0.0)
        lane = iota((256, 128), 1)
        merged = jnp.where(lane < 16, hi, jnp.where(lane < 32, pltpu.roll(mid, 16, 1), pltpu.roll(lo, 32, 1)))
        merged = jnp.where(lane < 48, merged, 0.0)
        out_ref[:, 256:272, :] = merged.astype(BF).reshape(16, 16, 128)


def prefix(lengths, base, got, k, v, rope):
    tok = k.shape[0]
    width = STEP * 128
    steps = 16 // STEP
    half = steps // 2
    return pl.pallas_call(
        prefix_kernel,
        grid=(steps,),
        out_shape=jax.ShapeDtypeStruct((16, 272, 128), BF),
        in_specs=[
            SM,
            SM,
            pl.BlockSpec((16, 400, 128), lambda g: (0, 0, 0)),
            pl.BlockSpec((tok, width), lambda g: (0, g)),
            pl.BlockSpec((tok, width), lambda g: (0, g)),
            pl.BlockSpec((tok, 128), lambda g: (0, g // half)),
        ],
        out_specs=pl.BlockSpec((16, 272, 128), lambda g: (0, 0, 0)),
        scratch_shapes=[
            pltpu.VMEM((256, 256), BF),
            pltpu.VMEM((256, 256), BF),
            pltpu.VMEM((256, 128), F32),
            pltpu.VMEM((16, 256, 256), BF),
            pltpu.VMEM((256, tok), F32),
            pltpu.VMEM((16, 256, 128), BF),
            pltpu.VMEM((256, 128), F32),
            pltpu.SMEM((1,), jnp.int32),
        ],
        compiler_params=params(),
        cost_estimate=pl.CostEstimate(flops=6 << 30, bytes_accessed=20 << 20, transcendentals=4 << 20),
        name="prefix",
    )(lengths, base, got, k, v, rope)


def combine_kernel(got_ref, own_ref, own_lse_ref, out_ref):
    x = got_ref[:, 256:272, :].reshape(256, 128).astype(F32)
    lse = (x + pltpu.roll(x, 112, 1)) + pltpu.roll(x, 96, 1)
    lse = lse.reshape(16, 16, 128)
    mine = own_lse_ref[...]
    lane = iota((16, 128), 1)
    lse = jnp.where((lane < 16)[None], lse, NEG)
    top = jnp.maximum(jnp.max(lse, axis=0), mine)
    w = jnp.exp2(lse - top[None])
    w_own = jnp.exp2(mine - top)
    total = jnp.sum(w, axis=0) + w_own
    w = w / total[None]
    w_own = w_own / total
    for h in range(16):
        rows = slice(h * 16, h * 16 + 16)
        o = jnp.sum(got_ref[:, rows, :].astype(F32) * w[:, :, h : h + 1], axis=0)
        o = (o + own_ref[rows, :] * w_own[:, h : h + 1]).astype(BF)
        for k in range(out_ref.shape[0]):
            out_ref[k, rows, :] = o


def combine(got, own_o, own_lse):
    return pl.pallas_call(
        combine_kernel,
        out_shape=jax.ShapeDtypeStruct((16, 256, 128), BF),
        in_specs=[VM, VM, VM],
        out_specs=VM,
        compiler_params=params(),
        name="combine",
    )(got, own_o, own_lse)


def project_kernel(x_ref, w_ref, out_ref):
    total = None
    for h in range(0, 16, 2):
        a = x_ref[:, h * 16 : h * 16 + 16, :].reshape(256, 128)
        b = x_ref[:, h * 16 + 16 : h * 16 + 32, :].reshape(256, 128)
        part = mm(jnp.concatenate([a, b], axis=1), w_ref[h * 128 : h * 128 + 256, :])
        total = part if total is None else total + part
    out_ref[...] = total.astype(BF).reshape(out_ref.shape)


def project(x, w):
    return pl.pallas_call(
        project_kernel,
        out_shape=jax.ShapeDtypeStruct((8, 32, w.shape[1]), BF),
        in_specs=[VM, VM],
        out_specs=VM,
        compiler_params=params(),
        name="project",
    )(x, w)


def body(
    queries,
    w_uk,
    w_uv,
    prefix_cache,
    suffix_cache,
    new_latent,
    w_out,
    request_prefix,
    prefix_lengths,
    suffix_len,
):
    scale = math.log2(math.e) / queries.shape[-1] ** 0.5
    wide = lax.axis_size("wide")
    tok = prefix_cache.shape[0]
    base = (lax.axis_index("wide") * tok).astype(jnp.int32).reshape(1)
    packed = pack(request_prefix, queries.reshape(256, 192), wide)
    got = lax.all_to_all(packed, "wide", split_axis=0, concat_axis=0, tiled=True)
    k, v, rope = expand(prefix_cache, w_uk, w_uv, scale)
    own_o, own_lse = own(
        suffix_len, packed, w_uk, w_uv, suffix_cache.reshape(2048, 576), new_latent.reshape(16, 576), scale
    )
    part = prefix(prefix_lengths, base, got, k, v, rope)
    part = lax.all_to_all(part, "wide", split_axis=0, concat_axis=0, tiled=True)
    head_out = combine(part, own_o, own_lse)
    head_out = lax.all_to_all(head_out, "wide", split_axis=0, concat_axis=0, tiled=True)
    out = project(head_out, w_out)
    out = lax.all_to_all(out, "head", split_axis=0, concat_axis=0, tiled=True)
    out = jnp.sum(out.astype(F32), axis=0).astype(BF)
    return out.reshape(8, 4, w_out.shape[1])


def solution(mesh):
    in_specs = (
        P("wide", None, "head", None),
        P("head", None, None),
        P("head", None, None),
        P("wide", None),
        P("wide", None, None),
        P("wide", None, None),
        P("head", "wide"),
        P("wide"),
        P(),
        P("wide"),
    )
    out_specs = P("head", None, "wide")
    return jax.shard_map(body, mesh=mesh, in_specs=in_specs, out_specs=out_specs, check_vma=False)
```

```python
import functools
import math
import jax
import jax.numpy as jnp
from jax import lax
from jax.experimental import pallas as pl
from jax.experimental.pallas import tpu as pltpu
from jax.sharding import PartitionSpec as P

NEG = -1e30
BF = jnp.bfloat16
F32 = jnp.float32
NT = (((1,), (1,)), ((), ()))
MIB = 1024 * 1024
VM = pl.BlockSpec(memory_space=pltpu.VMEM)
SM = pl.BlockSpec(memory_space=pltpu.SMEM)
HB = pl.BlockSpec(memory_space=pl.ANY)
TILE = 256
CHUNK = 128


def mm(a, b):
    return jnp.dot(a, b, preferred_element_type=F32)


def mm_nt(a, b):
    return lax.dot_general(a, b, NT, preferred_element_type=F32)


def iota(shape, dim):
    return lax.broadcasted_iota(jnp.int32, shape, dim)


def params(mib):
    return pltpu.CompilerParams(vmem_limit_bytes=mib * MIB)


def pack_kernel(copies, ids_ref, q_ref, out_ref):
    rows = q_ref.shape[0]
    a, b = iota((rows, rows), 0), iota((rows, rows), 1)
    turn = jnp.where((a // 16 == b % 16) & (a % 16 == b // 16), 1.0, 0.0).astype(BF)
    y = mm(turn, q_ref[...]).astype(BF)
    half = rows // 2
    c, d = iota((192, 128), 0), iota((192, 128), 1)
    left = jnp.where((c - 128 == d), 1.0, 0.0).astype(BF)
    right = jnp.where((c - 128 == d - 64) & (c >= 128), 1.0, 0.0).astype(BF)
    rope = (mm(y[:half], left) + mm(y[half:], right)).astype(BF)
    which = iota((16, 128), 0) // 4
    ids = jnp.zeros((16, 128), jnp.int32)
    for r in range(4):
        ids = jnp.where(which == r, ids_ref[r], ids)
    ids = ids.astype(F32).astype(BF)
    nope = y[:, :128]
    for k in range(copies):
        out_ref[k, 0:rows, :] = nope
        out_ref[k, rows : rows + half, :] = rope
        out_ref[k, rows + half : rows + half + 16, :] = ids


def pack(ids, queries, copies):
    return pl.pallas_call(
        functools.partial(pack_kernel, copies),
        out_shape=jax.ShapeDtypeStruct((copies, 400, 128), BF),
        in_specs=[SM, VM],
        out_specs=VM,
        compiler_params=params(8),
        name="pack",
    )(ids, queries)


def expand_kernel(scale, flip_ref, cache_ref, uk_ref, uv_ref, k_ref, v_ref, rope_ref):
    wk = uk_ref[...].reshape(256, 512)
    for t in range(k_ref.shape[0]):
        k_ref[t] = (mm(wk, flip_ref[0:512, t * TILE : (t + 1) * TILE]) * scale).astype(BF)
    wv = jnp.concatenate([uv_ref[0], uv_ref[1]], axis=1)
    v_ref[...] = mm(cache_ref[:, :512], wv).astype(BF)

    @pl.when(pl.program_id(0) == 0)
    def _():
        rope = (flip_ref[512:576, :].astype(F32) * scale).astype(BF)
        rope_ref[...] = jnp.zeros(rope_ref.shape, BF)
        for t in range(k_ref.shape[0]):
            rope_ref[t, 0:64, :] = rope[:, t * TILE : (t + 1) * TILE]
            rope_ref[t, 192:256, :] = rope[:, t * TILE : (t + 1) * TILE]


def expand(cache, w_uk, w_uv, scale):
    tok = cache.shape[0]
    return pl.pallas_call(
        functools.partial(expand_kernel, scale),
        grid=(8,),
        out_shape=[
            jax.ShapeDtypeStruct((tok // TILE, 2048, TILE), BF),
            jax.ShapeDtypeStruct((tok, 2048), BF),
            jax.ShapeDtypeStruct((tok // TILE, 256, TILE), BF),
        ],
        in_specs=[
            pl.BlockSpec((576, tok), lambda g: (0, 0)),
            pl.BlockSpec((tok, 576), lambda g: (0, 0)),
            pl.BlockSpec((2, 128, 512), lambda g: (g, 0, 0)),
            pl.BlockSpec((2, 512, 128), lambda g: (g, 0, 0)),
        ],
        out_specs=[
            pl.BlockSpec((tok // TILE, 256, TILE), lambda g: (0, g, 0)),
            pl.BlockSpec((tok, 256), lambda g: (0, g)),
            pl.BlockSpec((tok // TILE, 256, TILE), lambda g: (0, 0, 0)),
        ],
        compiler_params=params(28),
        cost_estimate=pl.CostEstimate(
            flops=2 * 2 * tok * 512 * 2048, bytes_accessed=24 << 20, transcendentals=0
        ),
        name="expand",
    )(cache.T, cache, w_uk, w_uv)


def own_kernel(scale, len_ref, q_ref, uk_ref, uv_ref, suf_ref, new_ref, o_ref, lse_ref, ql, sc):
    for h in range(16):
        ql[h * 16 : h * 16 + 16, 0:512] = mm(q_ref[0, h * 16 : h * 16 + 16, :], uk_ref[h]).astype(BF)
    c, d = iota((128, 64), 0), iota((128, 64), 1)
    first = jnp.where(c == d, 1.0, 0.0).astype(BF)
    second = jnp.where(c == d + 64, 1.0, 0.0).astype(BF)
    rope = q_ref[0, 256:384, :]
    ql[0:128, 512:576] = mm(rope, first).astype(BF)
    ql[128:256, 512:576] = mm(rope, second).astype(BF)
    q = ql[...]
    req = (iota((256, 1), 0) % 16) // 4
    top = jnp.full((256, 1), NEG, F32)
    for r in range(4):
        s = mm_nt(q, suf_ref[r * 512 : (r + 1) * 512, :]) * scale
        ok = (req == r) & (iota((256, 512), 1) < len_ref[r])
        s = jnp.where(ok, s, NEG)
        sc[:, r * 512 : (r + 1) * 512] = s
        top = jnp.maximum(top, jnp.max(s, axis=1, keepdims=True))
    s = mm_nt(q, new_ref[...]) * scale
    row, col = iota((256, 16), 0) % 16, iota((256, 16), 1)
    ok = (row // 4 == col // 4) & (col % 4 <= row % 4)
    s = jnp.where(ok, s, NEG)
    top = jnp.maximum(top, jnp.max(s, axis=1, keepdims=True))
    p = jnp.exp2(s - top)
    total = jnp.sum(p, axis=1, keepdims=True)
    o = mm(p.astype(BF), new_ref[:, 0:512])
    for r in range(4):
        p = jnp.exp2(sc[:, r * 512 : (r + 1) * 512] - top)
        total = total + jnp.sum(p, axis=1, keepdims=True)
        o = o + mm(p.astype(BF), suf_ref[r * 512 : (r + 1) * 512, 0:512])
    o = (o / total).astype(BF)
    lse = top + jnp.log2(total)
    lane = iota((16, 128), 1)
    packed = jnp.zeros((16, 128), F32)
    for h in range(16):
        o_ref[h * 16 : h * 16 + 16, :] = mm(o[h * 16 : h * 16 + 16], uv_ref[h])
        packed = jnp.where(lane == h, lse[h * 16 : h * 16 + 16], packed)
    lse_ref[...] = packed


def own(suffix_len, packed, w_uk, w_uv, suffix, new, scale):
    return pl.pallas_call(
        functools.partial(own_kernel, scale),
        grid=(1,),
        out_shape=[jax.ShapeDtypeStruct((256, 128), F32), jax.ShapeDtypeStruct((16, 128), F32)],
        in_specs=[SM, pl.BlockSpec((1, 400, 128), lambda g: (0, 0, 0)), VM, VM, VM, VM],
        out_specs=[VM, VM],
        scratch_shapes=[pltpu.VMEM((256, 576), BF), pltpu.VMEM((256, 2048), F32)],
        compiler_params=params(20),
        cost_estimate=pl.CostEstimate(flops=3 << 30, bytes_accessed=8 << 20, transcendentals=1 << 19),
        name="own",
    )(suffix_len, packed, w_uk, w_uv, suffix, new)


def prefix_kernel(
    len_ref, base_ref, q_ref, kbuf, vbuf, rope_ref, out_ref,
    qs, sc, best, total, acc, osc, lsc, slots, low_ref, high_ref, start_ref,
):
    tok = vbuf.shape[0]
    ids = q_ref[:, 384:400, :].reshape(256, 128).astype(F32)
    index = iota((256, 128), 0).astype(F32)
    flat = jnp.transpose(ids)[0:8, :]
    key = index + 8192.0
    shift = jnp.full((256, 128), 0.0, F32)
    begin = jnp.int32(0) - base_ref[0]
    rows_before, units, slot = jnp.int32(0), jnp.int32(0), jnp.int32(0)
    for p in range(8):
        end = begin + len_ref[p]
        low, high = jnp.maximum(begin, 0), jnp.minimum(end, tok)
        begin = end
        rows = jnp.sum(jnp.where(flat[0:1, :] == float(p), 1.0, 0.0)).astype(jnp.int32)
        rows = jnp.where(high > low, rows, 0)
        hit = (ids == float(p)) & (rows > 0)
        key = jnp.where(hit, index + float(p * 256), key)
        shift = jnp.where(hit, (slot - rows_before).astype(F32), shift)
        for c in range(256 // CHUNK):
            @pl.when(rows > c * CHUNK)
            def _():
                low_ref[units + c] = low
                high_ref[units + c] = high
                start_ref[units + c] = slot + c * CHUNK
        units = units + (rows + (CHUNK - 1)) // CHUNK
        slot = slot + (rows + 15) // 16 * 16
        rows_before = rows_before + rows
    blocks = (slot + (CHUNK - 1)) // CHUNK

    across = jnp.transpose(key)[0:1, :]
    rank = jnp.sum(jnp.where(across < key[:, 0:1], 1.0, 0.0), axis=1, keepdims=True)
    mine = jnp.where(key < 8192.0, rank + shift, -1.0)
    slots[...] = mine
    across = jnp.transpose(mine)[0:1, :]
    osc[...] = jnp.zeros(osc.shape, BF)
    lsc[...] = jnp.zeros(lsc.shape, F32)

    def gather(b, _):
        rows = pl.ds(pl.multiple_of(b * CHUNK, CHUNK), CHUNK)
        want = (iota((CHUNK, 256), 0) + b * CHUNK).astype(F32)
        pick = jnp.where(across == want, 1.0, 0.0).astype(BF)
        for h in range(0, 24, 2):
            pair = [q_ref[:, g * 16 : g * 16 + 16, :].reshape(256, 128) for g in (h, h + 1)]
            both = mm(pick, jnp.concatenate(pair, axis=1)).astype(BF)
            for g in (0, 1):
                part = both[:, g * 128 : g * 128 + 128]
                if h < 16:
                    qs[h + g, rows, 0:128] = part
                else:
                    qs[h + g - 16, rows, 128:256] = part
                    qs[h + g - 8, rows, 128:256] = part
        return 0

    lax.fori_loop(0, blocks, gather, 0)
    rest = pl.ds(pl.multiple_of(blocks * CHUNK, CHUNK), CHUNK)
    qs[:, rest, :] = jnp.zeros((16, CHUNK, 256), BF)

    def unit(u, _):
        low, high = low_ref[u], high_ref[u]
        rows = pl.ds(pl.multiple_of(start_ref[u], 16), CHUNK)
        first, last = low // TILE, (high + (TILE - 1)) // TILE
        best[...] = jnp.full(best.shape, NEG, F32)

        def score(t, _):
            pos = iota((1, TILE), 1) + t * TILE
            bias = jnp.where((pos >= low) & (pos < high), 0.0, NEG)
            for h in range(16):
                side = slice(0, 128) if h < 8 else slice(128, 256)
                key = jnp.concatenate([kbuf[t, h * 128 : h * 128 + 128, :], rope_ref[t, side, :]], axis=0)
                s = mm(qs[h, rows, :], key) + bias
                sc[t, h] = s
                top = best[h]
                for v in range(0, TILE, 128):
                    top = jnp.maximum(top, s[:, v : v + 128])
                best[h] = top
            return 0

        lax.fori_loop(first, last, score, 0)

        for h in range(16):
            best[h] = jnp.broadcast_to(jnp.max(best[h], axis=1, keepdims=True), (CHUNK, 128))
        acc[...] = jnp.zeros(acc.shape, F32)
        total[...] = jnp.zeros(total.shape, F32)

        def weigh(t, _):
            here = pl.ds(pl.multiple_of(t * TILE, TILE), TILE)
            for h in range(16):
                top = best[h]
                p = jnp.exp2(sc[t, h] - jnp.concatenate([top] * (TILE // 128), axis=1))
                add = total[h]
                for v in range(0, TILE, 128):
                    add = add + p[:, v : v + 128]
                total[h] = add
                acc[h] += mm(p.astype(BF), vbuf[here, h * 128 : h * 128 + 128])
            return 0

        lax.fori_loop(first, last, weigh, 0)
        lane = iota((CHUNK, 128), 1)
        lse = jnp.zeros((CHUNK, 128), F32)
        for h in range(16):
            full = jnp.sum(total[h], axis=1, keepdims=True)
            osc[h, rows, :] = (acc[h] / full).astype(BF)
            lse = jnp.where(lane == h, best[h] + jnp.log2(full), lse)
        lsc[rows, :] = lse
        return 0

    lax.fori_loop(0, units, unit, 0)

    lane = iota((256, 128), 1)
    ok = slots[...] >= 0.0
    empty = jnp.where((lane < 16) & ~ok, NEG, 0.0).astype(BF)
    out_ref[:, 0:256, :] = jnp.zeros((16, 256, 128), BF)
    out_ref[:, 256:272, :] = empty.reshape(16, 16, 128)

    def scatter(b, _):
        rows = pl.ds(pl.multiple_of(b * CHUNK, CHUNK), CHUNK)
        back = jnp.where(slots[...] == (lane + b * CHUNK).astype(F32), 1.0, 0.0).astype(BF)
        for h in range(0, 16, 2):
            both = mm(back, jnp.concatenate([osc[h, rows, :], osc[h + 1, rows, :]], axis=1))
            for g in (0, 1):
                here = slice((h + g) * 16, (h + g) * 16 + 16)
                part = both[:, g * 128 : g * 128 + 128].reshape(16, 16, 128)
                out_ref[:, here, :] = (out_ref[:, here, :].astype(F32) + part).astype(BF)
        lse = lsc[rows, :]
        hi = lse.astype(BF)
        rest = lse - hi.astype(F32)
        mid = rest.astype(BF)
        lo = (rest - mid.astype(F32)).astype(BF)
        merged = hi.astype(F32) + pltpu.roll(mid.astype(F32), 16, 1) + pltpu.roll(lo.astype(F32), 32, 1)
        part = mm(back, merged.astype(BF)).reshape(16, 16, 128)
        out_ref[:, 256:272, :] = (out_ref[:, 256:272, :].astype(F32) + part).astype(BF)
        return 0

    lax.fori_loop(0, blocks, scatter, 0)


def prefix(lengths, base, got, k, v, rope):
    tiles, tok = k.shape[0], v.shape[0]
    room = 384 + CHUNK
    return pl.pallas_call(
        prefix_kernel,
        out_shape=jax.ShapeDtypeStruct((16, 272, 128), BF),
        in_specs=[SM, SM, VM, VM, VM, VM],
        out_specs=VM,
        scratch_shapes=[
            pltpu.VMEM((16, room, 256), BF),
            pltpu.VMEM((tiles, 16, CHUNK, TILE), F32),
            pltpu.VMEM((16, CHUNK, 128), F32),
            pltpu.VMEM((16, CHUNK, 128), F32),
            pltpu.VMEM((16, CHUNK, 128), F32),
            pltpu.VMEM((16, room, 128), BF),
            pltpu.VMEM((room, 128), F32),
            pltpu.VMEM((256, 128), F32),
            pltpu.SMEM((16,), jnp.int32),
            pltpu.SMEM((16,), jnp.int32),
            pltpu.SMEM((16,), jnp.int32),
        ],
        compiler_params=params(32),
        cost_estimate=pl.CostEstimate(flops=6 << 30, bytes_accessed=20 << 20, transcendentals=4 << 20),
        name="prefix",
    )(lengths, base, got, k, v, rope)


def combine_kernel(got_ref, own_ref, own_lse_ref, out_ref):
    x = got_ref[:, 256:272, :].reshape(256, 128).astype(F32)
    lse = (x + pltpu.roll(x, 112, 1)) + pltpu.roll(x, 96, 1)
    lse = lse.reshape(16, 16, 128)
    mine = own_lse_ref[...]
    lane = iota((16, 128), 1)
    lse = jnp.where((lane < 16)[None], lse, NEG)
    top = jnp.maximum(jnp.max(lse, axis=0), mine)
    w = jnp.exp2(lse - top[None])
    w_own = jnp.exp2(mine - top)
    total = jnp.sum(w, axis=0) + w_own
    w = w / total[None]
    w_own = w_own / total
    for h in range(16):
        rows = slice(h * 16, h * 16 + 16)
        o = jnp.sum(got_ref[:, rows, :].astype(F32) * w[:, :, h : h + 1], axis=0)
        o = (o + own_ref[rows, :] * w_own[:, h : h + 1]).astype(BF)
        for k in range(out_ref.shape[0]):
            out_ref[k, rows, :] = o


def combine(got, own_o, own_lse):
    return pl.pallas_call(
        combine_kernel,
        out_shape=jax.ShapeDtypeStruct((16, 256, 128), BF),
        in_specs=[VM, VM, VM],
        out_specs=VM,
        compiler_params=params(12),
        name="combine",
    )(got, own_o, own_lse)


def project_kernel(x_ref, w_ref, out_ref):
    total = None
    for h in range(0, 16, 2):
        a = x_ref[:, h * 16 : h * 16 + 16, :].reshape(256, 128)
        b = x_ref[:, h * 16 + 16 : h * 16 + 32, :].reshape(256, 128)
        part = mm(jnp.concatenate([a, b], axis=1), w_ref[h * 128 : h * 128 + 256, :])
        total = part if total is None else total + part
    out_ref[...] = total.astype(BF).reshape(out_ref.shape)


def project(x, w):
    return pl.pallas_call(
        project_kernel,
        out_shape=jax.ShapeDtypeStruct((8, 32, w.shape[1]), BF),
        in_specs=[VM, VM],
        out_specs=VM,
        compiler_params=params(12),
        name="project",
    )(x, w)


def body(
    queries,
    w_uk,
    w_uv,
    prefix_cache,
    suffix_cache,
    new_latent,
    w_out,
    request_prefix,
    prefix_lengths,
    suffix_len,
):
    scale = math.log2(math.e) / queries.shape[-1] ** 0.5
    wide = lax.axis_size("wide")
    tok = prefix_cache.shape[0]
    base = (lax.axis_index("wide") * tok).astype(jnp.int32).reshape(1)
    packed = pack(request_prefix, queries.reshape(256, 192), wide)
    got = lax.all_to_all(packed, "wide", split_axis=0, concat_axis=0, tiled=True)
    k, v, rope = expand(prefix_cache, w_uk, w_uv, scale)
    own_o, own_lse = own(
        suffix_len, packed, w_uk, w_uv, suffix_cache.reshape(2048, 576), new_latent.reshape(16, 576), scale
    )
    part = prefix(prefix_lengths, base, got, k, v, rope)
    part = lax.all_to_all(part, "wide", split_axis=0, concat_axis=0, tiled=True)
    head_out = combine(part, own_o, own_lse)
    head_out = lax.all_to_all(head_out, "wide", split_axis=0, concat_axis=0, tiled=True)
    out = project(head_out, w_out)
    out = lax.all_to_all(out, "head", split_axis=0, concat_axis=0, tiled=True)
    out = jnp.sum(out.astype(F32), axis=0).astype(BF)
    return out.reshape(8, 4, w_out.shape[1])


def solution(mesh):
    in_specs = (
        P("wide", None, "head", None),
        P("head", None, None),
        P("head", None, None),
        P("wide", None),
        P("wide", None, None),
        P("wide", None, None),
        P("head", "wide"),
        P("wide"),
        P(),
        P("wide"),
    )
    out_specs = P("head", None, "wide")
    return jax.shard_map(body, mesh=mesh, in_specs=in_specs, out_specs=out_specs, check_vma=False)
```

```python
import functools
import math
import jax
import jax.numpy as jnp
from jax import lax
from jax.experimental import pallas as pl
from jax.experimental.pallas import tpu as pltpu
from jax.sharding import PartitionSpec as P

NEG = -1e30
BF = jnp.bfloat16
F32 = jnp.float32
NT = (((1,), (1,)), ((), ()))
MIB = 1024 * 1024
VM = pl.BlockSpec(memory_space=pltpu.VMEM)
SM = pl.BlockSpec(memory_space=pltpu.SMEM)
HB = pl.BlockSpec(memory_space=pl.ANY)
TILE = 256
CHUNK = 128


def mm(a, b):
    return jnp.dot(a, b, preferred_element_type=F32)


def mm_nt(a, b):
    return lax.dot_general(a, b, NT, preferred_element_type=F32)


def iota(shape, dim):
    return lax.broadcasted_iota(jnp.int32, shape, dim)


def params(mib):
    return pltpu.CompilerParams(vmem_limit_bytes=mib * MIB)


def pack_kernel(copies, ids_ref, q_ref, out_ref):
    rows = q_ref.shape[0]
    a, b = iota((rows, rows), 0), iota((rows, rows), 1)
    turn = jnp.where((a // 16 == b % 16) & (a % 16 == b // 16), 1.0, 0.0).astype(BF)
    y = mm(turn, q_ref[...]).astype(BF)
    half = rows // 2
    c, d = iota((192, 128), 0), iota((192, 128), 1)
    left = jnp.where((c - 128 == d), 1.0, 0.0).astype(BF)
    right = jnp.where((c - 128 == d - 64) & (c >= 128), 1.0, 0.0).astype(BF)
    rope = (mm(y[:half], left) + mm(y[half:], right)).astype(BF)
    which = iota((16, 128), 0) // 4
    ids = jnp.zeros((16, 128), jnp.int32)
    for r in range(4):
        ids = jnp.where(which == r, ids_ref[r], ids)
    ids = ids.astype(F32).astype(BF)
    nope = y[:, :128]
    for k in range(copies):
        out_ref[k, 0:rows, :] = nope
        out_ref[k, rows : rows + half, :] = rope
        out_ref[k, rows + half : rows + half + 16, :] = ids


def pack(ids, queries, copies):
    return pl.pallas_call(
        functools.partial(pack_kernel, copies),
        out_shape=jax.ShapeDtypeStruct((copies, 400, 128), BF),
        in_specs=[SM, VM],
        out_specs=VM,
        compiler_params=params(56),
        name="pack",
    )(ids, queries)


def expand_kernel(scale, flip_ref, uk_ref, uv_ref, k_ref, v_ref, rope_ref, lat_ref):
    @pl.when(pl.program_id(0) == 0)
    def _():
        rope = (flip_ref[512:576, :].astype(F32) * scale).astype(BF)
        rope_ref[...] = jnp.zeros(rope_ref.shape, BF)
        for t in range(k_ref.shape[0]):
            here = slice(t * TILE, (t + 1) * TILE)
            rope_ref[t, 0:64, :] = rope[:, here]
            rope_ref[t, 192:256, :] = rope[:, here]
            lat_ref[here, :] = jnp.transpose(flip_ref[0:512, here])

    wk = uk_ref[...].reshape(256, 512)
    for t in range(k_ref.shape[0]):
        k_ref[t] = (mm(wk, flip_ref[0:512, t * TILE : (t + 1) * TILE]) * scale).astype(BF)
    wv = jnp.concatenate([uv_ref[0], uv_ref[1]], axis=1)
    v_ref[...] = mm(lat_ref[...], wv).astype(BF)


def expand(cache, w_uk, w_uv, scale):
    tok = cache.shape[0]
    return pl.pallas_call(
        functools.partial(expand_kernel, scale),
        grid=(8,),
        out_shape=[
            jax.ShapeDtypeStruct((tok // TILE, 2048, TILE), BF),
            jax.ShapeDtypeStruct((tok, 2048), BF),
            jax.ShapeDtypeStruct((tok // TILE, 256, TILE), BF),
        ],
        in_specs=[
            pl.BlockSpec((576, tok), lambda g: (0, 0)),
            pl.BlockSpec((2, 128, 512), lambda g: (g, 0, 0)),
            pl.BlockSpec((2, 512, 128), lambda g: (g, 0, 0)),
        ],
        out_specs=[
            pl.BlockSpec((tok // TILE, 256, TILE), lambda g: (0, g, 0)),
            pl.BlockSpec((tok, 256), lambda g: (0, g)),
            pl.BlockSpec((tok // TILE, 256, TILE), lambda g: (0, 0, 0)),
        ],
        scratch_shapes=[pltpu.VMEM((tok, 512), BF)],
        compiler_params=params(56),
        cost_estimate=pl.CostEstimate(
            flops=2 * 2 * tok * 512 * 2048, bytes_accessed=24 << 20, transcendentals=0
        ),
        name="expand",
    )(cache.T, w_uk, w_uv)


def own_kernel(scale, len_ref, q_ref, uk_ref, uv_ref, suf_ref, new_ref, o_ref, lse_ref, ql, sc):
    for h in range(16):
        ql[h * 16 : h * 16 + 16, 0:512] = mm(q_ref[0, h * 16 : h * 16 + 16, :], uk_ref[h]).astype(BF)
    c, d = iota((128, 64), 0), iota((128, 64), 1)
    first = jnp.where(c == d, 1.0, 0.0).astype(BF)
    second = jnp.where(c == d + 64, 1.0, 0.0).astype(BF)
    rope = q_ref[0, 256:384, :]
    ql[0:128, 512:576] = mm(rope, first).astype(BF)
    ql[128:256, 512:576] = mm(rope, second).astype(BF)
    q = ql[...]
    req = (iota((256, 1), 0) % 16) // 4
    top = jnp.full((256, 1), NEG, F32)
    for r in range(4):
        s = mm(q, suf_ref[r]) * scale
        ok = (req == r) & (iota((256, 512), 1) < len_ref[r])
        s = jnp.where(ok, s, NEG)
        sc[:, r * 512 : (r + 1) * 512] = s
        top = jnp.maximum(top, jnp.max(s, axis=1, keepdims=True))
    s = mm_nt(q, new_ref[...]) * scale
    row, col = iota((256, 16), 0) % 16, iota((256, 16), 1)
    ok = (row // 4 == col // 4) & (col % 4 <= row % 4)
    s = jnp.where(ok, s, NEG)
    top = jnp.maximum(top, jnp.max(s, axis=1, keepdims=True))
    p = jnp.exp2(s - top)
    total = jnp.sum(p, axis=1, keepdims=True)
    o = mm(p.astype(BF), new_ref[:, 0:512])
    for r in range(4):
        p = jnp.exp2(sc[:, r * 512 : (r + 1) * 512] - top)
        total = total + jnp.sum(p, axis=1, keepdims=True)
        o = o + mm_nt(p.astype(BF), suf_ref[r, 0:512, :])
    o = (o / total).astype(BF)
    lse = top + jnp.log2(total)
    lane = iota((16, 128), 1)
    packed = jnp.zeros((16, 128), F32)
    for h in range(16):
        o_ref[h * 16 : h * 16 + 16, :] = mm(o[h * 16 : h * 16 + 16], uv_ref[h])
        packed = jnp.where(lane == h, lse[h * 16 : h * 16 + 16], packed)
    lse_ref[...] = packed


def own(suffix_len, packed, w_uk, w_uv, suffix, new, scale):
    return pl.pallas_call(
        functools.partial(own_kernel, scale),
        grid=(1,),
        out_shape=[jax.ShapeDtypeStruct((256, 128), F32), jax.ShapeDtypeStruct((16, 128), F32)],
        in_specs=[SM, pl.BlockSpec((1, 400, 128), lambda g: (0, 0, 0)), VM, VM, VM, VM],
        out_specs=[VM, VM],
        scratch_shapes=[pltpu.VMEM((256, 576), BF), pltpu.VMEM((256, 2048), F32)],
        compiler_params=params(56),
        cost_estimate=pl.CostEstimate(flops=3 << 30, bytes_accessed=8 << 20, transcendentals=1 << 19),
        name="own",
    )(suffix_len, packed, w_uk, w_uv, suffix, new)


def prefix_kernel(
    len_ref, base_ref, q_hbm, k_hbm, v_hbm, rope_hbm, out_ref,
    id_ref, q_ref, rope_ref, kbuf, vbuf, qs, sc, best, total, acc, osc, lsc, slots,
    low_ref, high_ref, start_ref, seen, sems, ksems, vsems,
):
    tok, tiles = vbuf.shape[0], kbuf.shape[0]
    loads = [
        pltpu.make_async_copy(q_hbm.at[:, 384:400, :], id_ref, sems.at[0]),
        pltpu.make_async_copy(q_hbm.at[:, 0:384, :], q_ref, sems.at[1]),
        pltpu.make_async_copy(rope_hbm, rope_ref, sems.at[2]),
    ]
    for load in loads:
        load.start()

    def load_k(t):
        return pltpu.make_async_copy(k_hbm.at[t], kbuf.at[t], ksems.at[t])

    def load_v(t):
        here = pl.ds(t * TILE, TILE)
        return pltpu.make_async_copy(v_hbm.at[here, :], vbuf.at[here, :], vsems.at[t])

    for t in range(tiles):
        load_k(t).start()
    seen[0] = 0
    seen[1] = 0

    def arrive(t, which, load):
        def one(i, _):
            load(i).wait()
            return 0

        lax.fori_loop(seen[which], t + 1, one, 0)
        seen[which] = jnp.maximum(seen[which], t + 1)

    loads[0].wait()
    ids = id_ref[...].reshape(256, 128).astype(F32)
    index = iota((256, 128), 0).astype(F32)
    flat = jnp.transpose(ids)[0:8, :]
    key = index + 8192.0
    shift = jnp.full((256, 128), 0.0, F32)
    begin = jnp.int32(0) - base_ref[0]
    rows_before, units, slot = jnp.int32(0), jnp.int32(0), jnp.int32(0)
    for p in range(8):
        end = begin + len_ref[p]
        low, high = jnp.maximum(begin, 0), jnp.minimum(end, tok)
        begin = end
        rows = jnp.sum(jnp.where(flat[0:1, :] == float(p), 1.0, 0.0)).astype(jnp.int32)
        rows = jnp.where(high > low, rows, 0)
        hit = (ids == float(p)) & (rows > 0)
        key = jnp.where(hit, index + float(p * 256), key)
        shift = jnp.where(hit, (slot - rows_before).astype(F32), shift)
        for c in range(256 // CHUNK):
            @pl.when(rows > c * CHUNK)
            def _():
                low_ref[units + c] = low
                high_ref[units + c] = high
                start_ref[units + c] = slot + c * CHUNK
        units = units + (rows + (CHUNK - 1)) // CHUNK
        slot = slot + (rows + 15) // 16 * 16
        rows_before = rows_before + rows
    blocks = (slot + (CHUNK - 1)) // CHUNK

    across = jnp.transpose(key)[0:1, :]
    rank = jnp.sum(jnp.where(across < key[:, 0:1], 1.0, 0.0), axis=1, keepdims=True)
    mine = jnp.where(key < 8192.0, rank + shift, -1.0)
    slots[...] = mine
    across = jnp.transpose(mine)[0:1, :]
    osc[...] = jnp.zeros(osc.shape, BF)
    lsc[...] = jnp.zeros(lsc.shape, F32)

    loads[1].wait()

    def gather(b, _):
        rows = pl.ds(pl.multiple_of(b * CHUNK, CHUNK), CHUNK)
        want = (iota((CHUNK, 256), 0) + b * CHUNK).astype(F32)
        pick = jnp.where(across == want, 1.0, 0.0).astype(BF)
        for h in range(0, 24, 2):
            pair = [q_ref[:, g * 16 : g * 16 + 16, :].reshape(256, 128) for g in (h, h + 1)]
            both = mm(pick, jnp.concatenate(pair, axis=1)).astype(BF)
            for g in (0, 1):
                part = both[:, g * 128 : g * 128 + 128]
                if h < 16:
                    qs[h + g, rows, 0:128] = part
                else:
                    qs[h + g - 16, rows, 128:256] = part
                    qs[h + g - 8, rows, 128:256] = part
        return 0

    lax.fori_loop(0, blocks, gather, 0)
    rest = pl.ds(pl.multiple_of(blocks * CHUNK, CHUNK), CHUNK)
    qs[:, rest, :] = jnp.zeros((16, CHUNK, 256), BF)
    loads[2].wait()

    def unit(u, _):
        low, high = low_ref[u], high_ref[u]
        rows = pl.ds(pl.multiple_of(start_ref[u], 16), CHUNK)
        first, last = low // TILE, (high + (TILE - 1)) // TILE
        best[...] = jnp.full(best.shape, NEG, F32)

        def score(t, _):
            arrive(t, 0, load_k)
            pos = iota((1, TILE), 1) + t * TILE
            bias = jnp.where((pos >= low) & (pos < high), 0.0, NEG)
            for h in range(16):
                side = slice(0, 128) if h < 8 else slice(128, 256)
                key = jnp.concatenate([kbuf[t, h * 128 : h * 128 + 128, :], rope_ref[t, side, :]], axis=0)
                s = mm(qs[h, rows, :], key) + bias
                sc[t, h] = s
                top = best[h]
                for v in range(0, TILE, 128):
                    top = jnp.maximum(top, s[:, v : v + 128])
                best[h] = top
            return 0

        lax.fori_loop(first, last, score, 0)

        for h in range(16):
            best[h] = jnp.broadcast_to(jnp.max(best[h], axis=1, keepdims=True), (CHUNK, 128))
        acc[...] = jnp.zeros(acc.shape, F32)
        total[...] = jnp.zeros(total.shape, F32)

        def weigh(t, _):
            arrive(t, 1, load_v)
            here = pl.ds(pl.multiple_of(t * TILE, TILE), TILE)
            for h in range(16):
                top = best[h]
                p = jnp.exp2(sc[t, h] - jnp.concatenate([top] * (TILE // 128), axis=1))
                add = total[h]
                for v in range(0, TILE, 128):
                    add = add + p[:, v : v + 128]
                total[h] = add
                acc[h] += mm(p.astype(BF), vbuf[here, h * 128 : h * 128 + 128])
            return 0

        lax.fori_loop(first, last, weigh, 0)
        lane = iota((CHUNK, 128), 1)
        lse = jnp.zeros((CHUNK, 128), F32)
        for h in range(16):
            full = jnp.sum(total[h], axis=1, keepdims=True)
            osc[h, rows, :] = (acc[h] / full).astype(BF)
            lse = jnp.where(lane == h, best[h] + jnp.log2(full), lse)
        lsc[rows, :] = lse
        return 0

    for t in range(tiles):
        load_v(t).start()
    lax.fori_loop(0, units, unit, 0)
    arrive(tiles - 1, 0, load_k)
    arrive(tiles - 1, 1, load_v)

    lane = iota((256, 128), 1)
    ok = slots[...] >= 0.0
    empty = jnp.where((lane < 16) & ~ok, NEG, 0.0).astype(BF)
    out_ref[:, 0:256, :] = jnp.zeros((16, 256, 128), BF)
    out_ref[:, 256:272, :] = empty.reshape(16, 16, 128)

    def scatter(b, _):
        rows = pl.ds(pl.multiple_of(b * CHUNK, CHUNK), CHUNK)
        back = jnp.where(slots[...] == (lane + b * CHUNK).astype(F32), 1.0, 0.0).astype(BF)
        for h in range(0, 16, 2):
            both = mm(back, jnp.concatenate([osc[h, rows, :], osc[h + 1, rows, :]], axis=1))
            for g in (0, 1):
                here = slice((h + g) * 16, (h + g) * 16 + 16)
                part = both[:, g * 128 : g * 128 + 128].reshape(16, 16, 128)
                out_ref[:, here, :] = (out_ref[:, here, :].astype(F32) + part).astype(BF)
        lse = lsc[rows, :]
        hi = lse.astype(BF)
        rest = lse - hi.astype(F32)
        mid = rest.astype(BF)
        lo = (rest - mid.astype(F32)).astype(BF)
        merged = hi.astype(F32) + pltpu.roll(mid.astype(F32), 16, 1) + pltpu.roll(lo.astype(F32), 32, 1)
        part = mm(back, merged.astype(BF)).reshape(16, 16, 128)
        out_ref[:, 256:272, :] = (out_ref[:, 256:272, :].astype(F32) + part).astype(BF)
        return 0

    lax.fori_loop(0, blocks, scatter, 0)


def prefix(lengths, base, got, k, v, rope):
    tiles, tok = k.shape[0], v.shape[0]
    room = 384 + CHUNK
    return pl.pallas_call(
        prefix_kernel,
        out_shape=jax.ShapeDtypeStruct((16, 272, 128), BF),
        in_specs=[SM, SM, HB, HB, HB, HB],
        out_specs=VM,
        scratch_shapes=[
            pltpu.VMEM((16, 16, 128), BF),
            pltpu.VMEM((16, 384, 128), BF),
            pltpu.VMEM(rope.shape, BF),
            pltpu.VMEM(k.shape, BF),
            pltpu.VMEM(v.shape, BF),
            pltpu.VMEM((16, room, 256), BF),
            pltpu.VMEM((tiles, 16, CHUNK, TILE), F32),
            pltpu.VMEM((16, CHUNK, 128), F32),
            pltpu.VMEM((16, CHUNK, 128), F32),
            pltpu.VMEM((16, CHUNK, 128), F32),
            pltpu.VMEM((16, room, 128), BF),
            pltpu.VMEM((room, 128), F32),
            pltpu.VMEM((256, 128), F32),
            pltpu.SMEM((16,), jnp.int32),
            pltpu.SMEM((16,), jnp.int32),
            pltpu.SMEM((16,), jnp.int32),
            pltpu.SMEM((2,), jnp.int32),
            pltpu.SemaphoreType.DMA((3,)),
            pltpu.SemaphoreType.DMA((tiles,)),
            pltpu.SemaphoreType.DMA((tiles,)),
        ],
        compiler_params=params(56),
        cost_estimate=pl.CostEstimate(flops=6 << 30, bytes_accessed=20 << 20, transcendentals=4 << 20),
        name="prefix",
    )(lengths, base, got, k, v, rope)


def combine_kernel(got_ref, own_ref, own_lse_ref, out_ref):
    x = got_ref[:, 256:272, :].reshape(256, 128).astype(F32)
    lse = (x + pltpu.roll(x, 112, 1)) + pltpu.roll(x, 96, 1)
    lse = lse.reshape(16, 16, 128)
    mine = own_lse_ref[...]
    lane = iota((16, 128), 1)
    lse = jnp.where((lane < 16)[None], lse, NEG)
    top = jnp.maximum(jnp.max(lse, axis=0), mine)
    w = jnp.exp2(lse - top[None])
    w_own = jnp.exp2(mine - top)
    total = jnp.sum(w, axis=0) + w_own
    w = w / total[None]
    w_own = w_own / total
    for h in range(16):
        rows = slice(h * 16, h * 16 + 16)
        o = jnp.sum(got_ref[:, rows, :].astype(F32) * w[:, :, h : h + 1], axis=0)
        o = (o + own_ref[rows, :] * w_own[:, h : h + 1]).astype(BF)
        for k in range(out_ref.shape[0]):
            out_ref[k, rows, :] = o


def combine(got, own_o, own_lse):
    return pl.pallas_call(
        combine_kernel,
        out_shape=jax.ShapeDtypeStruct((16, 256, 128), BF),
        in_specs=[VM, VM, VM],
        out_specs=VM,
        compiler_params=params(12),
        name="combine",
    )(got, own_o, own_lse)


def project_kernel(x_ref, w_ref, out_ref):
    total = None
    for h in range(0, 16, 2):
        a = x_ref[:, h * 16 : h * 16 + 16, :].reshape(256, 128)
        b = x_ref[:, h * 16 + 16 : h * 16 + 32, :].reshape(256, 128)
        part = mm(jnp.concatenate([a, b], axis=1), w_ref[h * 128 : h * 128 + 256, :])
        total = part if total is None else total + part
    out_ref[...] = total.astype(BF).reshape(out_ref.shape)


def project(x, w):
    return pl.pallas_call(
        project_kernel,
        out_shape=jax.ShapeDtypeStruct((8, 32, w.shape[1]), BF),
        in_specs=[VM, VM],
        out_specs=VM,
        compiler_params=params(12),
        name="project",
    )(x, w)


def body(
    queries,
    w_uk,
    w_uv,
    prefix_cache,
    suffix_cache,
    new_latent,
    w_out,
    request_prefix,
    prefix_lengths,
    suffix_len,
):
    scale = math.log2(math.e) / queries.shape[-1] ** 0.5
    wide = lax.axis_size("wide")
    tok = prefix_cache.shape[0]
    base = (lax.axis_index("wide") * tok).astype(jnp.int32).reshape(1)
    packed = pack(request_prefix, queries.reshape(256, 192), wide)
    got = lax.all_to_all(packed, "wide", split_axis=0, concat_axis=0, tiled=True)
    k, v, rope = expand(prefix_cache, w_uk, w_uv, scale)
    own_o, own_lse = own(
        suffix_len, packed, w_uk, w_uv, jnp.swapaxes(suffix_cache, 1, 2), new_latent.reshape(16, 576), scale
    )
    part = prefix(prefix_lengths, base, got, k, v, rope)
    part = lax.all_to_all(part, "wide", split_axis=0, concat_axis=0, tiled=True)
    head_out = combine(part, own_o, own_lse)
    head_out = lax.all_to_all(head_out, "wide", split_axis=0, concat_axis=0, tiled=True)
    out = project(head_out, w_out)
    out = lax.all_to_all(out, "head", split_axis=0, concat_axis=0, tiled=True)
    out = jnp.sum(out.astype(F32), axis=0).astype(BF)
    return out.reshape(8, 4, w_out.shape[1])


def solution(mesh):
    in_specs = (
        P("wide", None, "head", None),
        P("head", None, None),
        P("head", None, None),
        P("wide", None),
        P("wide", None, None),
        P("wide", None, None),
        P("head", "wide"),
        P("wide"),
        P(),
        P("wide"),
    )
    out_specs = P("head", None, "wide")
    return jax.shard_map(body, mesh=mesh, in_specs=in_specs, out_specs=out_specs, check_vma=False)
```

```python
import functools
import math
import jax
import jax.numpy as jnp
from jax import lax
from jax.experimental import pallas as pl
from jax.experimental.pallas import tpu as pltpu
from jax.sharding import PartitionSpec as P

NEG = -1e30
BF = jnp.bfloat16
F32 = jnp.float32
NT = (((1,), (1,)), ((), ()))
MIB = 1024 * 1024
VM = pl.BlockSpec(memory_space=pltpu.VMEM)
SM = pl.BlockSpec(memory_space=pltpu.SMEM)
HB = pl.BlockSpec(memory_space=pltpu.HBM)
TILE = 256
CHUNK = 128


def mm(a, b):
    return jnp.dot(a, b, preferred_element_type=F32)


def mm_nt(a, b):
    return lax.dot_general(a, b, NT, preferred_element_type=F32)


def iota(shape, dim):
    return lax.broadcasted_iota(jnp.int32, shape, dim)


def params(mib):
    return pltpu.CompilerParams(vmem_limit_bytes=mib * MIB)


def pack_kernel(copies, ids_ref, q_ref, out_ref):
    rows = q_ref.shape[0]
    a, b = iota((rows, rows), 0), iota((rows, rows), 1)
    turn = jnp.where((a // 16 == b % 16) & (a % 16 == b // 16), 1.0, 0.0).astype(BF)
    y = mm(turn, q_ref[...]).astype(BF)
    half = rows // 2
    c, d = iota((192, 128), 0), iota((192, 128), 1)
    left = jnp.where((c - 128 == d), 1.0, 0.0).astype(BF)
    right = jnp.where((c - 128 == d - 64) & (c >= 128), 1.0, 0.0).astype(BF)
    rope = (mm(y[:half], left) + mm(y[half:], right)).astype(BF)
    which = iota((16, 128), 0) // 4
    ids = jnp.zeros((16, 128), jnp.int32)
    for r in range(4):
        ids = jnp.where(which == r, ids_ref[r], ids)
    ids = ids.astype(F32).astype(BF)
    nope = y[:, :128]
    for k in range(copies):
        out_ref[k, 0:rows, :] = nope
        out_ref[k, rows : rows + half, :] = rope
        out_ref[k, rows + half : rows + half + 16, :] = ids


def pack(ids, queries, copies):
    return pl.pallas_call(
        functools.partial(pack_kernel, copies),
        out_shape=jax.ShapeDtypeStruct((copies, 400, 128), BF),
        in_specs=[SM, VM],
        out_specs=VM,
        compiler_params=params(56),
        name="pack",
    )(ids, queries)


def expand_kernel(scale, flip_ref, uk_ref, uv_ref, k_ref, v_ref, lat_ref):
    step = pl.program_id(0)

    @pl.when(step == 0)
    def _():
        rope = (flip_ref[512:576, :].astype(F32) * scale).astype(BF)
        k_ref[...] = jnp.zeros(k_ref.shape, BF)
        for t in range(k_ref.shape[0]):
            here = slice(t * TILE, (t + 1) * TILE)
            k_ref[t, 0:64, :] = rope[:, here]
            k_ref[t, 192:256, :] = rope[:, here]
            lat_ref[here, :] = jnp.transpose(flip_ref[0:512, here])

    @pl.when(step > 0)
    def _():
        wk = uk_ref[...].reshape(256, 512)
        for t in range(k_ref.shape[0]):
            k_ref[t] = (mm(wk, flip_ref[0:512, t * TILE : (t + 1) * TILE]) * scale).astype(BF)
        wv = jnp.concatenate([uv_ref[0], uv_ref[1]], axis=1)
        v_ref[...] = mm(lat_ref[...], wv).astype(BF)


def expand(cache, w_uk, w_uv, scale):
    tok = cache.shape[0]
    return pl.pallas_call(
        functools.partial(expand_kernel, scale),
        grid=(9,),
        out_shape=[
            jax.ShapeDtypeStruct((tok // TILE, 2304, TILE), BF),
            jax.ShapeDtypeStruct((tok, 2048), BF),
        ],
        in_specs=[
            pl.BlockSpec((576, tok), lambda g: (0, 0)),
            pl.BlockSpec((2, 128, 512), lambda g: (jnp.maximum(g - 1, 0), 0, 0)),
            pl.BlockSpec((2, 512, 128), lambda g: (jnp.maximum(g - 1, 0), 0, 0)),
        ],
        out_specs=[
            pl.BlockSpec((tok // TILE, 256, TILE), lambda g: (0, g, 0)),
            pl.BlockSpec((tok, 256), lambda g: (0, jnp.maximum(g - 1, 0))),
        ],
        scratch_shapes=[pltpu.VMEM((tok, 512), BF)],
        compiler_params=params(56),
        cost_estimate=pl.CostEstimate(
            flops=2 * 2 * tok * 512 * 2048, bytes_accessed=24 << 20, transcendentals=0
        ),
        name="expand",
    )(cache.T, w_uk, w_uv)


def own_kernel(
    scale, len_ref, q_ref, draft_ref, uk_hbm, uv_hbm, suf_hbm, o_ref, lse_ref,
    uk_ref, uv_ref, suf_ref, new_ref, ql, sc, sems,
):
    loads = [
        pltpu.make_async_copy(uk_hbm, uk_ref, sems.at[0]),
        pltpu.make_async_copy(suf_hbm, suf_ref, sems.at[1]),
        pltpu.make_async_copy(uv_hbm, uv_ref, sems.at[2]),
    ]
    for load in loads:
        load.start()
    loads[0].wait()
    for h in range(16):
        ql[h * 16 : h * 16 + 16, 0:512] = mm(q_ref[0, h * 16 : h * 16 + 16, :], uk_ref[h]).astype(BF)
    c, d = iota((128, 64), 0), iota((128, 64), 1)
    first = jnp.where(c == d, 1.0, 0.0).astype(BF)
    second = jnp.where(c == d + 64, 1.0, 0.0).astype(BF)
    rope = q_ref[0, 256:384, :]
    ql[0:128, 512:576] = mm(rope, first).astype(BF)
    ql[128:256, 512:576] = mm(rope, second).astype(BF)
    q = ql[...]
    req = (iota((256, 1), 0) % 16) // 4
    top = jnp.full((256, 1), NEG, F32)
    loads[1].wait()
    for r in range(4):
        s = mm(q, suf_ref[r]) * scale
        ok = (req == r) & (iota((256, 512), 1) < len_ref[r])
        s = jnp.where(ok, s, NEG)
        sc[:, r * 512 : (r + 1) * 512] = s
        top = jnp.maximum(top, jnp.max(s, axis=1, keepdims=True))
    for r in range(4):
        new_ref[r * 4 : r * 4 + 4, :] = draft_ref[r].astype(F32)
    new = new_ref[...].astype(BF)
    s = mm_nt(q, new) * scale
    row, col = iota((256, 16), 0) % 16, iota((256, 16), 1)
    ok = (row // 4 == col // 4) & (col % 4 <= row % 4)
    s = jnp.where(ok, s, NEG)
    top = jnp.maximum(top, jnp.max(s, axis=1, keepdims=True))
    p = jnp.exp2(s - top)
    total = jnp.sum(p, axis=1, keepdims=True)
    o = mm(p.astype(BF), new[:, 0:512])
    for r in range(4):
        p = jnp.exp2(sc[:, r * 512 : (r + 1) * 512] - top)
        total = total + jnp.sum(p, axis=1, keepdims=True)
        o = o + mm_nt(p.astype(BF), suf_ref[r, 0:512, :])
    o = (o / total).astype(BF)
    lse = top + jnp.log2(total)
    loads[2].wait()
    lane = iota((16, 128), 1)
    packed = jnp.zeros((16, 128), F32)
    for h in range(16):
        o_ref[h * 16 : h * 16 + 16, :] = mm(o[h * 16 : h * 16 + 16], uv_ref[h])
        packed = jnp.where(lane == h, lse[h * 16 : h * 16 + 16], packed)
    lse_ref[...] = packed


def own(suffix_len, packed, w_uk, w_uv, suffix, new, scale):
    return pl.pallas_call(
        functools.partial(own_kernel, scale),
        grid=(1,),
        out_shape=[jax.ShapeDtypeStruct((256, 128), F32), jax.ShapeDtypeStruct((16, 128), F32)],
        in_specs=[SM, pl.BlockSpec((1, 400, 128), lambda g: (0, 0, 0)), VM, HB, HB, HB],
        out_specs=[VM, VM],
        scratch_shapes=[
            pltpu.VMEM(w_uk.shape, BF),
            pltpu.VMEM(w_uv.shape, BF),
            pltpu.VMEM(suffix.shape, BF),
            pltpu.VMEM((16, 576), F32),
            pltpu.VMEM((256, 576), BF),
            pltpu.VMEM((256, 2048), F32),
            pltpu.SemaphoreType.DMA((3,)),
        ],
        compiler_params=params(56),
        cost_estimate=pl.CostEstimate(flops=3 << 30, bytes_accessed=8 << 20, transcendentals=1 << 19),
        name="own",
    )(suffix_len, packed, new, w_uk, w_uv, suffix)


def prefix_kernel(
    len_ref, base_ref, q_ref, k_hbm, v_hbm, own_hbm, out_ref,
    kbuf, vbuf, qs, sc, best, total, acc, osc, lsc, slots, bias, row_low, row_high,
    low_ref, high_ref, start_ref, seen, ksems, vsems,
):
    tok, tiles = vbuf.shape[0], kbuf.shape[0]

    def load_k(t):
        return pltpu.make_async_copy(k_hbm.at[t], kbuf.at[t], ksems.at[t])

    def load_v(t):
        here = pl.ds(t * TILE, TILE)
        return pltpu.make_async_copy(v_hbm.at[here, :], vbuf.at[here, :], vsems.at[t])

    for t in range(tiles):
        load_k(t).start()
    seen[0] = 0
    seen[1] = 0

    def arrive(t, which, load):
        def one(i, _):
            load(i).wait()
            return 0

        lax.fori_loop(seen[which], t + 1, one, 0)
        seen[which] = jnp.maximum(seen[which], t + 1)

    ids = q_ref[:, 384:400, :].reshape(256, 128).astype(F32)
    index = iota((256, 128), 0).astype(F32)
    flat = jnp.transpose(ids)[0:8, :]
    key = index + 8192.0
    shift = jnp.full((256, 128), 0.0, F32)
    begin = jnp.int32(0) - base_ref[0]
    zero = jnp.int32(0)
    rows_before, units, slot, room_left = zero, zero, zero, zero
    lows, highs = [], []
    for p in range(8):
        end = begin + len_ref[p]
        low, high = jnp.maximum(begin, 0), jnp.minimum(end, tok)
        lows.append(low)
        highs.append(high)
        begin = end
        rows = jnp.sum(jnp.where(flat[0:1, :] == float(p), 1.0, 0.0)).astype(jnp.int32)
        rows = jnp.where(high > low, rows, 0)
        hit = (ids == float(p)) & (rows > 0)
        key = jnp.where(hit, index + float(p * 256), key)
        shift = jnp.where(hit, (slot - rows_before).astype(F32), shift)
        padded = (rows + 15) // 16 * 16
        joins = padded <= room_left
        more = jnp.where(joins, 0, (rows + (CHUNK - 1)) // CHUNK)

        @pl.when(joins & (rows > 0))
        def _():
            high_ref[units - 1] = high

        for c in range(256 // CHUNK):
            @pl.when(c < more)
            def _():
                low_ref[units + c] = low
                high_ref[units + c] = high
                start_ref[units + c] = slot + c * CHUNK
        units = units + more
        room_left = jnp.where(joins, room_left, more * CHUNK) - padded
        slot = slot + padded
        rows_before = rows_before + rows
    blocks = (slot + (CHUNK - 1)) // CHUNK

    across = jnp.transpose(key)[0:1, :]
    rank = jnp.sum(jnp.where(across < key[:, 0:1], 1.0, 0.0), axis=1, keepdims=True)
    mine = jnp.where(key < 8192.0, rank + shift, -1.0)
    slots[...] = mine
    across = jnp.transpose(mine)[0:1, :]
    osc[...] = jnp.zeros(osc.shape, BF)
    lsc[...] = jnp.zeros(lsc.shape, F32)

    def gather(b, _):
        rows = pl.ds(pl.multiple_of(b * CHUNK, CHUNK), CHUNK)
        want = (iota((CHUNK, 256), 0) + b * CHUNK).astype(F32)
        pick = jnp.where(across == want, 1.0, 0.0).astype(BF)
        which = mm(pick, (ids + 1.0).astype(BF))
        low = jnp.zeros((CHUNK, 128), jnp.int32)
        high = jnp.zeros((CHUNK, 128), jnp.int32)
        for p in range(8):
            low = jnp.where(which == p + 1.0, lows[p], low)
            high = jnp.where(which == p + 1.0, highs[p], high)
        row_low[rows, :] = low
        row_high[rows, :] = high
        for h in range(0, 24, 2):
            pair = [q_ref[:, g * 16 : g * 16 + 16, :].reshape(256, 128) for g in (h, h + 1)]
            both = mm(pick, jnp.concatenate(pair, axis=1)).astype(BF)
            for g in (0, 1):
                part = both[:, g * 128 : g * 128 + 128]
                if h < 16:
                    qs[h + g, rows, 0:128] = part
                else:
                    qs[h + g - 16, rows, 128:256] = part
                    qs[h + g - 8, rows, 128:256] = part
        return 0

    lax.fori_loop(0, blocks, gather, 0)
    rest = pl.ds(pl.multiple_of(blocks * CHUNK, CHUNK), CHUNK)
    qs[:, rest, :] = jnp.zeros((16, CHUNK, 256), BF)
    row_low[rest, :] = jnp.zeros((CHUNK, 128), jnp.int32)
    row_high[rest, :] = jnp.zeros((CHUNK, 128), jnp.int32)

    def unit(u, _):
        low, high = low_ref[u], high_ref[u]
        rows = pl.ds(pl.multiple_of(start_ref[u], 16), CHUNK)
        first, last = low // TILE, (high + (TILE - 1)) // TILE
        best[...] = jnp.full(best.shape, NEG, F32)

        def score(t, _):
            arrive(t, 0, load_k)
            pos = iota((CHUNK, TILE), 1) + t * TILE
            row_from = jnp.concatenate([row_low[rows, :]] * (TILE // 128), axis=1)
            row_to = jnp.concatenate([row_high[rows, :]] * (TILE // 128), axis=1)
            bias[...] = jnp.where((pos >= row_from) & (pos < row_to), 0.0, NEG)
            for h in range(16):
                side = slice(0, 128) if h < 8 else slice(128, 256)
                key = jnp.concatenate([kbuf[t, h * 128 + 256 : h * 128 + 384, :], kbuf[t, side, :]], axis=0)
                s = mm(qs[h, rows, :], key) + bias[...]
                sc[t, h] = s
                top = best[h]
                for v in range(0, TILE, 128):
                    top = jnp.maximum(top, s[:, v : v + 128])
                best[h] = top
            return 0

        lax.fori_loop(first, last, score, 0)

        for h in range(16):
            best[h] = jnp.broadcast_to(jnp.max(best[h], axis=1, keepdims=True), (CHUNK, 128))
        acc[...] = jnp.zeros(acc.shape, F32)
        total[...] = jnp.zeros(total.shape, F32)

        def weigh(t, _):
            arrive(t, 1, load_v)
            here = pl.ds(pl.multiple_of(t * TILE, TILE), TILE)
            for h in range(16):
                top = best[h]
                p = jnp.exp2(sc[t, h] - jnp.concatenate([top] * (TILE // 128), axis=1))
                add = total[h]
                for v in range(0, TILE, 128):
                    add = add + p[:, v : v + 128]
                total[h] = add
                acc[h] += mm(p.astype(BF), vbuf[here, h * 128 : h * 128 + 128])
            return 0

        lax.fori_loop(first, last, weigh, 0)
        lane = iota((CHUNK, 128), 1)
        lse = jnp.zeros((CHUNK, 128), F32)
        for h in range(16):
            full = jnp.sum(total[h], axis=1, keepdims=True)
            osc[h, rows, :] = (acc[h] / full).astype(BF)
            lse = jnp.where(lane == h, best[h] + jnp.log2(full), lse)
        lsc[rows, :] = lse
        return 0

    for t in range(tiles):
        load_v(t).start()
    lax.fori_loop(0, units, unit, 0)
    arrive(tiles - 1, 0, load_k)
    arrive(tiles - 1, 1, load_v)

    lane = iota((256, 128), 1)
    ok = slots[...] >= 0.0
    empty = jnp.where((lane < 16) & ~ok, NEG, 0.0).astype(BF)
    out_ref[:, 0:256, :] = jnp.zeros((16, 256, 128), BF)
    out_ref[:, 256:272, :] = empty.reshape(16, 16, 128)

    def scatter(b, _):
        rows = pl.ds(pl.multiple_of(b * CHUNK, CHUNK), CHUNK)
        back = jnp.where(slots[...] == (lane + b * CHUNK).astype(F32), 1.0, 0.0).astype(BF)
        for h in range(0, 16, 2):
            both = mm(back, jnp.concatenate([osc[h, rows, :], osc[h + 1, rows, :]], axis=1))
            for g in (0, 1):
                here = slice((h + g) * 16, (h + g) * 16 + 16)
                part = both[:, g * 128 : g * 128 + 128].reshape(16, 16, 128)
                out_ref[:, here, :] = (out_ref[:, here, :].astype(F32) + part).astype(BF)
        lse = lsc[rows, :]
        hi = lse.astype(BF)
        rest = lse - hi.astype(F32)
        mid = rest.astype(BF)
        lo = (rest - mid.astype(F32)).astype(BF)
        merged = hi.astype(F32) + pltpu.roll(mid.astype(F32), 16, 1) + pltpu.roll(lo.astype(F32), 32, 1)
        part = mm(back, merged.astype(BF)).reshape(16, 16, 128)
        out_ref[:, 256:272, :] = (out_ref[:, 256:272, :].astype(F32) + part).astype(BF)
        return 0

    lax.fori_loop(0, blocks, scatter, 0)


def prefix(lengths, base, got, k, v, own_lse):
    tiles, tok = k.shape[0], v.shape[0]
    room = 384 + CHUNK
    return pl.pallas_call(
        prefix_kernel,
        out_shape=jax.ShapeDtypeStruct((16, 272, 128), BF),
        in_specs=[SM, SM, VM, HB, HB, HB],
        out_specs=VM,
        scratch_shapes=[
            pltpu.VMEM(k.shape, BF),
            pltpu.VMEM(v.shape, BF),
            pltpu.VMEM((16, room, 256), BF),
            pltpu.VMEM((tiles, 16, CHUNK, TILE), F32),
            pltpu.VMEM((16, CHUNK, 128), F32),
            pltpu.VMEM((16, CHUNK, 128), F32),
            pltpu.VMEM((16, CHUNK, 128), F32),
            pltpu.VMEM((16, room, 128), BF),
            pltpu.VMEM((room, 128), F32),
            pltpu.VMEM((256, 128), F32),
            pltpu.VMEM((CHUNK, TILE), F32),
            pltpu.VMEM((room, 128), jnp.int32),
            pltpu.VMEM((room, 128), jnp.int32),
            pltpu.SMEM((16,), jnp.int32),
            pltpu.SMEM((16,), jnp.int32),
            pltpu.SMEM((16,), jnp.int32),
            pltpu.SMEM((2,), jnp.int32),
            pltpu.SemaphoreType.DMA((tiles,)),
            pltpu.SemaphoreType.DMA((tiles,)),
        ],
        compiler_params=params(48),
        cost_estimate=pl.CostEstimate(flops=6 << 30, bytes_accessed=20 << 20, transcendentals=4 << 20),
        name="prefix",
    )(lengths, base, got, k, v, own_lse)


def combine_kernel(got_ref, own_hbm, own_lse_hbm, out_ref, own_ref, own_lse_ref, sems):
    loads = [
        pltpu.make_async_copy(own_lse_hbm, own_lse_ref, sems.at[0]),
        pltpu.make_async_copy(own_hbm, own_ref, sems.at[1]),
    ]
    for load in loads:
        load.start()
    x = got_ref[:, 256:272, :].reshape(256, 128).astype(F32)
    lse = (x + pltpu.roll(x, 112, 1)) + pltpu.roll(x, 96, 1)
    lse = lse.reshape(16, 16, 128)
    loads[0].wait()
    mine = own_lse_ref[...]
    lane = iota((16, 128), 1)
    lse = jnp.where((lane < 16)[None], lse, NEG)
    top = jnp.maximum(jnp.max(lse, axis=0), mine)
    w = jnp.exp2(lse - top[None])
    w_own = jnp.exp2(mine - top)
    total = jnp.sum(w, axis=0) + w_own
    w = w / total[None]
    w_own = w_own / total
    loads[1].wait()
    for h in range(16):
        rows = slice(h * 16, h * 16 + 16)
        o = jnp.sum(got_ref[:, rows, :].astype(F32) * w[:, :, h : h + 1], axis=0)
        o = (o + own_ref[rows, :] * w_own[:, h : h + 1]).astype(BF)
        for k in range(out_ref.shape[0]):
            out_ref[k, rows, :] = o


def combine(got, own_o, own_lse):
    return pl.pallas_call(
        combine_kernel,
        out_shape=jax.ShapeDtypeStruct((16, 256, 128), BF),
        in_specs=[VM, HB, HB],
        scratch_shapes=[
            pltpu.VMEM((256, 128), F32),
            pltpu.VMEM((16, 128), F32),
            pltpu.SemaphoreType.DMA((2,)),
        ],
        out_specs=VM,
        compiler_params=params(12),
        name="combine",
    )(got, own_o, own_lse)


def project_kernel(x_ref, w_ref, out_ref):
    total = None
    for h in range(0, 16, 2):
        a = x_ref[:, h * 16 : h * 16 + 16, :].reshape(256, 128)
        b = x_ref[:, h * 16 + 16 : h * 16 + 32, :].reshape(256, 128)
        part = mm_nt(jnp.concatenate([a, b], axis=1), w_ref[:, h * 128 : h * 128 + 256])
        total = part if total is None else total + part
    out_ref[...] = total.astype(BF).reshape(out_ref.shape)


def project(x, w):
    return pl.pallas_call(
        project_kernel,
        out_shape=jax.ShapeDtypeStruct((8, 32, w.shape[0]), BF),
        in_specs=[VM, VM],
        out_specs=VM,
        compiler_params=params(12),
        name="project",
    )(x, w)


def body(
    queries,
    w_uk,
    w_uv,
    prefix_cache,
    suffix_cache,
    new_latent,
    w_out,
    request_prefix,
    prefix_lengths,
    suffix_len,
):
    scale = math.log2(math.e) / queries.shape[-1] ** 0.5
    wide = lax.axis_size("wide")
    tok = prefix_cache.shape[0]
    base = (lax.axis_index("wide") * tok).astype(jnp.int32).reshape(1)
    packed = pack(request_prefix, queries.reshape(256, 192), wide)
    got = lax.all_to_all(packed, "wide", split_axis=0, concat_axis=0, tiled=True)
    k, v = expand(prefix_cache, w_uk, w_uv, scale)
    own_o, own_lse = own(
        suffix_len, packed, w_uk, w_uv, jnp.swapaxes(suffix_cache, 1, 2), new_latent, scale
    )
    part = prefix(prefix_lengths, base, got, k, v, own_lse)
    part = lax.all_to_all(part, "wide", split_axis=0, concat_axis=0, tiled=True)
    head_out = combine(part, own_o, own_lse)
    head_out = lax.all_to_all(head_out, "wide", split_axis=0, concat_axis=0, tiled=True)
    out = project(head_out, w_out.T)
    out = lax.all_to_all(out, "head", split_axis=0, concat_axis=0, tiled=True)
    out = jnp.sum(out.astype(F32), axis=0).astype(BF)
    return out.reshape(8, 4, w_out.shape[1])


def solution(mesh):
    in_specs = (
        P("wide", None, "head", None),
        P("head", None, None),
        P("head", None, None),
        P("wide", None),
        P("wide", None, None),
        P("wide", None, None),
        P("head", "wide"),
        P("wide"),
        P(),
        P("wide"),
    )
    out_specs = P("head", None, "wide")
    return jax.shard_map(body, mesh=mesh, in_specs=in_specs, out_specs=out_specs, check_vma=False)
```

```python
import functools
import math
import jax
import jax.numpy as jnp
from jax import lax
from jax.experimental import pallas as pl
from jax.experimental.pallas import tpu as pltpu
from jax.sharding import PartitionSpec as P

NEG = -1e30
BF = jnp.bfloat16
F32 = jnp.float32
NT = (((1,), (1,)), ((), ()))
MIB = 1024 * 1024
VM = pl.BlockSpec(memory_space=pltpu.VMEM)
SM = pl.BlockSpec(memory_space=pltpu.SMEM)
HB = pl.BlockSpec(memory_space=pltpu.HBM)
TILE = 256
CHUNK = 128


def mm(a, b):
    return jnp.dot(a, b, preferred_element_type=F32)


def mm_nt(a, b):
    return lax.dot_general(a, b, NT, preferred_element_type=F32)


def iota(shape, dim):
    return lax.broadcasted_iota(jnp.int32, shape, dim)


def params(mib):
    return pltpu.CompilerParams(vmem_limit_bytes=mib * MIB)


def pack_kernel(copies, ids_ref, q_ref, out_ref):
    rows = q_ref.shape[0]
    a, b = iota((rows, rows), 0), iota((rows, rows), 1)
    turn = jnp.where((a // 16 == b % 16) & (a % 16 == b // 16), 1.0, 0.0).astype(BF)
    y = mm(turn, q_ref[...]).astype(BF)
    half = rows // 2
    c, d = iota((192, 128), 0), iota((192, 128), 1)
    left = jnp.where((c - 128 == d), 1.0, 0.0).astype(BF)
    right = jnp.where((c - 128 == d - 64) & (c >= 128), 1.0, 0.0).astype(BF)
    rope = (mm(y[:half], left) + mm(y[half:], right)).astype(BF)
    which = iota((16, 128), 0) // 4
    ids = jnp.zeros((16, 128), jnp.int32)
    for r in range(4):
        ids = jnp.where(which == r, ids_ref[r], ids)
    ids = ids.astype(F32).astype(BF)
    nope = y[:, :128]
    for k in range(copies):
        out_ref[k, 0:rows, :] = nope
        out_ref[k, rows : rows + half, :] = rope
        out_ref[k, rows + half : rows + half + 16, :] = ids


def pack(ids, queries, copies):
    return pl.pallas_call(
        functools.partial(pack_kernel, copies),
        out_shape=jax.ShapeDtypeStruct((copies, 400, 128), BF),
        in_specs=[SM, VM],
        out_specs=VM,
        compiler_params=params(56),
        name="pack",
    )(ids, queries)


OWN_STEP = 5


def expand_kernel(
    scale, len_ref, q_ref, draft_ref, flip_ref, uk_ref, uv_ref, uk_hbm, uv_hbm, suf_hbm,
    k_ref, v_ref, o_ref, lse_ref,
    lat_ref, uk_own, uv_own, suf_ref, new_ref, ql, sc, sems,
):
    step = pl.program_id(0)
    uk_load = pltpu.make_async_copy(uk_hbm, uk_own, sems.at[0])
    suf_load = pltpu.make_async_copy(suf_hbm, suf_ref, sems.at[1])
    uv_load = pltpu.make_async_copy(uv_hbm, uv_own, sems.at[2])

    @pl.when(step == 0)
    def _():
        rope = (flip_ref[512:576, :].astype(F32) * scale).astype(BF)
        k_ref[...] = jnp.zeros(k_ref.shape, BF)
        for t in range(k_ref.shape[0]):
            here = slice(t * TILE, (t + 1) * TILE)
            k_ref[t, 0:64, :] = rope[:, here]
            k_ref[t, 192:256, :] = rope[:, here]
            lat_ref[here, :] = jnp.transpose(flip_ref[0:512, here])

    @pl.when(step == 1)
    def _():
        uk_load.start()
        suf_load.start()
        uv_load.start()

    def keys(first, last):
        wk = uk_ref[...].reshape(256, 512)
        for t in range(first, last):
            k_ref[t] = (mm(wk, flip_ref[0:512, t * TILE : (t + 1) * TILE]) * scale).astype(BF)

    def values(first, last):
        wv = jnp.concatenate([uv_ref[0], uv_ref[1]], axis=1)
        for t in range(first, last):
            here = slice(t * TILE, (t + 1) * TILE)
            v_ref[here, :] = mm(lat_ref[here, :], wv).astype(BF)

    tiles = k_ref.shape[0]

    @pl.when((step > 0) & (step != OWN_STEP))
    def _():
        keys(0, tiles)
        values(0, tiles)

    @pl.when(step == OWN_STEP)
    def _():
        uk_load.wait()
        suf_load.wait()
        uv_load.wait()
        for h in range(16):
            ql[h * 16 : h * 16 + 16, 0:512] = mm(q_ref[0, h * 16 : h * 16 + 16, :], uk_own[h]).astype(BF)
        keys(0, tiles // 4)
        c, d = iota((128, 64), 0), iota((128, 64), 1)
        first = jnp.where(c == d, 1.0, 0.0).astype(BF)
        second = jnp.where(c == d + 64, 1.0, 0.0).astype(BF)
        rope = q_ref[0, 256:384, :]
        ql[0:128, 512:576] = mm(rope, first).astype(BF)
        ql[128:256, 512:576] = mm(rope, second).astype(BF)
        q = ql[...]
        req = (iota((256, 1), 0) % 16) // 4
        top = jnp.full((256, 1), NEG, F32)
        for r in range(4):
            s = mm(q, suf_ref[r]) * scale
            ok = (req == r) & (iota((256, 512), 1) < len_ref[r])
            s = jnp.where(ok, s, NEG)
            sc[:, r * 512 : (r + 1) * 512] = s
            top = jnp.maximum(top, jnp.max(s, axis=1, keepdims=True))
            keys(tiles // 4 + r, tiles // 4 + r + 1)
        for r in range(4):
            new_ref[r * 4 : r * 4 + 4, :] = draft_ref[r].astype(F32)
        new = new_ref[...].astype(BF)
        s = mm_nt(q, new) * scale
        row, col = iota((256, 16), 0) % 16, iota((256, 16), 1)
        ok = (row // 4 == col // 4) & (col % 4 <= row % 4)
        s = jnp.where(ok, s, NEG)
        top = jnp.maximum(top, jnp.max(s, axis=1, keepdims=True))
        keys(tiles // 4 + 4, tiles)
        p = jnp.exp2(s - top)
        total = jnp.sum(p, axis=1, keepdims=True)
        o = mm(p.astype(BF), new[:, 0:512])
        for r in range(4):
            p = jnp.exp2(sc[:, r * 512 : (r + 1) * 512] - top)
            total = total + jnp.sum(p, axis=1, keepdims=True)
            o = o + mm_nt(p.astype(BF), suf_ref[r, 0:512, :])
            values(r, r + 1)
        o = (o / total).astype(BF)
        lse = top + jnp.log2(total)
        values(4, tiles)
        lane = iota((16, 128), 1)
        packed = jnp.zeros((16, 128), F32)
        for h in range(16):
            o_ref[h * 16 : h * 16 + 16, :] = mm(o[h * 16 : h * 16 + 16], uv_own[h])
            packed = jnp.where(lane == h, lse[h * 16 : h * 16 + 16], packed)
        lse_ref[...] = packed


def expand(cache, w_uk, w_uv, scale, suffix_len, packed, suffix, draft):
    tok = cache.shape[0]
    return pl.pallas_call(
        functools.partial(expand_kernel, scale),
        grid=(9,),
        out_shape=[
            jax.ShapeDtypeStruct((tok // TILE, 2304, TILE), BF),
            jax.ShapeDtypeStruct((tok, 2048), BF),
            jax.ShapeDtypeStruct((256, 128), F32),
            jax.ShapeDtypeStruct((16, 128), F32),
        ],
        in_specs=[
            SM,
            pl.BlockSpec((1, 400, 128), lambda g: (0, 0, 0)),
            pl.BlockSpec((4, 4, 576), lambda g: (0, 0, 0)),
            pl.BlockSpec((576, tok), lambda g: (0, 0)),
            pl.BlockSpec((2, 128, 512), lambda g: (jnp.maximum(g - 1, 0), 0, 0)),
            pl.BlockSpec((2, 512, 128), lambda g: (jnp.maximum(g - 1, 0), 0, 0)),
            HB,
            HB,
            HB,
        ],
        out_specs=[
            pl.BlockSpec((tok // TILE, 256, TILE), lambda g: (0, g, 0)),
            pl.BlockSpec((tok, 256), lambda g: (0, jnp.maximum(g - 1, 0))),
            pl.BlockSpec((256, 128), lambda g: (0, 0)),
            pl.BlockSpec((16, 128), lambda g: (0, 0)),
        ],
        scratch_shapes=[
            pltpu.VMEM((tok, 512), BF),
            pltpu.VMEM(w_uk.shape, BF),
            pltpu.VMEM(w_uv.shape, BF),
            pltpu.VMEM(suffix.shape, BF),
            pltpu.VMEM((16, 576), F32),
            pltpu.VMEM((256, 576), BF),
            pltpu.VMEM((256, 2048), F32),
            pltpu.SemaphoreType.DMA((3,)),
        ],
        compiler_params=params(56),
        cost_estimate=pl.CostEstimate(
            flops=2 * 2 * tok * 512 * 2048 + (3 << 30), bytes_accessed=31 << 20, transcendentals=1 << 19
        ),
        name="expand",
    )(suffix_len, packed, draft, cache.T, w_uk, w_uv, w_uk, w_uv, suffix)


def prefix_kernel(
    len_ref, base_ref, q_ref, k_hbm, v_hbm, out_ref,
    kbuf, vbuf, qs, sc, best, total, acc, osc, lsc, slots, bias, row_low, row_high,
    low_ref, high_ref, start_ref, seen, ksems, vsems,
):
    tok, tiles = vbuf.shape[0], kbuf.shape[0]

    def load_k(t):
        return pltpu.make_async_copy(k_hbm.at[t], kbuf.at[t], ksems.at[t])

    def load_v(t):
        here = pl.ds(t * TILE, TILE)
        return pltpu.make_async_copy(v_hbm.at[here, :], vbuf.at[here, :], vsems.at[t])

    for t in range(tiles):
        load_k(t).start()
    seen[0] = 0
    seen[1] = 0

    def arrive(t, which, load):
        def one(i, _):
            load(i).wait()
            return 0

        lax.fori_loop(seen[which], t + 1, one, 0)
        seen[which] = jnp.maximum(seen[which], t + 1)

    ids = q_ref[:, 384:400, :].reshape(256, 128).astype(F32)
    index = iota((256, 128), 0).astype(F32)
    flat = jnp.transpose(ids)[0:8, :]
    key = index + 8192.0
    shift = jnp.full((256, 128), 0.0, F32)
    begin = jnp.int32(0) - base_ref[0]
    zero = jnp.int32(0)
    rows_before, units, slot, room_left = zero, zero, zero, zero
    lows, highs = [], []
    for p in range(8):
        end = begin + len_ref[p]
        low, high = jnp.maximum(begin, 0), jnp.minimum(end, tok)
        lows.append(low)
        highs.append(high)
        begin = end
        rows = jnp.sum(jnp.where(flat[0:1, :] == float(p), 1.0, 0.0)).astype(jnp.int32)
        rows = jnp.where(high > low, rows, 0)
        hit = (ids == float(p)) & (rows > 0)
        key = jnp.where(hit, index + float(p * 256), key)
        shift = jnp.where(hit, (slot - rows_before).astype(F32), shift)
        padded = (rows + 15) // 16 * 16
        joins = padded <= room_left
        more = jnp.where(joins, 0, (rows + (CHUNK - 1)) // CHUNK)

        @pl.when(joins & (rows > 0))
        def _():
            high_ref[units - 1] = high

        for c in range(256 // CHUNK):
            @pl.when(c < more)
            def _():
                low_ref[units + c] = low
                high_ref[units + c] = high
                start_ref[units + c] = slot + c * CHUNK
        units = units + more
        room_left = jnp.where(joins, room_left, more * CHUNK) - padded
        slot = slot + padded
        rows_before = rows_before + rows
    blocks = (slot + (CHUNK - 1)) // CHUNK

    across = jnp.transpose(key)[0:1, :]
    rank = jnp.sum(jnp.where(across < key[:, 0:1], 1.0, 0.0), axis=1, keepdims=True)
    mine = jnp.where(key < 8192.0, rank + shift, -1.0)
    slots[...] = mine
    across = jnp.transpose(mine)[0:1, :]
    osc[...] = jnp.zeros(osc.shape, BF)
    lsc[...] = jnp.zeros(lsc.shape, F32)

    def gather(b, _):
        rows = pl.ds(pl.multiple_of(b * CHUNK, CHUNK), CHUNK)
        want = (iota((CHUNK, 256), 0) + b * CHUNK).astype(F32)
        pick = jnp.where(across == want, 1.0, 0.0).astype(BF)
        which = mm(pick, (ids + 1.0).astype(BF))
        low = jnp.zeros((CHUNK, 128), jnp.int32)
        high = jnp.zeros((CHUNK, 128), jnp.int32)
        for p in range(8):
            low = jnp.where(which == p + 1.0, lows[p], low)
            high = jnp.where(which == p + 1.0, highs[p], high)
        row_low[rows, :] = low
        row_high[rows, :] = high
        for h in range(0, 24, 2):
            pair = [q_ref[:, g * 16 : g * 16 + 16, :].reshape(256, 128) for g in (h, h + 1)]
            both = mm(pick, jnp.concatenate(pair, axis=1)).astype(BF)
            for g in (0, 1):
                part = both[:, g * 128 : g * 128 + 128]
                if h < 16:
                    qs[h + g, rows, 0:128] = part
                else:
                    qs[h + g - 16, rows, 128:256] = part
                    qs[h + g - 8, rows, 128:256] = part
        return 0

    lax.fori_loop(0, blocks, gather, 0)
    rest = pl.ds(pl.multiple_of(blocks * CHUNK, CHUNK), CHUNK)
    qs[:, rest, :] = jnp.zeros((16, CHUNK, 256), BF)
    row_low[rest, :] = jnp.zeros((CHUNK, 128), jnp.int32)
    row_high[rest, :] = jnp.zeros((CHUNK, 128), jnp.int32)

    def unit(u, _):
        low, high = low_ref[u], high_ref[u]
        rows = pl.ds(pl.multiple_of(start_ref[u], 16), CHUNK)
        first, last = low // TILE, (high + (TILE - 1)) // TILE
        best[...] = jnp.full(best.shape, NEG, F32)

        def score(t, _):
            arrive(t, 0, load_k)
            pos = iota((CHUNK, TILE), 1) + t * TILE
            row_from = jnp.concatenate([row_low[rows, :]] * (TILE // 128), axis=1)
            row_to = jnp.concatenate([row_high[rows, :]] * (TILE // 128), axis=1)
            bias[...] = jnp.where((pos >= row_from) & (pos < row_to), 0.0, NEG)
            for h in range(16):
                side = slice(0, 128) if h < 8 else slice(128, 256)
                key = jnp.concatenate([kbuf[t, h * 128 + 256 : h * 128 + 384, :], kbuf[t, side, :]], axis=0)
                s = mm(qs[h, rows, :], key) + bias[...]
                sc[t, h] = s
                top = best[h]
                for v in range(0, TILE, 128):
                    top = jnp.maximum(top, s[:, v : v + 128])
                best[h] = top
            return 0

        lax.fori_loop(first, last, score, 0)

        for h in range(16):
            best[h] = jnp.broadcast_to(jnp.max(best[h], axis=1, keepdims=True), (CHUNK, 128))
        acc[...] = jnp.zeros(acc.shape, F32)
        total[...] = jnp.zeros(total.shape, F32)

        def weigh(t, _):
            arrive(t, 1, load_v)
            here = pl.ds(pl.multiple_of(t * TILE, TILE), TILE)
            for h in range(16):
                top = best[h]
                p = jnp.exp2(sc[t, h] - jnp.concatenate([top] * (TILE // 128), axis=1))
                add = total[h]
                for v in range(0, TILE, 128):
                    add = add + p[:, v : v + 128]
                total[h] = add
                acc[h] += mm(p.astype(BF), vbuf[here, h * 128 : h * 128 + 128])
            return 0

        lax.fori_loop(first, last, weigh, 0)
        lane = iota((CHUNK, 128), 1)
        lse = jnp.zeros((CHUNK, 128), F32)
        for h in range(16):
            full = jnp.sum(total[h], axis=1, keepdims=True)
            osc[h, rows, :] = (acc[h] / full).astype(BF)
            lse = jnp.where(lane == h, best[h] + jnp.log2(full), lse)
        lsc[rows, :] = lse
        return 0

    for t in range(tiles):
        load_v(t).start()
    lax.fori_loop(0, units, unit, 0)
    arrive(tiles - 1, 0, load_k)
    arrive(tiles - 1, 1, load_v)

    lane = iota((256, 128), 1)
    ok = slots[...] >= 0.0
    empty = jnp.where((lane < 16) & ~ok, NEG, 0.0).astype(BF)
    out_ref[:, 0:256, :] = jnp.zeros((16, 256, 128), BF)
    out_ref[:, 256:272, :] = empty.reshape(16, 16, 128)

    def scatter(b, _):
        rows = pl.ds(pl.multiple_of(b * CHUNK, CHUNK), CHUNK)
        back = jnp.where(slots[...] == (lane + b * CHUNK).astype(F32), 1.0, 0.0).astype(BF)
        for h in range(0, 16, 2):
            both = mm(back, jnp.concatenate([osc[h, rows, :], osc[h + 1, rows, :]], axis=1))
            for g in (0, 1):
                here = slice((h + g) * 16, (h + g) * 16 + 16)
                part = both[:, g * 128 : g * 128 + 128].reshape(16, 16, 128)
                out_ref[:, here, :] = (out_ref[:, here, :].astype(F32) + part).astype(BF)
        lse = lsc[rows, :]
        hi = lse.astype(BF)
        rest = lse - hi.astype(F32)
        mid = rest.astype(BF)
        lo = (rest - mid.astype(F32)).astype(BF)
        merged = hi.astype(F32) + pltpu.roll(mid.astype(F32), 16, 1) + pltpu.roll(lo.astype(F32), 32, 1)
        part = mm(back, merged.astype(BF)).reshape(16, 16, 128)
        out_ref[:, 256:272, :] = (out_ref[:, 256:272, :].astype(F32) + part).astype(BF)
        return 0

    lax.fori_loop(0, blocks, scatter, 0)


def prefix(lengths, base, got, k, v):
    tiles, tok = k.shape[0], v.shape[0]
    room = 384 + CHUNK
    return pl.pallas_call(
        prefix_kernel,
        out_shape=jax.ShapeDtypeStruct((16, 272, 128), BF),
        in_specs=[SM, SM, VM, HB, HB],
        out_specs=VM,
        scratch_shapes=[
            pltpu.VMEM(k.shape, BF),
            pltpu.VMEM(v.shape, BF),
            pltpu.VMEM((16, room, 256), BF),
            pltpu.VMEM((tiles, 16, CHUNK, TILE), F32),
            pltpu.VMEM((16, CHUNK, 128), F32),
            pltpu.VMEM((16, CHUNK, 128), F32),
            pltpu.VMEM((16, CHUNK, 128), F32),
            pltpu.VMEM((16, room, 128), BF),
            pltpu.VMEM((room, 128), F32),
            pltpu.VMEM((256, 128), F32),
            pltpu.VMEM((CHUNK, TILE), F32),
            pltpu.VMEM((room, 128), jnp.int32),
            pltpu.VMEM((room, 128), jnp.int32),
            pltpu.SMEM((16,), jnp.int32),
            pltpu.SMEM((16,), jnp.int32),
            pltpu.SMEM((16,), jnp.int32),
            pltpu.SMEM((2,), jnp.int32),
            pltpu.SemaphoreType.DMA((tiles,)),
            pltpu.SemaphoreType.DMA((tiles,)),
        ],
        compiler_params=params(48),
        cost_estimate=pl.CostEstimate(flops=6 << 30, bytes_accessed=20 << 20, transcendentals=4 << 20),
        name="prefix",
    )(lengths, base, got, k, v)


def combine_kernel(got_ref, own_hbm, own_lse_hbm, out_ref, own_ref, own_lse_ref, sems):
    loads = [
        pltpu.make_async_copy(own_lse_hbm, own_lse_ref, sems.at[0]),
        pltpu.make_async_copy(own_hbm, own_ref, sems.at[1]),
    ]
    for load in loads:
        load.start()
    x = got_ref[:, 256:272, :].reshape(256, 128).astype(F32)
    lse = (x + pltpu.roll(x, 112, 1)) + pltpu.roll(x, 96, 1)
    lse = lse.reshape(16, 16, 128)
    loads[0].wait()
    mine = own_lse_ref[...]
    lane = iota((16, 128), 1)
    lse = jnp.where((lane < 16)[None], lse, NEG)
    top = jnp.maximum(jnp.max(lse, axis=0), mine)
    w = jnp.exp2(lse - top[None])
    w_own = jnp.exp2(mine - top)
    total = jnp.sum(w, axis=0) + w_own
    w = w / total[None]
    w_own = w_own / total
    loads[1].wait()
    for h in range(16):
        rows = slice(h * 16, h * 16 + 16)
        o = jnp.sum(got_ref[:, rows, :].astype(F32) * w[:, :, h : h + 1], axis=0)
        o = (o + own_ref[rows, :] * w_own[:, h : h + 1]).astype(BF)
        for k in range(out_ref.shape[0]):
            out_ref[k, rows, :] = o


def combine(got, own_o, own_lse):
    return pl.pallas_call(
        combine_kernel,
        out_shape=jax.ShapeDtypeStruct((16, 256, 128), BF),
        in_specs=[VM, HB, HB],
        scratch_shapes=[
            pltpu.VMEM((256, 128), F32),
            pltpu.VMEM((16, 128), F32),
            pltpu.SemaphoreType.DMA((2,)),
        ],
        out_specs=VM,
        compiler_params=params(12),
        name="combine",
    )(got, own_o, own_lse)


def project_kernel(x_ref, w_ref, out_ref):
    total = None
    for h in range(0, 16, 2):
        a = x_ref[:, h * 16 : h * 16 + 16, :].reshape(256, 128)
        b = x_ref[:, h * 16 + 16 : h * 16 + 32, :].reshape(256, 128)
        part = mm_nt(jnp.concatenate([a, b], axis=1), w_ref[:, h * 128 : h * 128 + 256])
        total = part if total is None else total + part
    out_ref[...] = total.astype(BF).reshape(out_ref.shape)


def project(x, w):
    return pl.pallas_call(
        project_kernel,
        out_shape=jax.ShapeDtypeStruct((8, 32, w.shape[0]), BF),
        in_specs=[VM, VM],
        out_specs=VM,
        compiler_params=params(12),
        name="project",
    )(x, w)


def body(
    queries,
    w_uk,
    w_uv,
    prefix_cache,
    suffix_cache,
    new_latent,
    w_out,
    request_prefix,
    prefix_lengths,
    suffix_len,
):
    scale = math.log2(math.e) / queries.shape[-1] ** 0.5
    wide = lax.axis_size("wide")
    tok = prefix_cache.shape[0]
    base = (lax.axis_index("wide") * tok).astype(jnp.int32).reshape(1)
    packed = pack(request_prefix, queries.reshape(256, 192), wide)
    got = lax.all_to_all(packed, "wide", split_axis=0, concat_axis=0, tiled=True)
    k, v, own_o, own_lse = expand(
        prefix_cache, w_uk, w_uv, scale, suffix_len, packed, jnp.swapaxes(suffix_cache, 1, 2), new_latent
    )
    part = prefix(prefix_lengths, base, got, k, v)
    part = lax.all_to_all(part, "wide", split_axis=0, concat_axis=0, tiled=True)
    head_out = combine(part, own_o, own_lse)
    head_out = lax.all_to_all(head_out, "wide", split_axis=0, concat_axis=0, tiled=True)
    out = project(head_out, w_out.T)
    out = lax.all_to_all(out, "head", split_axis=0, concat_axis=0, tiled=True)
    out = jnp.sum(out.astype(F32), axis=0).astype(BF)
    return out.reshape(8, 4, w_out.shape[1])


def solution(mesh):
    in_specs = (
        P("wide", None, "head", None),
        P("head", None, None),
        P("head", None, None),
        P("wide", None),
        P("wide", None, None),
        P("wide", None, None),
        P("head", "wide"),
        P("wide"),
        P(),
        P("wide"),
    )
    out_specs = P("head", None, "wide")
    return jax.shard_map(body, mesh=mesh, in_specs=in_specs, out_specs=out_specs, check_vma=False)
```

```python
import functools
import math
import jax
import jax.numpy as jnp
from jax import lax
from jax.experimental import pallas as pl
from jax.experimental.pallas import tpu as pltpu
from jax.sharding import PartitionSpec as P

NEG = -1e30
BF = jnp.bfloat16
F32 = jnp.float32
NT = (((1,), (1,)), ((), ()))
MIB = 1024 * 1024
VM = pl.BlockSpec(memory_space=pltpu.VMEM)
SM = pl.BlockSpec(memory_space=pltpu.SMEM)
HB = pl.BlockSpec(memory_space=pltpu.HBM)
TILE = 256
CHUNK = 128


def mm(a, b):
    return jnp.dot(a, b, preferred_element_type=F32)


def mm_nt(a, b):
    return lax.dot_general(a, b, NT, preferred_element_type=F32)


def iota(shape, dim):
    return lax.broadcasted_iota(jnp.int32, shape, dim)


def params(mib):
    return pltpu.CompilerParams(vmem_limit_bytes=mib * MIB)


def pack_kernel(copies, ids_ref, q_ref, out_ref):
    rows = q_ref.shape[0]
    a, b = iota((rows, rows), 0), iota((rows, rows), 1)
    turn = jnp.where((a // 16 == b % 16) & (a % 16 == b // 16), 1.0, 0.0).astype(BF)
    y = mm(turn, q_ref[...]).astype(BF)
    half = rows // 2
    c, d = iota((192, 128), 0), iota((192, 128), 1)
    left = jnp.where((c - 128 == d), 1.0, 0.0).astype(BF)
    right = jnp.where((c - 128 == d - 64) & (c >= 128), 1.0, 0.0).astype(BF)
    rope = (mm(y[:half], left) + mm(y[half:], right)).astype(BF)
    which = iota((16, 128), 0) // 4
    ids = jnp.zeros((16, 128), jnp.int32)
    for r in range(4):
        ids = jnp.where(which == r, ids_ref[r], ids)
    ids = ids.astype(F32).astype(BF)
    nope = y[:, :128]
    for k in range(copies):
        out_ref[k, 0:rows, :] = nope
        out_ref[k, rows : rows + half, :] = rope
        out_ref[k, rows + half : rows + half + 16, :] = ids


def pack(ids, queries, copies):
    return pl.pallas_call(
        functools.partial(pack_kernel, copies),
        out_shape=jax.ShapeDtypeStruct((copies, 400, 128), BF),
        in_specs=[SM, VM],
        out_specs=VM,
        compiler_params=params(56),
        name="pack",
    )(ids, queries)


OWN_STEP = 5


def expand_kernel(
    scale, len_ref, q_ref, draft_ref, flip_ref, uk_ref, uv_ref, uk_hbm, uv_hbm, suf_hbm,
    k_ref, v_ref, o_ref, lse_ref,
    lat_ref, uk_own, uv_own, suf_ref, new_ref, ql, sc, sems,
):
    step = pl.program_id(0)
    uk_load = pltpu.make_async_copy(uk_hbm, uk_own, sems.at[0])
    suf_load = pltpu.make_async_copy(suf_hbm, suf_ref, sems.at[1])
    uv_load = pltpu.make_async_copy(uv_hbm, uv_own, sems.at[2])

    @pl.when(step == 0)
    def _():
        rope = (flip_ref[512:576, :].astype(F32) * scale).astype(BF)
        k_ref[...] = jnp.zeros(k_ref.shape, BF)
        for t in range(k_ref.shape[0]):
            here = slice(t * TILE, (t + 1) * TILE)
            k_ref[t, 0:64, :] = rope[:, here]
            k_ref[t, 192:256, :] = rope[:, here]
            lat_ref[here, :] = jnp.transpose(flip_ref[0:512, here])

    @pl.when(step == 1)
    def _():
        uk_load.start()
        suf_load.start()
        uv_load.start()

    def keys(first, last):
        wk = uk_ref[...].reshape(256, 512)
        for t in range(first, last):
            k_ref[t] = (mm(wk, flip_ref[0:512, t * TILE : (t + 1) * TILE]) * scale).astype(BF)

    def values(first, last):
        wv = jnp.concatenate([uv_ref[0], uv_ref[1]], axis=1)
        for t in range(first, last):
            here = slice(t * TILE, (t + 1) * TILE)
            v_ref[here, :] = mm(lat_ref[here, :], wv).astype(BF)

    tiles = k_ref.shape[0]

    @pl.when((step > 0) & (step != OWN_STEP))
    def _():
        keys(0, tiles)
        values(0, tiles)

    @pl.when(step == OWN_STEP)
    def _():
        uk_load.wait()
        suf_load.wait()
        uv_load.wait()
        for h in range(16):
            ql[h * 16 : h * 16 + 16, 0:512] = mm(q_ref[0, h * 16 : h * 16 + 16, :], uk_own[h]).astype(BF)
        keys(0, tiles // 4)
        c, d = iota((128, 64), 0), iota((128, 64), 1)
        first = jnp.where(c == d, 1.0, 0.0).astype(BF)
        second = jnp.where(c == d + 64, 1.0, 0.0).astype(BF)
        rope = q_ref[0, 256:384, :]
        ql[0:128, 512:576] = mm(rope, first).astype(BF)
        ql[128:256, 512:576] = mm(rope, second).astype(BF)
        q = ql[...]
        req = (iota((256, 1), 0) % 16) // 4
        top = jnp.full((256, 1), NEG, F32)
        for r in range(4):
            s = mm(q, suf_ref[r]) * scale
            ok = (req == r) & (iota((256, 512), 1) < len_ref[r])
            s = jnp.where(ok, s, NEG)
            sc[:, r * 512 : (r + 1) * 512] = s
            top = jnp.maximum(top, jnp.max(s, axis=1, keepdims=True))
            keys(tiles // 4 + r, tiles // 4 + r + 1)
        for r in range(4):
            new_ref[r * 4 : r * 4 + 4, :] = draft_ref[r].astype(F32)
        new = new_ref[...].astype(BF)
        s = mm_nt(q, new) * scale
        row, col = iota((256, 16), 0) % 16, iota((256, 16), 1)
        ok = (row // 4 == col // 4) & (col % 4 <= row % 4)
        s = jnp.where(ok, s, NEG)
        top = jnp.maximum(top, jnp.max(s, axis=1, keepdims=True))
        keys(tiles // 4 + 4, tiles)
        p = jnp.exp2(s - top)
        total = jnp.sum(p, axis=1, keepdims=True)
        o = mm(p.astype(BF), new[:, 0:512])
        for r in range(4):
            p = jnp.exp2(sc[:, r * 512 : (r + 1) * 512] - top)
            total = total + jnp.sum(p, axis=1, keepdims=True)
            o = o + mm_nt(p.astype(BF), suf_ref[r, 0:512, :])
            values(r, r + 1)
        o = (o / total).astype(BF)
        lse = top + jnp.log2(total)
        values(4, tiles)
        lane = iota((16, 128), 1)
        packed = jnp.zeros((16, 128), F32)
        for h in range(16):
            o_ref[h * 16 : h * 16 + 16, :] = mm(o[h * 16 : h * 16 + 16], uv_own[h])
            packed = jnp.where(lane == h, lse[h * 16 : h * 16 + 16], packed)
        lse_ref[...] = packed


def expand(cache, w_uk, w_uv, scale, suffix_len, packed, suffix, draft):
    tok = cache.shape[0]
    return pl.pallas_call(
        functools.partial(expand_kernel, scale),
        grid=(9,),
        out_shape=[
            jax.ShapeDtypeStruct((tok // TILE, 2304, TILE), BF),
            jax.ShapeDtypeStruct((tok, 2048), BF),
            jax.ShapeDtypeStruct((256, 128), F32),
            jax.ShapeDtypeStruct((16, 128), F32),
        ],
        in_specs=[
            SM,
            pl.BlockSpec((1, 400, 128), lambda g: (0, 0, 0)),
            pl.BlockSpec((4, 4, 576), lambda g: (0, 0, 0)),
            pl.BlockSpec((576, tok), lambda g: (0, 0)),
            pl.BlockSpec((2, 128, 512), lambda g: (jnp.maximum(g - 1, 0), 0, 0)),
            pl.BlockSpec((2, 512, 128), lambda g: (jnp.maximum(g - 1, 0), 0, 0)),
            HB,
            HB,
            HB,
        ],
        out_specs=[
            pl.BlockSpec((tok // TILE, 256, TILE), lambda g: (0, g, 0)),
            pl.BlockSpec((tok, 256), lambda g: (0, jnp.maximum(g - 1, 0))),
            pl.BlockSpec((256, 128), lambda g: (0, 0)),
            pl.BlockSpec((16, 128), lambda g: (0, 0)),
        ],
        scratch_shapes=[
            pltpu.VMEM((tok, 512), BF),
            pltpu.VMEM(w_uk.shape, BF),
            pltpu.VMEM(w_uv.shape, BF),
            pltpu.VMEM(suffix.shape, BF),
            pltpu.VMEM((16, 576), F32),
            pltpu.VMEM((256, 576), BF),
            pltpu.VMEM((256, 2048), F32),
            pltpu.SemaphoreType.DMA((3,)),
        ],
        compiler_params=params(56),
        cost_estimate=pl.CostEstimate(
            flops=2 * 2 * tok * 512 * 2048 + (3 << 30), bytes_accessed=31 << 20, transcendentals=1 << 19
        ),
        name="expand",
    )(suffix_len, packed, draft, cache.T, w_uk, w_uv, w_uk, w_uv, suffix)


def prefix_kernel(
    len_ref, base_ref, q_ref, k_hbm, v_hbm, out_ref,
    kbuf, vbuf, qs, sc, best, total, acc, osc, lsc, slots, bias, row_low, row_high,
    low_ref, high_ref, start_ref, seen, ksems, vsems,
):
    tok, tiles = vbuf.shape[0], kbuf.shape[0]

    def load_k(t):
        return pltpu.make_async_copy(k_hbm.at[t], kbuf.at[t], ksems.at[t])

    def load_v(t):
        here = pl.ds(t * TILE, TILE)
        return pltpu.make_async_copy(v_hbm.at[here, :], vbuf.at[here, :], vsems.at[t])

    for t in range(tiles):
        load_k(t).start()
    seen[0] = 0
    seen[1] = 0

    def arrive(t, which, load):
        def one(i, _):
            load(i).wait()
            return 0

        lax.fori_loop(seen[which], t + 1, one, 0)
        seen[which] = jnp.maximum(seen[which], t + 1)

    ids = q_ref[:, 384:400, :].reshape(256, 128).astype(F32)
    index = iota((256, 128), 0).astype(F32)
    flat = jnp.transpose(ids)[0:8, :]
    key = index + 8192.0
    shift = jnp.full((256, 128), 0.0, F32)
    begin = jnp.int32(0) - base_ref[0]
    zero = jnp.int32(0)
    rows_before, units, slot, room_left = zero, zero, zero, zero
    lows, highs = [], []
    for p in range(8):
        end = begin + len_ref[p]
        low, high = jnp.maximum(begin, 0), jnp.minimum(end, tok)
        lows.append(low)
        highs.append(high)
        begin = end
        rows = jnp.sum(jnp.where(flat[0:1, :] == float(p), 1.0, 0.0)).astype(jnp.int32)
        rows = jnp.where(high > low, rows, 0)
        hit = (ids == float(p)) & (rows > 0)
        key = jnp.where(hit, index + float(p * 256), key)
        shift = jnp.where(hit, (slot - rows_before).astype(F32), shift)
        padded = (rows + 15) // 16 * 16
        joins = padded <= room_left
        more = jnp.where(joins, 0, (rows + (CHUNK - 1)) // CHUNK)

        @pl.when(joins & (rows > 0))
        def _():
            high_ref[units - 1] = high

        for c in range(256 // CHUNK):
            @pl.when(c < more)
            def _():
                low_ref[units + c] = low
                high_ref[units + c] = high
                start_ref[units + c] = slot + c * CHUNK
        units = units + more
        room_left = jnp.where(joins, room_left, more * CHUNK) - padded
        slot = slot + padded
        rows_before = rows_before + rows
    blocks = (slot + (CHUNK - 1)) // CHUNK

    across = jnp.transpose(key)[0:1, :]
    rank = jnp.sum(jnp.where(across < key[:, 0:1], 1.0, 0.0), axis=1, keepdims=True)
    mine = jnp.where(key < 8192.0, rank + shift, -1.0)
    slots[...] = mine
    across = jnp.transpose(mine)[0:1, :]
    osc[...] = jnp.zeros(osc.shape, BF)
    lsc[...] = jnp.zeros(lsc.shape, F32)

    def gather(b, _):
        rows = pl.ds(pl.multiple_of(b * CHUNK, CHUNK), CHUNK)
        want = (iota((CHUNK, 256), 0) + b * CHUNK).astype(F32)
        pick = jnp.where(across == want, 1.0, 0.0).astype(BF)
        which = mm(pick, (ids + 1.0).astype(BF))
        low = jnp.zeros((CHUNK, 128), jnp.int32)
        high = jnp.zeros((CHUNK, 128), jnp.int32)
        for p in range(8):
            low = jnp.where(which == p + 1.0, lows[p], low)
            high = jnp.where(which == p + 1.0, highs[p], high)
        row_low[rows, :] = low
        row_high[rows, :] = high
        for h in range(0, 24, 2):
            pair = [q_ref[:, g * 16 : g * 16 + 16, :].reshape(256, 128) for g in (h, h + 1)]
            both = mm(pick, jnp.concatenate(pair, axis=1)).astype(BF)
            for g in (0, 1):
                part = both[:, g * 128 : g * 128 + 128]
                if h < 16:
                    qs[h + g, rows, 0:128] = part
                else:
                    qs[h + g - 16, rows, 128:256] = part
                    qs[h + g - 8, rows, 128:256] = part
        return 0

    lax.fori_loop(0, blocks, gather, 0)
    rest = pl.ds(pl.multiple_of(blocks * CHUNK, CHUNK), CHUNK)
    qs[:, rest, :] = jnp.zeros((16, CHUNK, 256), BF)
    row_low[rest, :] = jnp.zeros((CHUNK, 128), jnp.int32)
    row_high[rest, :] = jnp.zeros((CHUNK, 128), jnp.int32)

    def unit(u, _):
        low, high = low_ref[u], high_ref[u]
        rows = pl.ds(pl.multiple_of(start_ref[u], 16), CHUNK)
        first, last = low // TILE, (high + (TILE - 1)) // TILE
        best[...] = jnp.full(best.shape, NEG, F32)

        def score(t, _):
            arrive(t, 0, load_k)
            pos = iota((CHUNK, TILE), 1) + t * TILE
            row_from = jnp.concatenate([row_low[rows, :]] * (TILE // 128), axis=1)
            row_to = jnp.concatenate([row_high[rows, :]] * (TILE // 128), axis=1)
            bias[...] = jnp.where((pos >= row_from) & (pos < row_to), 0.0, NEG)
            for h in range(16):
                side = slice(0, 128) if h < 8 else slice(128, 256)
                key = jnp.concatenate([kbuf[t, h * 128 + 256 : h * 128 + 384, :], kbuf[t, side, :]], axis=0)
                s = mm(qs[h, rows, :], key) + bias[...]
                sc[t, h] = s
                top = best[h]
                for v in range(0, TILE, 128):
                    top = jnp.maximum(top, s[:, v : v + 128])
                best[h] = top
            return 0

        lax.fori_loop(first, last, score, 0)

        for h in range(16):
            best[h] = jnp.broadcast_to(jnp.max(best[h], axis=1, keepdims=True), (CHUNK, 128))
        acc[...] = jnp.zeros(acc.shape, F32)
        total[...] = jnp.zeros(total.shape, F32)

        def weigh(t, _):
            arrive(t, 1, load_v)
            here = pl.ds(pl.multiple_of(t * TILE, TILE), TILE)
            for h in range(16):
                top = best[h]
                p = jnp.exp2(sc[t, h] - jnp.concatenate([top] * (TILE // 128), axis=1))
                add = total[h]
                for v in range(0, TILE, 128):
                    add = add + p[:, v : v + 128]
                total[h] = add
                acc[h] += mm(p.astype(BF), vbuf[here, h * 128 : h * 128 + 128])
            return 0

        lax.fori_loop(first, last, weigh, 0)
        lane = iota((CHUNK, 128), 1)
        lse = jnp.zeros((CHUNK, 128), F32)
        for h in range(16):
            full = jnp.sum(total[h], axis=1, keepdims=True)
            osc[h, rows, :] = (acc[h] / full).astype(BF)
            lse = jnp.where(lane == h, best[h] + jnp.log2(full), lse)
        lsc[rows, :] = lse
        return 0

    for t in range(tiles):
        load_v(t).start()
    lax.fori_loop(0, units, unit, 0)
    arrive(tiles - 1, 0, load_k)
    arrive(tiles - 1, 1, load_v)

    lane = iota((256, 128), 1)
    ok = slots[...] >= 0.0
    empty = jnp.where((lane < 16) & ~ok, NEG, 0.0).astype(BF)
    out_ref[:, 0:256, :] = jnp.zeros((16, 256, 128), BF)
    out_ref[:, 256:272, :] = empty.reshape(16, 16, 128)

    def scatter(b, _):
        rows = pl.ds(pl.multiple_of(b * CHUNK, CHUNK), CHUNK)
        back = jnp.where(slots[...] == (lane + b * CHUNK).astype(F32), 1.0, 0.0).astype(BF)
        for h in range(0, 16, 2):
            both = mm(back, jnp.concatenate([osc[h, rows, :], osc[h + 1, rows, :]], axis=1))
            for g in (0, 1):
                here = slice((h + g) * 16, (h + g) * 16 + 16)
                part = both[:, g * 128 : g * 128 + 128].reshape(16, 16, 128)
                out_ref[:, here, :] = (out_ref[:, here, :].astype(F32) + part).astype(BF)
        lse = lsc[rows, :]
        hi = lse.astype(BF)
        rest = lse - hi.astype(F32)
        mid = rest.astype(BF)
        lo = (rest - mid.astype(F32)).astype(BF)
        merged = hi.astype(F32) + pltpu.roll(mid.astype(F32), 16, 1) + pltpu.roll(lo.astype(F32), 32, 1)
        part = mm(back, merged.astype(BF)).reshape(16, 16, 128)
        out_ref[:, 256:272, :] = (out_ref[:, 256:272, :].astype(F32) + part).astype(BF)
        return 0

    lax.fori_loop(0, blocks, scatter, 0)


def prefix(lengths, base, got, k, v):
    tiles, tok = k.shape[0], v.shape[0]
    room = 384 + CHUNK
    return pl.pallas_call(
        prefix_kernel,
        out_shape=jax.ShapeDtypeStruct((16, 272, 128), BF),
        in_specs=[SM, SM, VM, HB, HB],
        out_specs=VM,
        scratch_shapes=[
            pltpu.VMEM(k.shape, BF),
            pltpu.VMEM(v.shape, BF),
            pltpu.VMEM((16, room, 256), BF),
            pltpu.VMEM((tiles, 16, CHUNK, TILE), F32),
            pltpu.VMEM((16, CHUNK, 128), F32),
            pltpu.VMEM((16, CHUNK, 128), F32),
            pltpu.VMEM((16, CHUNK, 128), F32),
            pltpu.VMEM((16, room, 128), BF),
            pltpu.VMEM((room, 128), F32),
            pltpu.VMEM((256, 128), F32),
            pltpu.VMEM((CHUNK, TILE), F32),
            pltpu.VMEM((room, 128), jnp.int32),
            pltpu.VMEM((room, 128), jnp.int32),
            pltpu.SMEM((16,), jnp.int32),
            pltpu.SMEM((16,), jnp.int32),
            pltpu.SMEM((16,), jnp.int32),
            pltpu.SMEM((2,), jnp.int32),
            pltpu.SemaphoreType.DMA((tiles,)),
            pltpu.SemaphoreType.DMA((tiles,)),
        ],
        compiler_params=params(48),
        cost_estimate=pl.CostEstimate(flops=6 << 30, bytes_accessed=20 << 20, transcendentals=4 << 20),
        name="prefix",
    )(lengths, base, got, k, v)


def combine_kernel(got_ref, own_hbm, own_lse_hbm, out_ref, own_ref, own_lse_ref, sems):
    loads = [
        pltpu.make_async_copy(own_lse_hbm, own_lse_ref, sems.at[0]),
        pltpu.make_async_copy(own_hbm, own_ref, sems.at[1]),
    ]
    for load in loads:
        load.start()
    x = got_ref[:, 256:272, :].reshape(256, 128).astype(F32)
    lse = (x + pltpu.roll(x, 112, 1)) + pltpu.roll(x, 96, 1)
    lse = lse.reshape(16, 16, 128)
    loads[0].wait()
    mine = own_lse_ref[...]
    lane = iota((16, 128), 1)
    lse = jnp.where((lane < 16)[None], lse, NEG)
    top = jnp.maximum(jnp.max(lse, axis=0), mine)
    w = jnp.exp2(lse - top[None])
    w_own = jnp.exp2(mine - top)
    total = jnp.sum(w, axis=0) + w_own
    w = w / total[None]
    w_own = w_own / total
    loads[1].wait()
    for h in range(16):
        rows = slice(h * 16, h * 16 + 16)
        o = jnp.sum(got_ref[:, rows, :].astype(F32) * w[:, :, h : h + 1], axis=0)
        o = (o + own_ref[rows, :] * w_own[:, h : h + 1]).astype(BF)
        for k in range(out_ref.shape[0]):
            out_ref[k, rows, :] = o


def combine(got, own_o, own_lse):
    return pl.pallas_call(
        combine_kernel,
        out_shape=jax.ShapeDtypeStruct((16, 256, 128), BF),
        in_specs=[VM, HB, HB],
        scratch_shapes=[
            pltpu.VMEM((256, 128), F32),
            pltpu.VMEM((16, 128), F32),
            pltpu.SemaphoreType.DMA((2,)),
        ],
        out_specs=VM,
        compiler_params=params(12),
        name="combine",
    )(got, own_o, own_lse)


def project_kernel(place_ref, x_ref, w_ref, keep_ref, give_ref, sums):
    total = None
    for h in range(0, 16, 2):
        a = x_ref[:, h * 16 : h * 16 + 16, :].reshape(256, 128)
        b = x_ref[:, h * 16 + 16 : h * 16 + 32, :].reshape(256, 128)
        part = mm_nt(jnp.concatenate([a, b], axis=1), w_ref[:, h * 128 : h * 128 + 256])
        total = part if total is None else total + part
    sums[...] = total
    place = place_ref[0]
    x, core = place // 2, place % 2
    for d in range(4):
        first = (x + d) % 4 * 2
        keep_ref[d] = sums[pl.ds(pl.multiple_of((first + core) * 32, 32), 32), :].astype(BF)
        give_ref[d] = sums[pl.ds(pl.multiple_of((first + 1 - core) * 32, 32), 32), :].astype(BF)


def project(place, x, w):
    shape = jax.ShapeDtypeStruct((4, 32, w.shape[0]), BF)
    return pl.pallas_call(
        project_kernel,
        out_shape=[shape, shape],
        in_specs=[SM, VM, VM],
        out_specs=[VM, VM],
        scratch_shapes=[pltpu.VMEM((256, w.shape[0]), F32)],
        compiler_params=params(12),
        name="project",
    )(place, x, w)


def pair_kernel(a_ref, b_ref, *out_refs):
    for d, out_ref in enumerate(out_refs):
        out_ref[...] = (a_ref[d].astype(F32) + b_ref[d].astype(F32)).astype(BF)


def pair(a, b):
    return pl.pallas_call(
        pair_kernel,
        out_shape=[jax.ShapeDtypeStruct(a.shape[1:], BF)] * 4,
        in_specs=[VM, VM],
        out_specs=[VM] * 4,
        compiler_params=params(4),
        name="pair",
    )(a, b)


def sum_heads(keep, give):
    other = lax.ppermute(give, "head", [(i, i // 2 * 2 + 1 - i % 2) for i in range(8)])
    parts = pair(keep, other)
    total = parts[0].astype(F32)
    for d in range(1, 4):
        moved = lax.ppermute(parts[d], "head", [(i, (i // 2 + d) % 4 * 2 + i % 2) for i in range(8)])
        total = total + moved.astype(F32)
    return total.astype(BF)


def body(
    queries,
    w_uk,
    w_uv,
    prefix_cache,
    suffix_cache,
    new_latent,
    w_out,
    request_prefix,
    prefix_lengths,
    suffix_len,
):
    scale = math.log2(math.e) / queries.shape[-1] ** 0.5
    wide = lax.axis_size("wide")
    tok = prefix_cache.shape[0]
    base = (lax.axis_index("wide") * tok).astype(jnp.int32).reshape(1)
    packed = pack(request_prefix, queries.reshape(256, 192), wide)
    got = lax.all_to_all(packed, "wide", split_axis=0, concat_axis=0, tiled=True)
    k, v, own_o, own_lse = expand(
        prefix_cache, w_uk, w_uv, scale, suffix_len, packed, jnp.swapaxes(suffix_cache, 1, 2), new_latent
    )
    part = prefix(prefix_lengths, base, got, k, v)
    part = lax.all_to_all(part, "wide", split_axis=0, concat_axis=0, tiled=True)
    head_out = combine(part, own_o, own_lse)
    head_out = lax.all_to_all(head_out, "wide", split_axis=0, concat_axis=0, tiled=True)
    place = lax.axis_index("head").astype(jnp.int32).reshape(1)
    out = sum_heads(*project(place, head_out, w_out.T))
    return out.reshape(8, 4, w_out.shape[1])


def solution(mesh):
    in_specs = (
        P("wide", None, "head", None),
        P("head", None, None),
        P("head", None, None),
        P("wide", None),
        P("wide", None, None),
        P("wide", None, None),
        P("head", "wide"),
        P("wide"),
        P(),
        P("wide"),
    )
    out_specs = P("head", None, "wide")
    return jax.shard_map(body, mesh=mesh, in_specs=in_specs, out_specs=out_specs, check_vma=False)
```

```python
import functools
import math
import jax
import jax.numpy as jnp
from jax import lax
from jax.experimental import pallas as pl
from jax.experimental.pallas import tpu as pltpu
from jax.sharding import PartitionSpec as P

NEG = -1e30
BF = jnp.bfloat16
F32 = jnp.float32
NT = (((1,), (1,)), ((), ()))
MIB = 1024 * 1024
VM = pl.BlockSpec(memory_space=pltpu.VMEM)
SM = pl.BlockSpec(memory_space=pltpu.SMEM)
HB = pl.BlockSpec(memory_space=pltpu.HBM)
TILE = 256
CHUNK = 128


def mm(a, b):
    return jnp.dot(a, b, preferred_element_type=F32)


def mm_nt(a, b):
    return lax.dot_general(a, b, NT, preferred_element_type=F32)


def iota(shape, dim):
    return lax.broadcasted_iota(jnp.int32, shape, dim)


def params(mib):
    return pltpu.CompilerParams(vmem_limit_bytes=mib * MIB)


def pack_kernel(copies, ids_ref, q_ref, out_ref):
    rows = q_ref.shape[0]
    a, b = iota((rows, rows), 0), iota((rows, rows), 1)
    turn = jnp.where((a // 16 == b % 16) & (a % 16 == b // 16), 1.0, 0.0).astype(BF)
    y = mm(turn, q_ref[...]).astype(BF)
    half = rows // 2
    c, d = iota((192, 128), 0), iota((192, 128), 1)
    left = jnp.where((c - 128 == d), 1.0, 0.0).astype(BF)
    right = jnp.where((c - 128 == d - 64) & (c >= 128), 1.0, 0.0).astype(BF)
    rope = (mm(y[:half], left) + mm(y[half:], right)).astype(BF)
    which = iota((16, 128), 0) // 4
    ids = jnp.zeros((16, 128), jnp.int32)
    for r in range(4):
        ids = jnp.where(which == r, ids_ref[r], ids)
    ids = ids.astype(F32).astype(BF)
    nope = y[:, :128]
    for k in range(copies):
        out_ref[k, 0:rows, :] = nope
        out_ref[k, rows : rows + half, :] = rope
        out_ref[k, rows + half : rows + half + 16, :] = ids


def pack(ids, queries, copies):
    return pl.pallas_call(
        functools.partial(pack_kernel, copies),
        out_shape=jax.ShapeDtypeStruct((copies, 400, 128), BF),
        in_specs=[SM, VM],
        out_specs=VM,
        compiler_params=params(56),
        name="pack",
    )(ids, queries)


OWN_STEP = 5


def expand_kernel(
    scale, len_ref, q_ref, draft_ref, flip_ref, uk_ref, uv_ref, uk_hbm, uv_hbm, suf_hbm,
    k_ref, v_ref, o_ref, lse_ref,
    lat_ref, uk_own, uv_own, suf_ref, new_ref, ql, sc, sems,
):
    step = pl.program_id(0)
    uk_load = pltpu.make_async_copy(uk_hbm, uk_own, sems.at[0])
    suf_load = pltpu.make_async_copy(suf_hbm, suf_ref, sems.at[1])
    uv_load = pltpu.make_async_copy(uv_hbm, uv_own, sems.at[2])

    @pl.when(step == 0)
    def _():
        rope = (flip_ref[512:576, :].astype(F32) * scale).astype(BF)
        k_ref[...] = jnp.zeros(k_ref.shape, BF)
        for t in range(k_ref.shape[0]):
            here = slice(t * TILE, (t + 1) * TILE)
            k_ref[t, 0:64, :] = rope[:, here]
            k_ref[t, 192:256, :] = rope[:, here]
            lat_ref[here, :] = jnp.transpose(flip_ref[0:512, here])

    @pl.when(step == 1)
    def _():
        uk_load.start()
        suf_load.start()
        uv_load.start()

    def keys(first, last):
        wk = uk_ref[...].reshape(256, 512)
        for t in range(first, last):
            k_ref[t] = (mm(wk, flip_ref[0:512, t * TILE : (t + 1) * TILE]) * scale).astype(BF)

    def values(first, last):
        wv = jnp.concatenate([uv_ref[0], uv_ref[1]], axis=1)
        for t in range(first, last):
            here = slice(t * TILE, (t + 1) * TILE)
            v_ref[here, :] = mm(lat_ref[here, :], wv).astype(BF)

    tiles = k_ref.shape[0]

    @pl.when((step > 0) & (step != OWN_STEP))
    def _():
        keys(0, tiles)
        values(0, tiles)

    @pl.when(step == OWN_STEP)
    def _():
        uk_load.wait()
        suf_load.wait()
        uv_load.wait()
        for h in range(16):
            ql[h * 16 : h * 16 + 16, 0:512] = mm(q_ref[0, h * 16 : h * 16 + 16, :], uk_own[h]).astype(BF)
        keys(0, tiles // 4)
        c, d = iota((128, 64), 0), iota((128, 64), 1)
        first = jnp.where(c == d, 1.0, 0.0).astype(BF)
        second = jnp.where(c == d + 64, 1.0, 0.0).astype(BF)
        rope = q_ref[0, 256:384, :]
        ql[0:128, 512:576] = mm(rope, first).astype(BF)
        ql[128:256, 512:576] = mm(rope, second).astype(BF)
        q = ql[...]
        req = (iota((256, 1), 0) % 16) // 4
        top = jnp.full((256, 1), NEG, F32)
        for r in range(4):
            s = mm(q, suf_ref[r]) * scale
            ok = (req == r) & (iota((256, 512), 1) < len_ref[r])
            s = jnp.where(ok, s, NEG)
            sc[:, r * 512 : (r + 1) * 512] = s
            top = jnp.maximum(top, jnp.max(s, axis=1, keepdims=True))
            keys(tiles // 4 + r, tiles // 4 + r + 1)
        for r in range(4):
            new_ref[r * 4 : r * 4 + 4, :] = draft_ref[r].astype(F32)
        new = new_ref[...].astype(BF)
        s = mm_nt(q, new) * scale
        row, col = iota((256, 16), 0) % 16, iota((256, 16), 1)
        ok = (row // 4 == col // 4) & (col % 4 <= row % 4)
        s = jnp.where(ok, s, NEG)
        top = jnp.maximum(top, jnp.max(s, axis=1, keepdims=True))
        keys(tiles // 4 + 4, tiles)
        p = jnp.exp2(s - top)
        total = jnp.sum(p, axis=1, keepdims=True)
        o = mm(p.astype(BF), new[:, 0:512])
        for r in range(4):
            p = jnp.exp2(sc[:, r * 512 : (r + 1) * 512] - top)
            total = total + jnp.sum(p, axis=1, keepdims=True)
            o = o + mm_nt(p.astype(BF), suf_ref[r, 0:512, :])
            values(r, r + 1)
        o = (o / total).astype(BF)
        lse = top + jnp.log2(total)
        values(4, tiles)
        lane = iota((16, 128), 1)
        packed = jnp.zeros((16, 128), F32)
        for h in range(16):
            o_ref[h * 16 : h * 16 + 16, :] = mm(o[h * 16 : h * 16 + 16], uv_own[h])
            packed = jnp.where(lane == h, lse[h * 16 : h * 16 + 16], packed)
        lse_ref[...] = packed


def expand(cache, w_uk, w_uv, scale, suffix_len, packed, suffix, draft):
    tok = cache.shape[0]
    return pl.pallas_call(
        functools.partial(expand_kernel, scale),
        grid=(9,),
        out_shape=[
            jax.ShapeDtypeStruct((tok // TILE, 2304, TILE), BF),
            jax.ShapeDtypeStruct((tok, 2048), BF),
            jax.ShapeDtypeStruct((256, 128), F32),
            jax.ShapeDtypeStruct((16, 128), F32),
        ],
        in_specs=[
            SM,
            pl.BlockSpec((1, 400, 128), lambda g: (0, 0, 0)),
            pl.BlockSpec((4, 4, 576), lambda g: (0, 0, 0)),
            pl.BlockSpec((576, tok), lambda g: (0, 0)),
            pl.BlockSpec((2, 128, 512), lambda g: (jnp.maximum(g - 1, 0), 0, 0)),
            pl.BlockSpec((2, 512, 128), lambda g: (jnp.maximum(g - 1, 0), 0, 0)),
            HB,
            HB,
            HB,
        ],
        out_specs=[
            pl.BlockSpec((tok // TILE, 256, TILE), lambda g: (0, g, 0)),
            pl.BlockSpec((tok, 256), lambda g: (0, jnp.maximum(g - 1, 0))),
            pl.BlockSpec((256, 128), lambda g: (0, 0)),
            pl.BlockSpec((16, 128), lambda g: (0, 0)),
        ],
        scratch_shapes=[
            pltpu.VMEM((tok, 512), BF),
            pltpu.VMEM(w_uk.shape, BF),
            pltpu.VMEM(w_uv.shape, BF),
            pltpu.VMEM(suffix.shape, BF),
            pltpu.VMEM((16, 576), F32),
            pltpu.VMEM((256, 576), BF),
            pltpu.VMEM((256, 2048), F32),
            pltpu.SemaphoreType.DMA((3,)),
        ],
        compiler_params=params(56),
        cost_estimate=pl.CostEstimate(
            flops=2 * 2 * tok * 512 * 2048 + (3 << 30), bytes_accessed=31 << 20, transcendentals=1 << 19
        ),
        name="expand",
    )(suffix_len, packed, draft, cache.T, w_uk, w_uv, w_uk, w_uv, suffix)


def prefix_kernel(
    len_ref, base_ref, q_ref, k_hbm, v_hbm, out_ref,
    kbuf, vbuf, qs, sc, best, total, acc, osc, lsc, slots, bias, row_low, row_high,
    low_ref, high_ref, start_ref, seen, ksems, vsems,
):
    tok, tiles = vbuf.shape[0], kbuf.shape[0]

    def load_k(t):
        return pltpu.make_async_copy(k_hbm.at[t], kbuf.at[t], ksems.at[t])

    def load_v(t):
        here = pl.ds(t * TILE, TILE)
        return pltpu.make_async_copy(v_hbm.at[here, :], vbuf.at[here, :], vsems.at[t])

    for t in range(tiles):
        load_k(t).start()
    seen[0] = 0
    seen[1] = 0

    def arrive(t, which, load):
        def one(i, _):
            load(i).wait()
            return 0

        lax.fori_loop(seen[which], t + 1, one, 0)
        seen[which] = jnp.maximum(seen[which], t + 1)

    ids = q_ref[:, 384:400, :].reshape(256, 128).astype(F32)
    index = iota((256, 128), 0).astype(F32)
    flat = jnp.transpose(ids)[0:8, :]
    key = index + 8192.0
    shift = jnp.full((256, 128), 0.0, F32)
    begin = jnp.int32(0) - base_ref[0]
    zero = jnp.int32(0)
    rows_before, units, slot, room_left = zero, zero, zero, zero
    lows, highs = [], []
    for p in range(8):
        end = begin + len_ref[p]
        low, high = jnp.maximum(begin, 0), jnp.minimum(end, tok)
        lows.append(low)
        highs.append(high)
        begin = end
        rows = jnp.sum(jnp.where(flat[0:1, :] == float(p), 1.0, 0.0)).astype(jnp.int32)
        rows = jnp.where(high > low, rows, 0)
        hit = (ids == float(p)) & (rows > 0)
        key = jnp.where(hit, index + float(p * 256), key)
        shift = jnp.where(hit, (slot - rows_before).astype(F32), shift)
        padded = (rows + 15) // 16 * 16
        joins = padded <= room_left
        more = jnp.where(joins, 0, (rows + (CHUNK - 1)) // CHUNK)

        @pl.when(joins & (rows > 0))
        def _():
            high_ref[units - 1] = high

        for c in range(256 // CHUNK):
            @pl.when(c < more)
            def _():
                low_ref[units + c] = low
                high_ref[units + c] = high
                start_ref[units + c] = slot + c * CHUNK
        units = units + more
        room_left = jnp.where(joins, room_left, more * CHUNK) - padded
        slot = slot + padded
        rows_before = rows_before + rows
    blocks = (slot + (CHUNK - 1)) // CHUNK

    across = jnp.transpose(key)[0:1, :]
    rank = jnp.sum(jnp.where(across < key[:, 0:1], 1.0, 0.0), axis=1, keepdims=True)
    mine = jnp.where(key < 8192.0, rank + shift, -1.0)
    slots[...] = mine
    across = jnp.transpose(mine)[0:1, :]
    osc[...] = jnp.zeros(osc.shape, BF)
    lsc[...] = jnp.zeros(lsc.shape, F32)

    def gather(b, _):
        rows = pl.ds(pl.multiple_of(b * CHUNK, CHUNK), CHUNK)
        want = (iota((CHUNK, 256), 0) + b * CHUNK).astype(F32)
        pick = jnp.where(across == want, 1.0, 0.0).astype(BF)
        which = mm(pick, (ids + 1.0).astype(BF))
        low = jnp.zeros((CHUNK, 128), jnp.int32)
        high = jnp.zeros((CHUNK, 128), jnp.int32)
        for p in range(8):
            low = jnp.where(which == p + 1.0, lows[p], low)
            high = jnp.where(which == p + 1.0, highs[p], high)
        row_low[rows, :] = low
        row_high[rows, :] = high
        for h in range(0, 24, 2):
            pair = [q_ref[:, g * 16 : g * 16 + 16, :].reshape(256, 128) for g in (h, h + 1)]
            both = mm(pick, jnp.concatenate(pair, axis=1)).astype(BF)
            for g in (0, 1):
                part = both[:, g * 128 : g * 128 + 128]
                if h < 16:
                    qs[h + g, rows, 0:128] = part
                else:
                    qs[h + g - 16, rows, 128:256] = part
                    qs[h + g - 8, rows, 128:256] = part
        return 0

    lax.fori_loop(0, blocks, gather, 0)
    rest = pl.ds(pl.multiple_of(blocks * CHUNK, CHUNK), CHUNK)
    qs[:, rest, :] = jnp.zeros((16, CHUNK, 256), BF)
    row_low[rest, :] = jnp.zeros((CHUNK, 128), jnp.int32)
    row_high[rest, :] = jnp.zeros((CHUNK, 128), jnp.int32)

    def unit(u, _):
        low, high = low_ref[u], high_ref[u]
        rows = pl.ds(pl.multiple_of(start_ref[u], 16), CHUNK)
        first, last = low // TILE, (high + (TILE - 1)) // TILE
        best[...] = jnp.full(best.shape, NEG, F32)

        def score(t, _):
            arrive(t, 0, load_k)
            pos = iota((CHUNK, TILE), 1) + t * TILE
            row_from = jnp.concatenate([row_low[rows, :]] * (TILE // 128), axis=1)
            row_to = jnp.concatenate([row_high[rows, :]] * (TILE // 128), axis=1)
            bias[...] = jnp.where((pos >= row_from) & (pos < row_to), 0.0, NEG)
            for h in range(16):
                side = slice(0, 128) if h < 8 else slice(128, 256)
                key = jnp.concatenate([kbuf[t, h * 128 + 256 : h * 128 + 384, :], kbuf[t, side, :]], axis=0)
                s = mm(qs[h, rows, :], key) + bias[...]
                sc[t, h] = s
                top = best[h]
                for v in range(0, TILE, 128):
                    top = jnp.maximum(top, s[:, v : v + 128])
                best[h] = top
            return 0

        lax.fori_loop(first, last, score, 0)

        for h in range(16):
            best[h] = jnp.broadcast_to(jnp.max(best[h], axis=1, keepdims=True), (CHUNK, 128))
        acc[...] = jnp.zeros(acc.shape, F32)
        total[...] = jnp.zeros(total.shape, F32)

        def weigh(t, _):
            arrive(t, 1, load_v)
            here = pl.ds(pl.multiple_of(t * TILE, TILE), TILE)
            for h in range(16):
                top = best[h]
                p = jnp.exp2(sc[t, h] - jnp.concatenate([top] * (TILE // 128), axis=1))
                add = total[h]
                for v in range(0, TILE, 128):
                    add = add + p[:, v : v + 128]
                total[h] = add
                acc[h] += mm(p.astype(BF), vbuf[here, h * 128 : h * 128 + 128])
            return 0

        lax.fori_loop(first, last, weigh, 0)
        lane = iota((CHUNK, 128), 1)
        lse = jnp.zeros((CHUNK, 128), F32)
        for h in range(16):
            full = jnp.sum(total[h], axis=1, keepdims=True)
            osc[h, rows, :] = (acc[h] / full).astype(BF)
            lse = jnp.where(lane == h, best[h] + jnp.log2(full), lse)
        lsc[rows, :] = lse
        return 0

    for t in range(tiles):
        load_v(t).start()
    lax.fori_loop(0, units, unit, 0)
    arrive(tiles - 1, 0, load_k)
    arrive(tiles - 1, 1, load_v)

    lane = iota((256, 128), 1)
    ok = slots[...] >= 0.0
    empty = jnp.where((lane < 16) & ~ok, NEG, 0.0).astype(BF)
    out_ref[:, 0:256, :] = jnp.zeros((16, 256, 128), BF)
    out_ref[:, 256:272, :] = empty.reshape(16, 16, 128)

    def scatter(b, _):
        rows = pl.ds(pl.multiple_of(b * CHUNK, CHUNK), CHUNK)
        back = jnp.where(slots[...] == (lane + b * CHUNK).astype(F32), 1.0, 0.0).astype(BF)
        for h in range(0, 16, 2):
            both = mm(back, jnp.concatenate([osc[h, rows, :], osc[h + 1, rows, :]], axis=1))
            for g in (0, 1):
                here = slice((h + g) * 16, (h + g) * 16 + 16)
                part = both[:, g * 128 : g * 128 + 128].reshape(16, 16, 128)
                out_ref[:, here, :] = (out_ref[:, here, :].astype(F32) + part).astype(BF)
        lse = lsc[rows, :]
        hi = lse.astype(BF)
        rest = lse - hi.astype(F32)
        mid = rest.astype(BF)
        lo = (rest - mid.astype(F32)).astype(BF)
        merged = hi.astype(F32) + pltpu.roll(mid.astype(F32), 16, 1) + pltpu.roll(lo.astype(F32), 32, 1)
        part = mm(back, merged.astype(BF)).reshape(16, 16, 128)
        out_ref[:, 256:272, :] = (out_ref[:, 256:272, :].astype(F32) + part).astype(BF)
        return 0

    lax.fori_loop(0, blocks, scatter, 0)


def prefix(lengths, base, got, k, v):
    tiles, tok = k.shape[0], v.shape[0]
    room = 384 + CHUNK
    return pl.pallas_call(
        prefix_kernel,
        out_shape=jax.ShapeDtypeStruct((16, 272, 128), BF),
        in_specs=[SM, SM, VM, HB, HB],
        out_specs=VM,
        scratch_shapes=[
            pltpu.VMEM(k.shape, BF),
            pltpu.VMEM(v.shape, BF),
            pltpu.VMEM((16, room, 256), BF),
            pltpu.VMEM((tiles, 16, CHUNK, TILE), F32),
            pltpu.VMEM((16, CHUNK, 128), F32),
            pltpu.VMEM((16, CHUNK, 128), F32),
            pltpu.VMEM((16, CHUNK, 128), F32),
            pltpu.VMEM((16, room, 128), BF),
            pltpu.VMEM((room, 128), F32),
            pltpu.VMEM((256, 128), F32),
            pltpu.VMEM((CHUNK, TILE), F32),
            pltpu.VMEM((room, 128), jnp.int32),
            pltpu.VMEM((room, 128), jnp.int32),
            pltpu.SMEM((16,), jnp.int32),
            pltpu.SMEM((16,), jnp.int32),
            pltpu.SMEM((16,), jnp.int32),
            pltpu.SMEM((2,), jnp.int32),
            pltpu.SemaphoreType.DMA((tiles,)),
            pltpu.SemaphoreType.DMA((tiles,)),
        ],
        compiler_params=params(48),
        cost_estimate=pl.CostEstimate(flops=6 << 30, bytes_accessed=20 << 20, transcendentals=4 << 20),
        name="prefix",
    )(lengths, base, got, k, v)


def combine_kernel(got_ref, own_hbm, own_lse_hbm, out_ref, own_ref, own_lse_ref, sems):
    loads = [
        pltpu.make_async_copy(own_lse_hbm, own_lse_ref, sems.at[0]),
        pltpu.make_async_copy(own_hbm, own_ref, sems.at[1]),
    ]
    for load in loads:
        load.start()
    x = got_ref[:, 256:272, :].reshape(256, 128).astype(F32)
    lse = (x + pltpu.roll(x, 112, 1)) + pltpu.roll(x, 96, 1)
    lse = lse.reshape(16, 16, 128)
    loads[0].wait()
    mine = own_lse_ref[...]
    lane = iota((16, 128), 1)
    lse = jnp.where((lane < 16)[None], lse, NEG)
    top = jnp.maximum(jnp.max(lse, axis=0), mine)
    w = jnp.exp2(lse - top[None])
    w_own = jnp.exp2(mine - top)
    total = jnp.sum(w, axis=0) + w_own
    w = w / total[None]
    w_own = w_own / total
    loads[1].wait()
    for h in range(16):
        rows = slice(h * 16, h * 16 + 16)
        o = jnp.sum(got_ref[:, rows, :].astype(F32) * w[:, :, h : h + 1], axis=0)
        o = (o + own_ref[rows, :] * w_own[:, h : h + 1]).astype(BF)
        for k in range(out_ref.shape[0]):
            out_ref[k, rows, :] = o


def combine(got, own_o, own_lse):
    return pl.pallas_call(
        combine_kernel,
        out_shape=jax.ShapeDtypeStruct((16, 256, 128), BF),
        in_specs=[VM, HB, HB],
        scratch_shapes=[
            pltpu.VMEM((256, 128), F32),
            pltpu.VMEM((16, 128), F32),
            pltpu.SemaphoreType.DMA((2,)),
        ],
        out_specs=VM,
        compiler_params=params(12),
        name="combine",
    )(got, own_o, own_lse)


def project_kernel(place_ref, x_ref, w_ref, keep_ref, give_ref, sums):
    total = None
    for h in range(0, 16, 2):
        a = x_ref[:, h * 16 : h * 16 + 16, :].reshape(256, 128)
        b = x_ref[:, h * 16 + 16 : h * 16 + 32, :].reshape(256, 128)
        part = mm_nt(jnp.concatenate([a, b], axis=1), w_ref[:, h * 128 : h * 128 + 256])
        total = part if total is None else total + part
    sums[...] = total
    place = place_ref[0]
    x, core = place // 2, place % 2
    for d in range(4):
        first = (x + d) % 4 * 2
        keep_ref[d] = sums[pl.ds(pl.multiple_of((first + core) * 32, 32), 32), :].astype(BF)
        give_ref[d] = sums[pl.ds(pl.multiple_of((first + 1 - core) * 32, 32), 32), :].astype(BF)


def project(place, x, w):
    shape = jax.ShapeDtypeStruct((4, 32, w.shape[0]), BF)
    return pl.pallas_call(
        project_kernel,
        out_shape=[shape, shape],
        in_specs=[SM, VM, VM],
        out_specs=[VM, VM],
        scratch_shapes=[pltpu.VMEM((256, w.shape[0]), F32)],
        compiler_params=params(12),
        name="project",
    )(place, x, w)


def pair_kernel(a_ref, b_ref, *out_refs):
    for d, out_ref in enumerate(out_refs):
        out_ref[...] = (a_ref[d].astype(F32) + b_ref[d].astype(F32)).astype(BF)


def pair(a, b):
    return pl.pallas_call(
        pair_kernel,
        out_shape=[jax.ShapeDtypeStruct(a.shape[1:], BF)] * 4,
        in_specs=[VM, VM],
        out_specs=[VM] * 4,
        compiler_params=params(4),
        name="pair",
    )(a, b)


def sum_heads(keep, give):
    other = lax.ppermute(give, "head", [(i, i // 2 * 2 + 1 - i % 2) for i in range(8)])
    parts = pair(keep, other)
    total = parts[0].astype(F32)
    for d in range(1, 4):
        moved = lax.ppermute(parts[d], "head", [(i, (i // 2 + d) % 4 * 2 + i % 2) for i in range(8)])
        total = total + moved.astype(F32)
    return total.astype(BF)


def body(
    queries,
    w_uk,
    w_uv,
    prefix_cache,
    suffix_cache,
    new_latent,
    w_out,
    request_prefix,
    prefix_lengths,
    suffix_len,
):
    scale = math.log2(math.e) / queries.shape[-1] ** 0.5
    wide = lax.axis_size("wide")
    tok = prefix_cache.shape[0]
    base = (lax.axis_index("wide") * tok).astype(jnp.int32).reshape(1)
    place = lax.axis_index("head").astype(jnp.int32).reshape(1)
    base, place = lax.optimization_barrier((base, place))
    packed = pack(request_prefix, queries.reshape(256, 192), wide)
    got = lax.all_to_all(packed, "wide", split_axis=0, concat_axis=0, tiled=True)
    k, v, own_o, own_lse = expand(
        prefix_cache, w_uk, w_uv, scale, suffix_len, packed, jnp.swapaxes(suffix_cache, 1, 2), new_latent
    )
    part = prefix(prefix_lengths, base, got, k, v)
    part = lax.all_to_all(part, "wide", split_axis=0, concat_axis=0, tiled=True)
    head_out = combine(part, own_o, own_lse)
    head_out = lax.all_to_all(head_out, "wide", split_axis=0, concat_axis=0, tiled=True)
    out = sum_heads(*project(place, head_out, w_out.T))
    return out.reshape(8, 4, w_out.shape[1])


def solution(mesh):
    in_specs = (
        P("wide", None, "head", None),
        P("head", None, None),
        P("head", None, None),
        P("wide", None),
        P("wide", None, None),
        P("wide", None, None),
        P("head", "wide"),
        P("wide"),
        P(),
        P("wide"),
    )
    out_specs = P("head", None, "wide")
    return jax.shard_map(body, mesh=mesh, in_specs=in_specs, out_specs=out_specs, check_vma=False)
```

```python
import functools
import math
import jax
import jax.numpy as jnp
from jax import lax
from jax.experimental import pallas as pl
from jax.experimental.pallas import tpu as pltpu
from jax.sharding import PartitionSpec as P

NEG = -1e30
BF = jnp.bfloat16
F32 = jnp.float32
NT = (((1,), (1,)), ((), ()))
MIB = 1024 * 1024
VM = pl.BlockSpec(memory_space=pltpu.VMEM)
SM = pl.BlockSpec(memory_space=pltpu.SMEM)
HB = pl.BlockSpec(memory_space=pltpu.HBM)
TILE = 256
CHUNK = 128


def mm(a, b):
    return jnp.dot(a, b, preferred_element_type=F32)


def mm_nt(a, b):
    return lax.dot_general(a, b, NT, preferred_element_type=F32)


def iota(shape, dim):
    return lax.broadcasted_iota(jnp.int32, shape, dim)


def params(mib):
    return pltpu.CompilerParams(vmem_limit_bytes=mib * MIB)


def pack_kernel(copies, ids_ref, q_ref, out_ref):
    rows = q_ref.shape[0]
    a, b = iota((rows, rows), 0), iota((rows, rows), 1)
    turn = jnp.where((a // 16 == b % 16) & (a % 16 == b // 16), 1.0, 0.0).astype(BF)
    y = mm(turn, q_ref[...]).astype(BF)
    half = rows // 2
    c, d = iota((192, 128), 0), iota((192, 128), 1)
    left = jnp.where((c - 128 == d), 1.0, 0.0).astype(BF)
    right = jnp.where((c - 128 == d - 64) & (c >= 128), 1.0, 0.0).astype(BF)
    rope = (mm(y[:half], left) + mm(y[half:], right)).astype(BF)
    which = iota((16, 128), 0) // 4
    ids = jnp.zeros((16, 128), jnp.int32)
    for r in range(4):
        ids = jnp.where(which == r, ids_ref[r], ids)
    ids = ids.astype(F32).astype(BF)
    nope = y[:, :128]
    for k in range(copies):
        out_ref[k, 0:rows, :] = nope
        out_ref[k, rows : rows + half, :] = rope
        out_ref[k, rows + half : rows + half + 16, :] = ids


def pack(ids, queries, copies):
    return pl.pallas_call(
        functools.partial(pack_kernel, copies),
        out_shape=jax.ShapeDtypeStruct((copies, 400, 128), BF),
        in_specs=[SM, VM],
        out_specs=VM,
        compiler_params=params(56),
        name="pack",
    )(ids, queries)


OWN_STEP = 5


def expand_kernel(
    scale, len_ref, q_ref, draft_ref, flip_ref, uk_ref, uv_ref, uk_hbm, uv_hbm, suf_hbm,
    k_ref, v_ref, o_ref, lse_ref,
    lat_ref, uk_own, uv_own, suf_ref, new_ref, ql, sc, sems,
):
    step = pl.program_id(0)
    uk_load = pltpu.make_async_copy(uk_hbm, uk_own, sems.at[0])
    suf_load = pltpu.make_async_copy(suf_hbm, suf_ref, sems.at[1])
    uv_load = pltpu.make_async_copy(uv_hbm, uv_own, sems.at[2])

    @pl.when(step == 0)
    def _():
        rope = (flip_ref[512:576, :].astype(F32) * scale).astype(BF)
        k_ref[...] = jnp.zeros(k_ref.shape, BF)
        for t in range(k_ref.shape[0]):
            here = slice(t * TILE, (t + 1) * TILE)
            k_ref[t, 0:64, :] = rope[:, here]
            k_ref[t, 192:256, :] = rope[:, here]
            lat_ref[here, :] = jnp.transpose(flip_ref[0:512, here])

    @pl.when(step == 1)
    def _():
        uk_load.start()
        suf_load.start()
        uv_load.start()

    def keys(first, last):
        wk = uk_ref[...].reshape(256, 512)
        for t in range(first, last):
            k_ref[t] = (mm(wk, flip_ref[0:512, t * TILE : (t + 1) * TILE]) * scale).astype(BF)

    def values(first, last):
        wv = jnp.concatenate([uv_ref[0], uv_ref[1]], axis=1)
        for t in range(first, last):
            here = slice(t * TILE, (t + 1) * TILE)
            v_ref[here, :] = mm(lat_ref[here, :], wv).astype(BF)

    tiles = k_ref.shape[0]

    @pl.when((step > 0) & (step != OWN_STEP))
    def _():
        keys(0, tiles)
        values(0, tiles)

    @pl.when(step == OWN_STEP)
    def _():
        uk_load.wait()
        suf_load.wait()
        uv_load.wait()
        for h in range(16):
            ql[h * 16 : h * 16 + 16, 0:512] = mm(q_ref[0, h * 16 : h * 16 + 16, :], uk_own[h]).astype(BF)
        keys(0, tiles // 4)
        c, d = iota((128, 64), 0), iota((128, 64), 1)
        first = jnp.where(c == d, 1.0, 0.0).astype(BF)
        second = jnp.where(c == d + 64, 1.0, 0.0).astype(BF)
        rope = q_ref[0, 256:384, :]
        ql[0:128, 512:576] = mm(rope, first).astype(BF)
        ql[128:256, 512:576] = mm(rope, second).astype(BF)
        q = ql[...]
        req = (iota((256, 1), 0) % 16) // 4
        top = jnp.full((256, 1), NEG, F32)
        for r in range(4):
            s = mm(q, suf_ref[r]) * scale
            ok = (req == r) & (iota((256, 512), 1) < len_ref[r])
            s = jnp.where(ok, s, NEG)
            sc[:, r * 512 : (r + 1) * 512] = s
            top = jnp.maximum(top, jnp.max(s, axis=1, keepdims=True))
            keys(tiles // 4 + r, tiles // 4 + r + 1)
        for r in range(4):
            new_ref[r * 4 : r * 4 + 4, :] = draft_ref[r].astype(F32)
        new = new_ref[...].astype(BF)
        s = mm_nt(q, new) * scale
        row, col = iota((256, 16), 0) % 16, iota((256, 16), 1)
        ok = (row // 4 == col // 4) & (col % 4 <= row % 4)
        s = jnp.where(ok, s, NEG)
        top = jnp.maximum(top, jnp.max(s, axis=1, keepdims=True))
        keys(tiles // 4 + 4, tiles)
        p = jnp.exp2(s - top)
        total = jnp.sum(p, axis=1, keepdims=True)
        o = mm(p.astype(BF), new[:, 0:512])
        for r in range(4):
            p = jnp.exp2(sc[:, r * 512 : (r + 1) * 512] - top)
            total = total + jnp.sum(p, axis=1, keepdims=True)
            o = o + mm_nt(p.astype(BF), suf_ref[r, 0:512, :])
            values(r, r + 1)
        o = (o / total).astype(BF)
        lse = top + jnp.log2(total)
        values(4, tiles)
        lane = iota((16, 128), 1)
        packed = jnp.zeros((16, 128), F32)
        for h in range(16):
            o_ref[h * 16 : h * 16 + 16, :] = mm(o[h * 16 : h * 16 + 16], uv_own[h])
            packed = jnp.where(lane == h, lse[h * 16 : h * 16 + 16], packed)
        lse_ref[...] = packed


def expand(cache, w_uk, w_uv, scale, suffix_len, packed, suffix, draft):
    tok = cache.shape[0]
    return pl.pallas_call(
        functools.partial(expand_kernel, scale),
        grid=(9,),
        out_shape=[
            jax.ShapeDtypeStruct((tok // TILE, 2304, TILE), BF),
            jax.ShapeDtypeStruct((tok, 2048), BF),
            jax.ShapeDtypeStruct((256, 128), F32),
            jax.ShapeDtypeStruct((16, 128), F32),
        ],
        in_specs=[
            SM,
            pl.BlockSpec((1, 400, 128), lambda g: (0, 0, 0)),
            pl.BlockSpec((4, 4, 576), lambda g: (0, 0, 0)),
            pl.BlockSpec((576, tok), lambda g: (0, 0)),
            pl.BlockSpec((2, 128, 512), lambda g: (jnp.maximum(g - 1, 0), 0, 0)),
            pl.BlockSpec((2, 512, 128), lambda g: (jnp.maximum(g - 1, 0), 0, 0)),
            HB,
            HB,
            HB,
        ],
        out_specs=[
            pl.BlockSpec((tok // TILE, 256, TILE), lambda g: (0, g, 0)),
            pl.BlockSpec((tok, 256), lambda g: (0, jnp.maximum(g - 1, 0))),
            pl.BlockSpec((256, 128), lambda g: (0, 0)),
            pl.BlockSpec((16, 128), lambda g: (0, 0)),
        ],
        scratch_shapes=[
            pltpu.VMEM((tok, 512), BF),
            pltpu.VMEM(w_uk.shape, BF),
            pltpu.VMEM(w_uv.shape, BF),
            pltpu.VMEM(suffix.shape, BF),
            pltpu.VMEM((16, 576), F32),
            pltpu.VMEM((256, 576), BF),
            pltpu.VMEM((256, 2048), F32),
            pltpu.SemaphoreType.DMA((3,)),
        ],
        compiler_params=params(56),
        cost_estimate=pl.CostEstimate(
            flops=2 * 2 * tok * 512 * 2048 + (3 << 30), bytes_accessed=31 << 20, transcendentals=1 << 19
        ),
        name="expand",
    )(suffix_len, packed, draft, cache.T, w_uk, w_uv, w_uk, w_uv, suffix)


def prefix_kernel(
    len_ref, base_ref, q_ref, k_hbm, v_hbm, out_ref,
    kbuf, vbuf, qs, sc, best, acc, osc, lsc, slots, bias, row_low, row_high,
    low_ref, high_ref, start_ref, seen, ksems, vsems,
):
    tok, tiles = vbuf.shape[0], kbuf.shape[0]

    def load_k(t):
        return pltpu.make_async_copy(k_hbm.at[t], kbuf.at[t], ksems.at[t])

    def load_v(t):
        here = pl.ds(t * TILE, TILE)
        return pltpu.make_async_copy(v_hbm.at[here, :], vbuf.at[here, :], vsems.at[t])

    for t in range(tiles):
        load_k(t).start()
    seen[0] = 0
    seen[1] = 0

    def arrive(t, which, load):
        def one(i, _):
            load(i).wait()
            return 0

        lax.fori_loop(seen[which], t + 1, one, 0)
        seen[which] = jnp.maximum(seen[which], t + 1)

    ids = q_ref[:, 384:400, :].reshape(256, 128).astype(F32)
    index = iota((256, 128), 0).astype(F32)
    flat = jnp.transpose(ids)[0:8, :]
    key = index + 8192.0
    shift = jnp.full((256, 128), 0.0, F32)
    begin = jnp.int32(0) - base_ref[0]
    zero = jnp.int32(0)
    rows_before, units, slot, room_left = zero, zero, zero, zero
    lows, highs = [], []
    for p in range(8):
        end = begin + len_ref[p]
        low, high = jnp.maximum(begin, 0), jnp.minimum(end, tok)
        lows.append(low)
        highs.append(high)
        begin = end
        rows = jnp.sum(jnp.where(flat[0:1, :] == float(p), 1.0, 0.0)).astype(jnp.int32)
        rows = jnp.where(high > low, rows, 0)
        hit = (ids == float(p)) & (rows > 0)
        key = jnp.where(hit, index + float(p * 256), key)
        shift = jnp.where(hit, (slot - rows_before).astype(F32), shift)
        padded = (rows + 15) // 16 * 16
        joins = padded <= room_left
        more = jnp.where(joins, 0, (rows + (CHUNK - 1)) // CHUNK)

        @pl.when(joins & (rows > 0))
        def _():
            high_ref[units - 1] = high

        for c in range(256 // CHUNK):
            @pl.when(c < more)
            def _():
                low_ref[units + c] = low
                high_ref[units + c] = high
                start_ref[units + c] = slot + c * CHUNK
        units = units + more
        room_left = jnp.where(joins, room_left, more * CHUNK) - padded
        slot = slot + padded
        rows_before = rows_before + rows
    blocks = (slot + (CHUNK - 1)) // CHUNK

    across = jnp.transpose(key)[0:1, :]
    rank = jnp.sum(jnp.where(across < key[:, 0:1], 1.0, 0.0), axis=1, keepdims=True)
    mine = jnp.where(key < 8192.0, rank + shift, -1.0)
    slots[...] = mine
    across = jnp.transpose(mine)[0:1, :]
    osc[...] = jnp.zeros(osc.shape, BF)
    lsc[...] = jnp.zeros(lsc.shape, F32)

    def gather(b, _):
        rows = pl.ds(pl.multiple_of(b * CHUNK, CHUNK), CHUNK)
        want = (iota((CHUNK, 256), 0) + b * CHUNK).astype(F32)
        pick = jnp.where(across == want, 1.0, 0.0).astype(BF)
        which = mm(pick, (ids + 1.0).astype(BF))
        low = jnp.zeros((CHUNK, 128), jnp.int32)
        high = jnp.zeros((CHUNK, 128), jnp.int32)
        for p in range(8):
            low = jnp.where(which == p + 1.0, lows[p], low)
            high = jnp.where(which == p + 1.0, highs[p], high)
        row_low[rows, :] = low
        row_high[rows, :] = high
        for h in range(0, 24, 2):
            pair = [q_ref[:, g * 16 : g * 16 + 16, :].reshape(256, 128) for g in (h, h + 1)]
            both = mm(pick, jnp.concatenate(pair, axis=1)).astype(BF)
            for g in (0, 1):
                part = both[:, g * 128 : g * 128 + 128]
                if h < 16:
                    qs[h + g, rows, 0:128] = part
                else:
                    qs[h + g - 16, rows, 128:256] = part
                    qs[h + g - 8, rows, 128:256] = part
        return 0

    lax.fori_loop(0, blocks, gather, 0)
    rest = pl.ds(pl.multiple_of(blocks * CHUNK, CHUNK), CHUNK)
    qs[:, rest, :] = jnp.zeros((16, CHUNK, 256), BF)
    row_low[rest, :] = jnp.zeros((CHUNK, 128), jnp.int32)
    row_high[rest, :] = jnp.zeros((CHUNK, 128), jnp.int32)

    def unit(u, _):
        low, high = low_ref[u], high_ref[u]
        rows = pl.ds(pl.multiple_of(start_ref[u], 16), CHUNK)
        first, last = low // TILE, (high + (TILE - 1)) // TILE
        best[...] = jnp.full(best.shape, NEG, F32)

        def score(t, _):
            arrive(t, 0, load_k)
            pos = iota((CHUNK, TILE), 1) + t * TILE
            row_from = jnp.concatenate([row_low[rows, :]] * (TILE // 128), axis=1)
            row_to = jnp.concatenate([row_high[rows, :]] * (TILE // 128), axis=1)
            bias[...] = jnp.where((pos >= row_from) & (pos < row_to), 0.0, NEG)
            for h in range(16):
                side = slice(0, 128) if h < 8 else slice(128, 256)
                key = jnp.concatenate([kbuf[t, h * 128 + 256 : h * 128 + 384, :], kbuf[t, side, :]], axis=0)
                s = mm(qs[h, rows, :], key) + bias[...]
                sc[t, h] = s
                top = best[h]
                for v in range(0, TILE, 128):
                    top = jnp.maximum(top, s[:, v : v + 128])
                best[h] = top
            return 0

        lax.fori_loop(first, last, score, 0)

        for h in range(16):
            best[h] = jnp.broadcast_to(jnp.max(best[h], axis=1, keepdims=True), (CHUNK, 128))
        acc[...] = jnp.zeros(acc.shape, F32)

        def weigh(t, _):
            ones = jnp.ones((TILE, 128), BF)
            arrive(t, 1, load_v)
            here = pl.ds(pl.multiple_of(t * TILE, TILE), TILE)
            for h in range(16):
                top = best[h]
                p = jnp.exp2(sc[t, h] - jnp.concatenate([top] * (TILE // 128), axis=1))
                value = jnp.concatenate([vbuf[here, h * 128 : h * 128 + 128], ones], axis=1)
                acc[h] += mm(p.astype(BF), value)
            return 0

        lax.fori_loop(first, last, weigh, 0)
        lane = iota((CHUNK, 128), 1)
        lse = jnp.zeros((CHUNK, 128), F32)
        for h in range(16):
            full = acc[h, :, 128:256]
            osc[h, rows, :] = (acc[h, :, 0:128] / full).astype(BF)
            lse = jnp.where(lane == h, best[h] + jnp.log2(full), lse)
        lsc[rows, :] = lse
        return 0

    for t in range(tiles):
        load_v(t).start()
    lax.fori_loop(0, units, unit, 0)
    arrive(tiles - 1, 0, load_k)
    arrive(tiles - 1, 1, load_v)

    lane = iota((256, 128), 1)
    ok = slots[...] >= 0.0
    empty = jnp.where((lane < 16) & ~ok, NEG, 0.0).astype(BF)
    out_ref[:, 0:256, :] = jnp.zeros((16, 256, 128), BF)
    out_ref[:, 256:272, :] = empty.reshape(16, 16, 128)

    def scatter(b, _):
        rows = pl.ds(pl.multiple_of(b * CHUNK, CHUNK), CHUNK)
        back = jnp.where(slots[...] == (lane + b * CHUNK).astype(F32), 1.0, 0.0).astype(BF)
        for h in range(0, 16, 2):
            both = mm(back, jnp.concatenate([osc[h, rows, :], osc[h + 1, rows, :]], axis=1))
            for g in (0, 1):
                here = slice((h + g) * 16, (h + g) * 16 + 16)
                part = both[:, g * 128 : g * 128 + 128].reshape(16, 16, 128)
                out_ref[:, here, :] = (out_ref[:, here, :].astype(F32) + part).astype(BF)
        lse = lsc[rows, :]
        hi = lse.astype(BF)
        rest = lse - hi.astype(F32)
        mid = rest.astype(BF)
        lo = (rest - mid.astype(F32)).astype(BF)
        merged = hi.astype(F32) + pltpu.roll(mid.astype(F32), 16, 1) + pltpu.roll(lo.astype(F32), 32, 1)
        part = mm(back, merged.astype(BF)).reshape(16, 16, 128)
        out_ref[:, 256:272, :] = (out_ref[:, 256:272, :].astype(F32) + part).astype(BF)
        return 0

    lax.fori_loop(0, blocks, scatter, 0)


def prefix(lengths, base, got, k, v):
    tiles, tok = k.shape[0], v.shape[0]
    room = 384 + CHUNK
    return pl.pallas_call(
        prefix_kernel,
        out_shape=jax.ShapeDtypeStruct((16, 272, 128), BF),
        in_specs=[SM, SM, VM, HB, HB],
        out_specs=VM,
        scratch_shapes=[
            pltpu.VMEM(k.shape, BF),
            pltpu.VMEM(v.shape, BF),
            pltpu.VMEM((16, room, 256), BF),
            pltpu.VMEM((tiles, 16, CHUNK, TILE), F32),
            pltpu.VMEM((16, CHUNK, 128), F32),
            pltpu.VMEM((16, CHUNK, 256), F32),
            pltpu.VMEM((16, room, 128), BF),
            pltpu.VMEM((room, 128), F32),
            pltpu.VMEM((256, 128), F32),
            pltpu.VMEM((CHUNK, TILE), F32),
            pltpu.VMEM((room, 128), jnp.int32),
            pltpu.VMEM((room, 128), jnp.int32),
            pltpu.SMEM((16,), jnp.int32),
            pltpu.SMEM((16,), jnp.int32),
            pltpu.SMEM((16,), jnp.int32),
            pltpu.SMEM((2,), jnp.int32),
            pltpu.SemaphoreType.DMA((tiles,)),
            pltpu.SemaphoreType.DMA((tiles,)),
        ],
        compiler_params=params(48),
        cost_estimate=pl.CostEstimate(flops=6 << 30, bytes_accessed=20 << 20, transcendentals=4 << 20),
        name="prefix",
    )(lengths, base, got, k, v)


def combine_kernel(got_ref, own_hbm, own_lse_hbm, out_ref, own_ref, own_lse_ref, sems):
    loads = [
        pltpu.make_async_copy(own_lse_hbm, own_lse_ref, sems.at[0]),
        pltpu.make_async_copy(own_hbm, own_ref, sems.at[1]),
    ]
    for load in loads:
        load.start()
    x = got_ref[:, 256:272, :].reshape(256, 128).astype(F32)
    lse = (x + pltpu.roll(x, 112, 1)) + pltpu.roll(x, 96, 1)
    lse = lse.reshape(16, 16, 128)
    loads[0].wait()
    mine = own_lse_ref[...]
    lane = iota((16, 128), 1)
    lse = jnp.where((lane < 16)[None], lse, NEG)
    top = jnp.maximum(jnp.max(lse, axis=0), mine)
    w = jnp.exp2(lse - top[None])
    w_own = jnp.exp2(mine - top)
    total = jnp.sum(w, axis=0) + w_own
    w = w / total[None]
    w_own = w_own / total
    loads[1].wait()
    for h in range(16):
        rows = slice(h * 16, h * 16 + 16)
        o = jnp.sum(got_ref[:, rows, :].astype(F32) * w[:, :, h : h + 1], axis=0)
        o = (o + own_ref[rows, :] * w_own[:, h : h + 1]).astype(BF)
        for k in range(out_ref.shape[0]):
            out_ref[k, rows, :] = o


def combine(got, own_o, own_lse):
    return pl.pallas_call(
        combine_kernel,
        out_shape=jax.ShapeDtypeStruct((16, 256, 128), BF),
        in_specs=[VM, HB, HB],
        scratch_shapes=[
            pltpu.VMEM((256, 128), F32),
            pltpu.VMEM((16, 128), F32),
            pltpu.SemaphoreType.DMA((2,)),
        ],
        out_specs=VM,
        compiler_params=params(12),
        name="combine",
    )(got, own_o, own_lse)


def project_kernel(place_ref, x_ref, w_ref, keep_ref, give_ref, sums):
    total = None
    for h in range(0, 16, 2):
        a = x_ref[:, h * 16 : h * 16 + 16, :].reshape(256, 128)
        b = x_ref[:, h * 16 + 16 : h * 16 + 32, :].reshape(256, 128)
        part = mm_nt(jnp.concatenate([a, b], axis=1), w_ref[:, h * 128 : h * 128 + 256])
        total = part if total is None else total + part
    sums[...] = total
    place = place_ref[0]
    x, core = place // 2, place % 2
    for d in range(4):
        first = (x + d) % 4 * 2
        keep_ref[d] = sums[pl.ds(pl.multiple_of((first + core) * 32, 32), 32), :].astype(BF)
        give_ref[d] = sums[pl.ds(pl.multiple_of((first + 1 - core) * 32, 32), 32), :].astype(BF)


def project(place, x, w):
    shape = jax.ShapeDtypeStruct((4, 32, w.shape[0]), BF)
    return pl.pallas_call(
        project_kernel,
        out_shape=[shape, shape],
        in_specs=[SM, VM, VM],
        out_specs=[VM, VM],
        scratch_shapes=[pltpu.VMEM((256, w.shape[0]), F32)],
        compiler_params=params(12),
        name="project",
    )(place, x, w)


def pair_kernel(a_ref, b_ref, *out_refs):
    for d, out_ref in enumerate(out_refs):
        out_ref[...] = (a_ref[d].astype(F32) + b_ref[d].astype(F32)).astype(BF)


def pair(a, b):
    return pl.pallas_call(
        pair_kernel,
        out_shape=[jax.ShapeDtypeStruct(a.shape[1:], BF)] * 4,
        in_specs=[VM, VM],
        out_specs=[VM] * 4,
        compiler_params=params(4),
        name="pair",
    )(a, b)


def last_kernel(a_ref, b_ref, c_ref, d_ref, out_ref):
    total = (a_ref[...].astype(F32) + b_ref[...].astype(F32)) + (c_ref[...].astype(F32) + d_ref[...].astype(F32))
    for r in range(8):
        out_ref[r] = total[r * 4 : r * 4 + 4, :].astype(BF)


def last_sum(*parts):
    return pl.pallas_call(
        last_kernel,
        out_shape=jax.ShapeDtypeStruct((8, 4, parts[0].shape[1]), BF),
        in_specs=[VM] * 4,
        out_specs=VM,
        compiler_params=params(4),
        name="last_sum",
    )(*parts)


def sum_heads(keep, give):
    other = lax.ppermute(give, "head", [(i, i // 2 * 2 + 1 - i % 2) for i in range(8)])
    parts = pair(keep, other)
    moved = [
        lax.ppermute(parts[d], "head", [(i, (i // 2 + d) % 4 * 2 + i % 2) for i in range(8)]) for d in (1, 2, 3)
    ]
    return last_sum(parts[0], *moved)


def body(
    queries,
    w_uk,
    w_uv,
    prefix_cache,
    suffix_cache,
    new_latent,
    w_out,
    request_prefix,
    prefix_lengths,
    suffix_len,
):
    scale = math.log2(math.e) / queries.shape[-1] ** 0.5
    wide = lax.axis_size("wide")
    tok = prefix_cache.shape[0]
    base = (lax.axis_index("wide") * tok).astype(jnp.int32).reshape(1)
    place = lax.axis_index("head").astype(jnp.int32).reshape(1)
    base, place = lax.optimization_barrier((base, place))
    packed = pack(request_prefix, queries.reshape(256, 192), wide)
    got = lax.all_to_all(packed, "wide", split_axis=0, concat_axis=0, tiled=True)
    k, v, own_o, own_lse = expand(
        prefix_cache, w_uk, w_uv, scale, suffix_len, packed, jnp.swapaxes(suffix_cache, 1, 2), new_latent
    )
    part = prefix(prefix_lengths, base, got, k, v)
    part = lax.all_to_all(part, "wide", split_axis=0, concat_axis=0, tiled=True)
    head_out = combine(part, own_o, own_lse)
    head_out = lax.all_to_all(head_out, "wide", split_axis=0, concat_axis=0, tiled=True)
    out = sum_heads(*project(place, head_out, w_out.T))
    return out


def solution(mesh):
    in_specs = (
        P("wide", None, "head", None),
        P("head", None, None),
        P("head", None, None),
        P("wide", None),
        P("wide", None, None),
        P("wide", None, None),
        P("head", "wide"),
        P("wide"),
        P(),
        P("wide"),
    )
    out_specs = P("head", None, "wide")
    return jax.shard_map(body, mesh=mesh, in_specs=in_specs, out_specs=out_specs, check_vma=False)
```

```python
import functools
import math
import jax
import jax.numpy as jnp
from jax import lax
from jax.experimental import pallas as pl
from jax.experimental.pallas import tpu as pltpu
from jax.sharding import PartitionSpec as P

NEG = -1e30
BF = jnp.bfloat16
F32 = jnp.float32
NT = (((1,), (1,)), ((), ()))
MIB = 1024 * 1024
VM = pl.BlockSpec(memory_space=pltpu.VMEM)
SM = pl.BlockSpec(memory_space=pltpu.SMEM)
HB = pl.BlockSpec(memory_space=pltpu.HBM)
TILE = 256
CHUNK = 128


def mm(a, b):
    return jnp.dot(a, b, preferred_element_type=F32)


def mm_nt(a, b):
    return lax.dot_general(a, b, NT, preferred_element_type=F32)


def iota(shape, dim):
    return lax.broadcasted_iota(jnp.int32, shape, dim)


def params(mib):
    return pltpu.CompilerParams(vmem_limit_bytes=mib * MIB)


def pack_kernel(copies, ids_ref, q_ref, out_hbm, block, sems):
    rows = q_ref.shape[0]
    half = rows // 2

    def send(first, last, sem):
        sent = [
            pltpu.make_async_copy(block.at[first:last], out_hbm.at[k, first:last], sem.at[k]) for k in range(copies)
        ]
        for copy in sent:
            copy.start()
        return sent

    a, b = iota((rows, rows), 0), iota((rows, rows), 1)
    turn = jnp.where((a // 16 == b % 16) & (a % 16 == b // 16), 1.0, 0.0).astype(BF)
    y = mm(turn, q_ref[...]).astype(BF)
    block[0:rows, :] = y[:, :128]
    sent = send(0, rows, sems.at[0])
    c, d = iota((192, 128), 0), iota((192, 128), 1)
    left = jnp.where((c - 128 == d), 1.0, 0.0).astype(BF)
    right = jnp.where((c - 128 == d - 64) & (c >= 128), 1.0, 0.0).astype(BF)
    block[rows : rows + half, :] = (mm(y[:half], left) + mm(y[half:], right)).astype(BF)
    which = iota((16, 128), 0) // 4
    ids = jnp.zeros((16, 128), jnp.int32)
    for r in range(4):
        ids = jnp.where(which == r, ids_ref[r], ids)
    block[rows + half : rows + half + 16, :] = ids.astype(F32).astype(BF)
    sent += send(rows, rows + half + 16, sems.at[1])
    for copy in sent:
        copy.wait()


def pack(ids, queries, copies):
    return pl.pallas_call(
        functools.partial(pack_kernel, copies),
        out_shape=jax.ShapeDtypeStruct((copies, 400, 128), BF),
        in_specs=[SM, VM],
        out_specs=HB,
        scratch_shapes=[pltpu.VMEM((400, 128), BF), pltpu.SemaphoreType.DMA((2, copies))],
        compiler_params=params(56),
        name="pack",
    )(ids, queries)


OWN_STEP = 5


def expand_kernel(
    scale, len_ref, q_ref, draft_ref, flip_ref, uk_ref, uv_ref, uk_hbm, uv_hbm, suf_hbm,
    k_ref, v_ref, o_ref, lse_ref,
    lat_ref, uk_own, uv_own, suf_ref, new_ref, ql, sc, sems,
):
    step = pl.program_id(0)
    uk_load = pltpu.make_async_copy(uk_hbm, uk_own, sems.at[0])
    suf_load = pltpu.make_async_copy(suf_hbm, suf_ref, sems.at[1])
    uv_load = pltpu.make_async_copy(uv_hbm, uv_own, sems.at[2])

    @pl.when(step == 0)
    def _():
        rope = (flip_ref[512:576, :].astype(F32) * scale).astype(BF)
        k_ref[...] = jnp.zeros(k_ref.shape, BF)
        for t in range(k_ref.shape[0]):
            here = slice(t * TILE, (t + 1) * TILE)
            k_ref[t, 0:64, :] = rope[:, here]
            k_ref[t, 192:256, :] = rope[:, here]
            lat_ref[here, :] = jnp.transpose(flip_ref[0:512, here])

    @pl.when(step == 1)
    def _():
        uk_load.start()
        suf_load.start()
        uv_load.start()

    def keys(first, last):
        wk = uk_ref[...].reshape(256, 512)
        for t in range(first, last):
            k_ref[t] = (mm(wk, flip_ref[0:512, t * TILE : (t + 1) * TILE]) * scale).astype(BF)

    def values(first, last):
        wv = jnp.concatenate([uv_ref[0], uv_ref[1]], axis=1)
        for t in range(first, last):
            here = slice(t * TILE, (t + 1) * TILE)
            v_ref[here, :] = mm(lat_ref[here, :], wv).astype(BF)

    tiles = k_ref.shape[0]

    @pl.when((step > 0) & (step != OWN_STEP))
    def _():
        keys(0, tiles)
        values(0, tiles)

    @pl.when(step == OWN_STEP)
    def _():
        uk_load.wait()
        suf_load.wait()
        uv_load.wait()
        for h in range(16):
            ql[h * 16 : h * 16 + 16, 0:512] = mm(q_ref[0, h * 16 : h * 16 + 16, :], uk_own[h]).astype(BF)
        keys(0, tiles // 4)
        c, d = iota((128, 64), 0), iota((128, 64), 1)
        first = jnp.where(c == d, 1.0, 0.0).astype(BF)
        second = jnp.where(c == d + 64, 1.0, 0.0).astype(BF)
        rope = q_ref[0, 256:384, :]
        ql[0:128, 512:576] = mm(rope, first).astype(BF)
        ql[128:256, 512:576] = mm(rope, second).astype(BF)
        q = ql[...]
        req = (iota((256, 1), 0) % 16) // 4
        top = jnp.full((256, 1), NEG, F32)
        for r in range(4):
            s = mm(q, suf_ref[r]) * scale
            ok = (req == r) & (iota((256, 512), 1) < len_ref[r])
            s = jnp.where(ok, s, NEG)
            sc[:, r * 512 : (r + 1) * 512] = s
            top = jnp.maximum(top, jnp.max(s, axis=1, keepdims=True))
            keys(tiles // 4 + r, tiles // 4 + r + 1)
        for r in range(4):
            new_ref[r * 4 : r * 4 + 4, :] = draft_ref[r].astype(F32)
        new = new_ref[...].astype(BF)
        s = mm_nt(q, new) * scale
        row, col = iota((256, 16), 0) % 16, iota((256, 16), 1)
        ok = (row // 4 == col // 4) & (col % 4 <= row % 4)
        s = jnp.where(ok, s, NEG)
        top = jnp.maximum(top, jnp.max(s, axis=1, keepdims=True))
        keys(tiles // 4 + 4, tiles)
        p = jnp.exp2(s - top)
        total = jnp.sum(p, axis=1, keepdims=True)
        o = mm(p.astype(BF), new[:, 0:512])
        for r in range(4):
            p = jnp.exp2(sc[:, r * 512 : (r + 1) * 512] - top)
            total = total + jnp.sum(p, axis=1, keepdims=True)
            o = o + mm_nt(p.astype(BF), suf_ref[r, 0:512, :])
            values(r, r + 1)
        o = (o / total).astype(BF)
        lse = top + jnp.log2(total)
        values(4, tiles)
        lane = iota((16, 128), 1)
        packed = jnp.zeros((16, 128), F32)
        for h in range(16):
            o_ref[h * 16 : h * 16 + 16, :] = mm(o[h * 16 : h * 16 + 16], uv_own[h])
            packed = jnp.where(lane == h, lse[h * 16 : h * 16 + 16], packed)
        lse_ref[...] = packed


def expand(cache, w_uk, w_uv, scale, suffix_len, packed, suffix, draft):
    tok = cache.shape[0]
    return pl.pallas_call(
        functools.partial(expand_kernel, scale),
        grid=(9,),
        out_shape=[
            jax.ShapeDtypeStruct((tok // TILE, 2304, TILE), BF),
            jax.ShapeDtypeStruct((tok, 2048), BF),
            jax.ShapeDtypeStruct((256, 128), F32),
            jax.ShapeDtypeStruct((16, 128), F32),
        ],
        in_specs=[
            SM,
            pl.BlockSpec((1, 400, 128), lambda g: (0, 0, 0)),
            pl.BlockSpec((4, 4, 576), lambda g: (0, 0, 0)),
            pl.BlockSpec((576, tok), lambda g: (0, 0)),
            pl.BlockSpec((2, 128, 512), lambda g: (jnp.maximum(g - 1, 0), 0, 0)),
            pl.BlockSpec((2, 512, 128), lambda g: (jnp.maximum(g - 1, 0), 0, 0)),
            HB,
            HB,
            HB,
        ],
        out_specs=[
            pl.BlockSpec((tok // TILE, 256, TILE), lambda g: (0, g, 0)),
            pl.BlockSpec((tok, 256), lambda g: (0, jnp.maximum(g - 1, 0))),
            pl.BlockSpec((256, 128), lambda g: (0, 0)),
            pl.BlockSpec((16, 128), lambda g: (0, 0)),
        ],
        scratch_shapes=[
            pltpu.VMEM((tok, 512), BF),
            pltpu.VMEM(w_uk.shape, BF),
            pltpu.VMEM(w_uv.shape, BF),
            pltpu.VMEM(suffix.shape, BF),
            pltpu.VMEM((16, 576), F32),
            pltpu.VMEM((256, 576), BF),
            pltpu.VMEM((256, 2048), F32),
            pltpu.SemaphoreType.DMA((3,)),
        ],
        compiler_params=params(56),
        cost_estimate=pl.CostEstimate(
            flops=2 * 2 * tok * 512 * 2048 + (3 << 30), bytes_accessed=31 << 20, transcendentals=1 << 19
        ),
        name="expand",
    )(suffix_len, packed, draft, cache.T, w_uk, w_uv, w_uk, w_uv, suffix)


def prefix_kernel(
    len_ref, base_ref, q_ref, k_hbm, v_hbm, out_ref,
    kbuf, vbuf, qs, sc, best, acc, osc, lsc, slots, bias, row_low, row_high,
    low_ref, high_ref, start_ref, seen, ksems, vsems,
):
    tok, tiles = vbuf.shape[0], kbuf.shape[0]

    def load_k(t):
        return pltpu.make_async_copy(k_hbm.at[t], kbuf.at[t], ksems.at[t])

    def load_v(t):
        here = pl.ds(t * TILE, TILE)
        return pltpu.make_async_copy(v_hbm.at[here, :], vbuf.at[here, :], vsems.at[t])

    for t in range(tiles):
        load_k(t).start()
    seen[0] = 0
    seen[1] = 0

    def arrive(t, which, load):
        def one(i, _):
            load(i).wait()
            return 0

        lax.fori_loop(seen[which], t + 1, one, 0)
        seen[which] = jnp.maximum(seen[which], t + 1)

    ids = q_ref[:, 384:400, :].reshape(256, 128).astype(F32)
    index = iota((256, 128), 0).astype(F32)
    flat = jnp.transpose(ids)[0:8, :]
    key = index + 8192.0
    shift = jnp.full((256, 128), 0.0, F32)
    begin = jnp.int32(0) - base_ref[0]
    zero = jnp.int32(0)
    rows_before, units, slot, room_left = zero, zero, zero, zero
    lows, highs = [], []
    for p in range(8):
        end = begin + len_ref[p]
        low, high = jnp.maximum(begin, 0), jnp.minimum(end, tok)
        lows.append(low)
        highs.append(high)
        begin = end
        rows = jnp.sum(jnp.where(flat[0:1, :] == float(p), 1.0, 0.0)).astype(jnp.int32)
        rows = jnp.where(high > low, rows, 0)
        hit = (ids == float(p)) & (rows > 0)
        key = jnp.where(hit, index + float(p * 256), key)
        shift = jnp.where(hit, (slot - rows_before).astype(F32), shift)
        padded = (rows + 15) // 16 * 16
        joins = padded <= room_left
        more = jnp.where(joins, 0, (rows + (CHUNK - 1)) // CHUNK)

        @pl.when(joins & (rows > 0))
        def _():
            high_ref[units - 1] = high

        for c in range(256 // CHUNK):
            @pl.when(c < more)
            def _():
                low_ref[units + c] = low
                high_ref[units + c] = high
                start_ref[units + c] = slot + c * CHUNK
        units = units + more
        room_left = jnp.where(joins, room_left, more * CHUNK) - padded
        slot = slot + padded
        rows_before = rows_before + rows
    blocks = (slot + (CHUNK - 1)) // CHUNK

    across = jnp.transpose(key)[0:1, :]
    rank = jnp.sum(jnp.where(across < key[:, 0:1], 1.0, 0.0), axis=1, keepdims=True)
    mine = jnp.where(key < 8192.0, rank + shift, -1.0)
    slots[...] = mine
    across = jnp.transpose(mine)[0:1, :]
    osc[...] = jnp.zeros(osc.shape, BF)
    lsc[...] = jnp.zeros(lsc.shape, F32)

    def gather(b, _):
        rows = pl.ds(pl.multiple_of(b * CHUNK, CHUNK), CHUNK)
        want = (iota((CHUNK, 256), 0) + b * CHUNK).astype(F32)
        pick = jnp.where(across == want, 1.0, 0.0).astype(BF)
        which = mm(pick, (ids + 1.0).astype(BF))
        low = jnp.zeros((CHUNK, 128), jnp.int32)
        high = jnp.zeros((CHUNK, 128), jnp.int32)
        for p in range(8):
            low = jnp.where(which == p + 1.0, lows[p], low)
            high = jnp.where(which == p + 1.0, highs[p], high)
        row_low[rows, :] = low
        row_high[rows, :] = high
        for h in range(0, 24, 2):
            pair = [q_ref[:, g * 16 : g * 16 + 16, :].reshape(256, 128) for g in (h, h + 1)]
            both = mm(pick, jnp.concatenate(pair, axis=1)).astype(BF)
            for g in (0, 1):
                part = both[:, g * 128 : g * 128 + 128]
                if h < 16:
                    qs[h + g, rows, 0:128] = part
                else:
                    qs[h + g - 16, rows, 128:256] = part
                    qs[h + g - 8, rows, 128:256] = part
        return 0

    lax.fori_loop(0, blocks, gather, 0)
    rest = pl.ds(pl.multiple_of(blocks * CHUNK, CHUNK), CHUNK)
    qs[:, rest, :] = jnp.zeros((16, CHUNK, 256), BF)
    row_low[rest, :] = jnp.zeros((CHUNK, 128), jnp.int32)
    row_high[rest, :] = jnp.zeros((CHUNK, 128), jnp.int32)

    def unit(u, _):
        low, high = low_ref[u], high_ref[u]
        rows = pl.ds(pl.multiple_of(start_ref[u], 16), CHUNK)
        first, last = low // TILE, (high + (TILE - 1)) // TILE
        best[...] = jnp.full(best.shape, NEG, F32)

        def score(t, _):
            arrive(t, 0, load_k)
            pos = iota((CHUNK, TILE), 1) + t * TILE
            row_from = jnp.concatenate([row_low[rows, :]] * (TILE // 128), axis=1)
            row_to = jnp.concatenate([row_high[rows, :]] * (TILE // 128), axis=1)
            bias[...] = jnp.where((pos >= row_from) & (pos < row_to), 0.0, NEG)
            for h in range(16):
                side = slice(0, 128) if h < 8 else slice(128, 256)
                key = jnp.concatenate([kbuf[t, h * 128 + 256 : h * 128 + 384, :], kbuf[t, side, :]], axis=0)
                s = mm(qs[h, rows, :], key) + bias[...]
                sc[t, h] = s
                top = best[h]
                for v in range(0, TILE, 128):
                    top = jnp.maximum(top, s[:, v : v + 128])
                best[h] = top
            return 0

        lax.fori_loop(first, last, score, 0)

        for h in range(16):
            best[h] = jnp.broadcast_to(jnp.max(best[h], axis=1, keepdims=True), (CHUNK, 128))
        acc[...] = jnp.zeros(acc.shape, F32)

        def weigh(t, _):
            ones = jnp.ones((TILE, 128), BF)
            arrive(t, 1, load_v)
            here = pl.ds(pl.multiple_of(t * TILE, TILE), TILE)
            for h in range(16):
                top = best[h]
                p = jnp.exp2(sc[t, h] - jnp.concatenate([top] * (TILE // 128), axis=1))
                value = jnp.concatenate([vbuf[here, h * 128 : h * 128 + 128], ones], axis=1)
                acc[h] += mm(p.astype(BF), value)
            return 0

        lax.fori_loop(first, last, weigh, 0)
        lane = iota((CHUNK, 128), 1)
        lse = jnp.zeros((CHUNK, 128), F32)
        for h in range(16):
            full = acc[h, :, 128:256]
            osc[h, rows, :] = (acc[h, :, 0:128] / full).astype(BF)
            lse = jnp.where(lane == h, best[h] + jnp.log2(full), lse)
        lsc[rows, :] = lse
        return 0

    for t in range(tiles):
        load_v(t).start()
    lax.fori_loop(0, units, unit, 0)
    arrive(tiles - 1, 0, load_k)
    arrive(tiles - 1, 1, load_v)

    lane = iota((256, 128), 1)
    ok = slots[...] >= 0.0
    empty = jnp.where((lane < 16) & ~ok, NEG, 0.0).astype(BF)
    out_ref[:, 0:256, :] = jnp.zeros((16, 256, 128), BF)
    out_ref[:, 256:272, :] = empty.reshape(16, 16, 128)

    def scatter(b, _):
        rows = pl.ds(pl.multiple_of(b * CHUNK, CHUNK), CHUNK)
        back = jnp.where(slots[...] == (lane + b * CHUNK).astype(F32), 1.0, 0.0).astype(BF)
        for h in range(0, 16, 2):
            both = mm(back, jnp.concatenate([osc[h, rows, :], osc[h + 1, rows, :]], axis=1))
            for g in (0, 1):
                here = slice((h + g) * 16, (h + g) * 16 + 16)
                part = both[:, g * 128 : g * 128 + 128].reshape(16, 16, 128)
                out_ref[:, here, :] = (out_ref[:, here, :].astype(F32) + part).astype(BF)
        lse = lsc[rows, :]
        hi = lse.astype(BF)
        rest = lse - hi.astype(F32)
        mid = rest.astype(BF)
        lo = (rest - mid.astype(F32)).astype(BF)
        merged = hi.astype(F32) + pltpu.roll(mid.astype(F32), 16, 1) + pltpu.roll(lo.astype(F32), 32, 1)
        part = mm(back, merged.astype(BF)).reshape(16, 16, 128)
        out_ref[:, 256:272, :] = (out_ref[:, 256:272, :].astype(F32) + part).astype(BF)
        return 0

    lax.fori_loop(0, blocks, scatter, 0)


def prefix(lengths, base, got, k, v):
    tiles, tok = k.shape[0], v.shape[0]
    room = 384 + CHUNK
    return pl.pallas_call(
        prefix_kernel,
        out_shape=jax.ShapeDtypeStruct((16, 272, 128), BF),
        in_specs=[SM, SM, VM, HB, HB],
        out_specs=VM,
        scratch_shapes=[
            pltpu.VMEM(k.shape, BF),
            pltpu.VMEM(v.shape, BF),
            pltpu.VMEM((16, room, 256), BF),
            pltpu.VMEM((tiles, 16, CHUNK, TILE), F32),
            pltpu.VMEM((16, CHUNK, 128), F32),
            pltpu.VMEM((16, CHUNK, 256), F32),
            pltpu.VMEM((16, room, 128), BF),
            pltpu.VMEM((room, 128), F32),
            pltpu.VMEM((256, 128), F32),
            pltpu.VMEM((CHUNK, TILE), F32),
            pltpu.VMEM((room, 128), jnp.int32),
            pltpu.VMEM((room, 128), jnp.int32),
            pltpu.SMEM((16,), jnp.int32),
            pltpu.SMEM((16,), jnp.int32),
            pltpu.SMEM((16,), jnp.int32),
            pltpu.SMEM((2,), jnp.int32),
            pltpu.SemaphoreType.DMA((tiles,)),
            pltpu.SemaphoreType.DMA((tiles,)),
        ],
        compiler_params=params(48),
        cost_estimate=pl.CostEstimate(flops=6 << 30, bytes_accessed=20 << 20, transcendentals=4 << 20),
        name="prefix",
    )(lengths, base, got, k, v)


def combine_kernel(got_ref, own_hbm, own_lse_hbm, out_ref, own_ref, own_lse_ref, sems):
    loads = [
        pltpu.make_async_copy(own_lse_hbm, own_lse_ref, sems.at[0]),
        pltpu.make_async_copy(own_hbm, own_ref, sems.at[1]),
    ]
    for load in loads:
        load.start()
    x = got_ref[:, 256:272, :].reshape(256, 128).astype(F32)
    lse = (x + pltpu.roll(x, 112, 1)) + pltpu.roll(x, 96, 1)
    lse = lse.reshape(16, 16, 128)
    loads[0].wait()
    mine = own_lse_ref[...]
    lane = iota((16, 128), 1)
    lse = jnp.where((lane < 16)[None], lse, NEG)
    top = jnp.maximum(jnp.max(lse, axis=0), mine)
    w = jnp.exp2(lse - top[None])
    w_own = jnp.exp2(mine - top)
    total = jnp.sum(w, axis=0) + w_own
    w = w / total[None]
    w_own = w_own / total
    loads[1].wait()
    for h in range(16):
        rows = slice(h * 16, h * 16 + 16)
        o = jnp.sum(got_ref[:, rows, :].astype(F32) * w[:, :, h : h + 1], axis=0)
        o = (o + own_ref[rows, :] * w_own[:, h : h + 1]).astype(BF)
        for k in range(out_ref.shape[0]):
            out_ref[k, rows, :] = o


def combine(got, own_o, own_lse):
    return pl.pallas_call(
        combine_kernel,
        out_shape=jax.ShapeDtypeStruct((16, 256, 128), BF),
        in_specs=[VM, HB, HB],
        scratch_shapes=[
            pltpu.VMEM((256, 128), F32),
            pltpu.VMEM((16, 128), F32),
            pltpu.SemaphoreType.DMA((2,)),
        ],
        out_specs=VM,
        compiler_params=params(12),
        name="combine",
    )(got, own_o, own_lse)


def project_kernel(place_ref, x_ref, w_ref, keep_ref, give_ref, sums):
    total = None
    for h in range(0, 16, 2):
        a = x_ref[:, h * 16 : h * 16 + 16, :].reshape(256, 128)
        b = x_ref[:, h * 16 + 16 : h * 16 + 32, :].reshape(256, 128)
        part = mm_nt(jnp.concatenate([a, b], axis=1), w_ref[:, h * 128 : h * 128 + 256])
        total = part if total is None else total + part
    sums[...] = total
    place = place_ref[0]
    x, core = place // 2, place % 2
    for d in range(4):
        first = (x + d) % 4 * 2
        keep_ref[d] = sums[pl.ds(pl.multiple_of((first + core) * 32, 32), 32), :].astype(BF)
        give_ref[d] = sums[pl.ds(pl.multiple_of((first + 1 - core) * 32, 32), 32), :].astype(BF)


def project(place, x, w):
    shape = jax.ShapeDtypeStruct((4, 32, w.shape[0]), BF)
    return pl.pallas_call(
        project_kernel,
        out_shape=[shape, shape],
        in_specs=[SM, VM, VM],
        out_specs=[VM, VM],
        scratch_shapes=[pltpu.VMEM((256, w.shape[0]), F32)],
        compiler_params=params(12),
        name="project",
    )(place, x, w)


def pair_kernel(a_ref, b_ref, *out_refs):
    for d, out_ref in enumerate(out_refs):
        out_ref[...] = (a_ref[d].astype(F32) + b_ref[d].astype(F32)).astype(BF)


def pair(a, b):
    return pl.pallas_call(
        pair_kernel,
        out_shape=[jax.ShapeDtypeStruct(a.shape[1:], BF)] * 4,
        in_specs=[VM, VM],
        out_specs=[VM] * 4,
        compiler_params=params(4),
        name="pair",
    )(a, b)


def last_kernel(a_ref, b_ref, c_ref, d_ref, out_ref):
    total = (a_ref[...].astype(F32) + b_ref[...].astype(F32)) + (c_ref[...].astype(F32) + d_ref[...].astype(F32))
    for r in range(8):
        out_ref[r] = total[r * 4 : r * 4 + 4, :].astype(BF)


def last_sum(*parts):
    return pl.pallas_call(
        last_kernel,
        out_shape=jax.ShapeDtypeStruct((8, 4, parts[0].shape[1]), BF),
        in_specs=[VM] * 4,
        out_specs=VM,
        compiler_params=params(4),
        name="last_sum",
    )(*parts)


def sum_heads(keep, give):
    other = lax.ppermute(give, "head", [(i, i // 2 * 2 + 1 - i % 2) for i in range(8)])
    parts = pair(keep, other)
    moved = [
        lax.ppermute(parts[d], "head", [(i, (i // 2 + d) % 4 * 2 + i % 2) for i in range(8)]) for d in (1, 2, 3)
    ]
    return last_sum(parts[0], *moved)


def body(
    queries,
    w_uk,
    w_uv,
    prefix_cache,
    suffix_cache,
    new_latent,
    w_out,
    request_prefix,
    prefix_lengths,
    suffix_len,
):
    scale = math.log2(math.e) / queries.shape[-1] ** 0.5
    wide = lax.axis_size("wide")
    tok = prefix_cache.shape[0]
    base = (lax.axis_index("wide") * tok).astype(jnp.int32).reshape(1)
    place = lax.axis_index("head").astype(jnp.int32).reshape(1)
    base, place = lax.optimization_barrier((base, place))
    packed = pack(request_prefix, queries.reshape(256, 192), wide)
    got = lax.all_to_all(packed, "wide", split_axis=0, concat_axis=0, tiled=True)
    k, v, own_o, own_lse = expand(
        prefix_cache, w_uk, w_uv, scale, suffix_len, packed, jnp.swapaxes(suffix_cache, 1, 2), new_latent
    )
    part = prefix(prefix_lengths, base, got, k, v)
    part = lax.all_to_all(part, "wide", split_axis=0, concat_axis=0, tiled=True)
    head_out = combine(part, own_o, own_lse)
    head_out = lax.all_to_all(head_out, "wide", split_axis=0, concat_axis=0, tiled=True)
    out = sum_heads(*project(place, head_out, w_out.T))
    return out


def solution(mesh):
    in_specs = (
        P("wide", None, "head", None),
        P("head", None, None),
        P("head", None, None),
        P("wide", None),
        P("wide", None, None),
        P("wide", None, None),
        P("head", "wide"),
        P("wide"),
        P(),
        P("wide"),
    )
    out_specs = P("head", None, "wide")
    return jax.shard_map(body, mesh=mesh, in_specs=in_specs, out_specs=out_specs, check_vma=False)
```
